32 devices in a mesh: group: 2 (over y), scan: 4 (over z), tensor: 2 (over x), band: 2 (over core).
Axes of the slice: x: 2, y: 2, z: 4, core: 2. Of those that a mesh axis runs over, the one named last changes fastest.
Arguments:
- signal: bfloat16 [4096, 5120], P(('group', 'scan', 'band'), 'tensor'), parts along dimension 0, may hold values from -140 to 140
- gate_branch: bfloat16 [4096, 5120], P(('group', 'scan', 'band'), 'tensor'), parts along dimension 0, may hold values from -6 to 6
- write_proj: bfloat16 [4096, 128], P(('group', 'scan', 'band')), parts along dimension 0, may hold values from -1.796875 to 1.796875
- read_proj: bfloat16 [4096, 128], P(('group', 'scan', 'band')), parts along dimension 0, may hold values from -1.796875 to 1.796875
- step_logits: float32 [80, 4096], P('tensor', ('group', 'scan', 'band')), parts along dimension 1
- valid_mask: int32 [4096], P(('group', 'scan', 'band')), parts along dimension 0, may hold values from 0 to 1
- stretch_band: int32 [16], P(('group', 'scan', 'band')), parts along dimension 0, may hold values from 0 to 11
- band_offset: float32 [12, 80], P(None, 'tensor'), may hold values from -0.35 to 0.35
- decay_log: float32 [80], P('tensor'), may hold values from -8 to 0
- step_offset: float32 [80], P('tensor'), may hold values from -7 to -1
- skip_gain: float32 [80], P('tensor'), may hold values from 0.5 to 2
- norm_gain: float32 [5120], P('tensor'), may hold values from 0.1 to 1.9
- out_weight: bfloat16 [5120, 2560], P('tensor'), may hold values from -0.078125 to 0.078125
Outputs:
- layer_output: bfloat16 [4096, 2560], P(('group', 'scan', 'band'), 'tensor'), parts along dimension 0
The draws below stay inside these ranges and needn't reach their ends.
There are 2 independent parts, one for each index of `group`. The reference program is written for one: setup_inputs(seed, part) draws one part's arguments, and reference() takes and returns one part's arrays. A program takes and returns all parts, laid end to end along the dimension named above; an argument that names none is the same for every part. Nothing has to cross between parts.
All inputs are finite; a program needn't handle non-finite values.
Results may differ from the reference program's by a relative error of at most 0.015.
Values may be sent and summed in bfloat16 or wider, within the bound.
No kernel may reach another device: no remote copies, remote signals or barrier semaphores. Data moves between devices by JAX's collectives and lax.ppermute only.
A program may use at most 64 MiB of HBM per device.

```python
import math
import jax
import jax.numpy as jnp
from jax import lax

WIDTH = 2560
HEADS = 80
HEAD_DIM = 64
STATE = 128
STRETCH = 256
BANDS = 12
SEQUENCE_LENGTH = 2048
STRETCHES = 8
INNER = 5120
N_TENSOR = 2


def head_params(key):
    slow_share = 0.5
    chooser = jax.random.uniform(jax.random.fold_in(key, 101), (HEADS,))
    initial_sample = jax.random.uniform(jax.random.fold_in(key, 102), (HEADS,))
    second_draw = jax.random.uniform(jax.random.fold_in(key, 103), (HEADS,))
    root_length = jnp.sqrt(jnp.float32(SEQUENCE_LENGTH))
    slow_step = 0.5 * jnp.exp(initial_sample * jnp.log(4.0)) / root_length
    slow_rate = 0.3 * jnp.exp(second_draw * jnp.log(2.0)) / root_length
    fast_step = 0.1 * jnp.exp(initial_sample * jnp.log(2.0))
    fast_rate = jnp.exp(jnp.log(1.0 / 50.0) + second_draw * jnp.log(50.0 / 30.0)) / fast_step
    is_slow = chooser < slow_share
    return (jnp.where(is_slow, slow_step, fast_step), jnp.where(is_slow, slow_rate, fast_rate))


def spike_indices(key):
    return jax.random.randint(jax.random.fold_in(key, 211), (2,), 0, SEQUENCE_LENGTH)


def draw_decay_log(key, part):
    return jnp.log(head_params(key)[1])


def draw_step_offset(key, part):
    return jnp.log(jnp.expm1(head_params(key)[0]))


def draw_valid_mask(key, part):
    coin_outcome = jax.random.randint(jax.random.fold_in(key, 212), (SEQUENCE_LENGTH,), 0, 4)
    sample_places = spike_indices(key)
    spike_indicator = jnp.any(jnp.arange(SEQUENCE_LENGTH, dtype=jnp.int32)[:, None] == sample_places[None, :], axis=1)
    return jnp.where(spike_indicator | (coin_outcome == 0), 0, 1).astype(jnp.int32)


def draw_step_logits(key, part):
    rough_part = jax.random.uniform(jax.random.fold_in(key, 213), (HEADS, SEQUENCE_LENGTH), minval=-0.7, maxval=0.7)
    intensity = jax.random.uniform(jax.random.fold_in(key, 214), (2,), minval=0.8, maxval=1.1) * jnp.sqrt(jnp.float32(SEQUENCE_LENGTH))
    sample_places = spike_indices(key)
    boost = jnp.sum(jnp.where(jnp.arange(SEQUENCE_LENGTH, dtype=jnp.int32)[:, None] == sample_places[None, :], intensity[None, :], 0.0), axis=1)
    return rough_part + boost[None, :]


def draw_signal(key, part):
    row_scale = jnp.exp(jax.random.uniform(jax.random.fold_in(key, 301), (SEQUENCE_LENGTH, 1)) * jnp.log(10.0))
    column_scale = jnp.exp(jax.random.uniform(jax.random.fold_in(key, 302), (1, INNER)) * jnp.log(10.0))
    ramp_power = 0.5
    slope_scale = jnp.exp(ramp_power * jnp.log(3.0) * jnp.arange(INNER, dtype=jnp.float32)[None, :] / (INNER - 1))
    noise_part = jnp.clip(jax.random.normal(jax.random.fold_in(key, 303), (SEQUENCE_LENGTH, INNER)), -4.0, 4.0)
    return (0.2 * noise_part * row_scale * column_scale * slope_scale).astype(jnp.bfloat16)


def plant(values, rng, least, largest):
    longest = values.shape.index(max(values.shape))
    spots = []
    for shift in (0, 1):
        where = [jax.random.randint(jax.random.fold_in(rng, axis), (), 0, length) for axis, length in enumerate(values.shape)]
        where[longest] = (where[longest] + shift) % values.shape[longest]
        spots.append(tuple(where))
    return values.at[spots[0]].set(least).at[spots[1]].set(largest)


def level_of(key, extent, split, low, high):
    loudness, own = 1.0, jax.random.fold_in(key, 6)
    for dim, shards_of in split:
        draws = jnp.exp(jax.random.uniform(jax.random.fold_in(own, dim), (shards_of,), jnp.float32, low / len(split), high / len(split)))
        loudness = loudness * jnp.repeat(draws, extent[dim] // shards_of).reshape([-1 if axis == dim else 1 for axis in range(len(extent))])
    return loudness


def noise(stream_key, shape, scale, most, cuts=(), kind=jnp.bfloat16):
    values = scale * jax.random.normal(stream_key, shape, jnp.float32)
    if cuts:
        values = values * level_of(stream_key, shape, cuts, -0.22, 0.18)
    return jnp.clip(values, -most, most).astype(kind)


def setup_inputs(seed: int = 0, part: int = 0) -> dict:
    arg_keys = jax.random.split(jax.random.key(seed), 14)
    part_keys = jax.random.split(jax.random.fold_in(arg_keys[13], part), 14)
    return {
        "signal": draw_signal(jax.random.fold_in(jax.random.fold_in(arg_keys[13], part), 71), part),
        "gate_branch": noise(part_keys[1], (SEQUENCE_LENGTH, INNER), 1.0, 6.0, ((0, 8), (1, 2))),
        "write_proj": noise(part_keys[2], (SEQUENCE_LENGTH, STATE), 0.3, 1.796875, ((0, 8),)),
        "read_proj": noise(part_keys[3], (SEQUENCE_LENGTH, STATE), 0.3, 1.796875, ((0, 8),)),
        "step_logits": draw_step_logits(jax.random.fold_in(jax.random.fold_in(arg_keys[13], part), 71), part),
        "valid_mask": draw_valid_mask(jax.random.fold_in(jax.random.fold_in(arg_keys[13], part), 71), part),
        "stretch_band": plant(jax.random.randint(part_keys[6], (STRETCHES,), 0, BANDS), jax.random.fold_in(part_keys[6], 1), 0, BANDS - 1).astype(jnp.int32),
        "band_offset": jnp.clip(jax.random.uniform(arg_keys[7], (BANDS, HEADS), jnp.float32, -0.35, 0.35) * level_of(arg_keys[7], (BANDS, HEADS), ((1, 2),), -0.4, 0.0), -0.35, 0.35),
        "decay_log": draw_decay_log(jax.random.fold_in(arg_keys[13], 71), part),
        "step_offset": draw_step_offset(jax.random.fold_in(arg_keys[13], 71), part),
        "skip_gain": jnp.clip(jnp.exp(math.log(2.0) - 1.3862944 * jax.random.uniform(arg_keys[10], (HEADS,), jnp.float32) ** level_of(arg_keys[10], (HEADS,), ((0, 2),), -0.2, 0.2)), 0.5, 2.0),
        "norm_gain": jnp.clip(1.0 + 0.18 * jax.random.normal(arg_keys[11], (INNER,), jnp.float32), 0.1, 1.9),
        "out_weight": noise(arg_keys[12], (INNER, WIDTH), INNER ** -0.5, 0.078125, ((0, 2),)),
    }


EPSILON = 1e-05

def step_sizes(step_logits, stretch_band, band_offset, step_offset):
    one_hot = (stretch_band[:, None] == jnp.arange(BANDS, dtype=jnp.int32)[None, :]).astype(jnp.float32)
    stretch_offset = jnp.dot(one_hot, band_offset, precision=lax.Precision.HIGHEST)
    token_offset = jnp.repeat(stretch_offset, STRETCH, axis=0).T
    return jax.nn.softplus(step_logits + step_offset[:, None] + token_offset)

def split_state(state):
    state_high = state.astype(jnp.bfloat16)
    widened = lax.optimization_barrier(state_high).astype(jnp.float32)
    state_low = (state - widened).astype(jnp.bfloat16)
    return (state_high, state_low)

def stretch_pass(carry_state, pieces):
    signal_block, write_block, read_block, segment_damping, weight_block = pieces
    running = jnp.cumsum(segment_damping, axis=1)
    scores = jnp.dot(read_block, write_block.T, preferred_element_type=jnp.float32)
    lower_mask = jnp.arange(STRETCH)[:, None] >= jnp.arange(STRETCH)[None, :]
    span_logs = jnp.where(lower_mask[None], running[:, :, None] - running[:, None, :], -1e+30)
    mixing = (jnp.exp(span_logs) * scores[None] * weight_block[:, None, :]).astype(jnp.bfloat16)
    local_out = jnp.einsum('hij,jhp->ihp', mixing.astype(jnp.float32), signal_block.astype(jnp.float32), precision=lax.Precision.HIGHEST)
    state_high, state_low = split_state(carry_state)
    read_wide = read_block.astype(jnp.float32)
    high_part = jnp.einsum('in,hpn->ihp', read_wide, state_high.astype(jnp.float32), precision=lax.Precision.HIGHEST)
    low_part = jnp.einsum('in,hpn->ihp', read_wide, state_low.astype(jnp.float32), precision=lax.Precision.HIGHEST)
    carried_out = jnp.exp(running).T[:, :, None] * (high_part + low_part)
    tail_weight = jnp.exp(running[:, -1:] - running) * weight_block
    scaled = (signal_block.astype(jnp.float32) * tail_weight.T[:, :, None]).astype(jnp.bfloat16)
    stretch_state = jnp.einsum('jhp,jn->hpn', scaled.astype(jnp.float32), write_block.astype(jnp.float32), precision=lax.Precision.HIGHEST)
    next_state = jnp.exp(running[:, -1])[:, None, None] * carry_state + stretch_state
    return (next_state, local_out + carried_out)

def reference(signal, gate_branch, write_proj, read_proj, step_logits, valid_mask, stretch_band, band_offset, decay_log, step_offset, skip_gain, norm_gain, out_weight):
    step_size = step_sizes(step_logits, stretch_band, band_offset, step_offset)
    log_decay = step_size * (-jnp.exp(decay_log))[:, None]
    input_weight = step_size * valid_mask.astype(jnp.float32)[None, :]
    stretch_count = SEQUENCE_LENGTH // STRETCH
    signal_blocks = signal.reshape(stretch_count, STRETCH, HEADS, HEAD_DIM)
    write_blocks = write_proj.reshape(stretch_count, STRETCH, STATE)
    read_blocks = read_proj.reshape(stretch_count, STRETCH, STATE)
    decay_blocks = log_decay.reshape(HEADS, stretch_count, STRETCH).transpose(1, 0, 2)
    weight_blocks = input_weight.reshape(HEADS, stretch_count, STRETCH).transpose(1, 0, 2)
    start_state = jnp.zeros((HEADS, HEAD_DIM, STATE), jnp.float32)
    final_state, outputs = lax.scan(stretch_pass, start_state, (signal_blocks, write_blocks, read_blocks, decay_blocks, weight_blocks))
    ssm_out = outputs.reshape(SEQUENCE_LENGTH, HEADS, HEAD_DIM) + skip_gain[None, :, None] * signal.reshape(SEQUENCE_LENGTH, HEADS, HEAD_DIM).astype(jnp.float32)
    gated_out = ssm_out.reshape(SEQUENCE_LENGTH, INNER) * jax.nn.silu(gate_branch.astype(jnp.float32))
    mean_square = lax.optimization_barrier(jnp.mean(gated_out * gated_out, axis=1, keepdims=True))
    normed = (gated_out * lax.rsqrt(mean_square + EPSILON) * norm_gain[None, :]).astype(jnp.bfloat16)
    slice_width = INNER // N_TENSOR
    summed = jnp.zeros((SEQUENCE_LENGTH, WIDTH), jnp.float32)
    for member in range(N_TENSOR):
        partial_sum = jnp.dot(normed[:, member * slice_width:(member + 1) * slice_width], out_weight[member * slice_width:(member + 1) * slice_width], preferred_element_type=jnp.float32).astype(jnp.bfloat16)
        partial_sum = lax.optimization_barrier(partial_sum)
        summed = summed + partial_sum.astype(jnp.float32)
    return summed.astype(jnp.bfloat16)
```

```python
import functools

import jax
import jax.numpy as jnp
from jax import lax
from jax.experimental import pallas as pl
from jax.experimental.pallas import tpu as pltpu
from jax.sharding import PartitionSpec as P

HEAD_DIM = 64
STATE = 128
HALF = STATE // 2
PART = HALF // 2
STRETCH = 256
BANDS = 12
INNER = 5120
LANES = 128
CHUNK = 256

EPSILON = 1e-05
HIGHEST = lax.Precision.HIGHEST
F32 = jnp.float32
BF16 = jnp.bfloat16
MIB = 1 << 20


def dot(a, b):
    return lax.dot_general(a, b, (((1,), (0,)), ((), ())), preferred_element_type=F32)


def dot_rows(a, b):
    return lax.dot_general(a, b, (((0,), (0,)), ((), ())), preferred_element_type=F32)


def pieces(x):
    high = x.astype(BF16)
    rest = x - high.astype(F32)
    middle = rest.astype(BF16)
    return high, middle, (rest - middle.astype(F32)).astype(BF16)


def head_of_lane(heads, lanes, group, first=0):
    row = lax.broadcasted_iota(jnp.int32, (heads, lanes), 0)
    lane = lax.broadcasted_iota(jnp.int32, (heads, lanes), 1)
    return (row == first + lax.shift_right_logical(lane, group)).astype(F32).astype(BF16)


def spread_tokens(values, heads_map):
    return sum(dot_rows(piece, heads_map) for piece in pieces(values))


def spread_heads(row, heads_map):
    return sum(dot(piece, heads_map) for piece in pieces(jnp.broadcast_to(row, (8, row.shape[1]))))[:1]


def diagonal(rows, lanes):
    return lax.broadcasted_iota(jnp.int32, (rows, lanes), 0) == lax.broadcasted_iota(
        jnp.int32, (rows, lanes), 1
    )


def to_column(row):
    count = row.shape[1]
    return jnp.sum(jnp.where(diagonal(count, count), row, 0.0), axis=1, keepdims=True)


def decay_block(row, rows):
    place = lax.broadcasted_iota(jnp.int32, (rows, LANES), 0)
    high, middle, low = (piece.astype(F32) for piece in pieces(row))
    block = jnp.where(place == 0, high, jnp.where(place == 1, middle, jnp.where(place == 2, low, 0.0)))
    return block.astype(BF16)


def decay_row(block):
    return jnp.sum(block.astype(F32), axis=0, keepdims=True)


def decay_lanes(block, heads_map):
    return jnp.sum(dot(block[:16], heads_map), axis=0, keepdims=True)


def column_block(width):
    return width // 5 if width % (5 * LANES) == 0 else width


def local_call(body, name, outs, args, scratch=(), smem=(), limit=32 * MIB, flops=0):
    size = sum(a.size * a.dtype.itemsize for a in args) + sum(o.size * o.dtype.itemsize for o in outs)
    return pl.pallas_call(
        body,
        name=name,
        out_shape=outs,
        in_specs=[
            pl.BlockSpec(memory_space=pltpu.SMEM if i in smem else pltpu.VMEM) for i in range(len(args))
        ],
        out_specs=[pl.BlockSpec(memory_space=pltpu.VMEM)] * len(outs),
        scratch_shapes=list(scratch),
        compiler_params=pltpu.CompilerParams(vmem_limit_bytes=limit),
        cost_estimate=pl.CostEstimate(flops=flops, bytes_accessed=size, transcendentals=0),
    )(*args)


def state_kernel(
    band_ref,
    logits_ref,
    mask_ref,
    offset_ref,
    decay_log_ref,
    step_offset_ref,
    write_ref,
    signal_ref,
    running_ref,
    weight_ref,
    decay_ref,
    keep_ref,
    send_ref,
    state_ref,
):
    heads, tokens = logits_ref.shape
    width = signal_ref.shape[1]
    core = lax.axis_index("band")
    offset = to_column(step_offset_ref[...] + offset_ref[pl.ds(band_ref[0], 1), :])
    raw = logits_ref[...] + offset
    step_size = jnp.maximum(raw, 0.0) + jnp.log1p(jnp.exp(-jnp.abs(raw)))
    log_decay = step_size * to_column(-jnp.exp(decay_log_ref[...]))
    earlier = lax.broadcasted_iota(jnp.int32, (tokens, tokens), 0)
    later = lax.broadcasted_iota(jnp.int32, (tokens, tokens), 1)
    running = lax.dot_general(
        log_decay,
        (earlier <= later).astype(F32),
        (((1,), (0,)), ((), ())),
        precision=HIGHEST,
        preferred_element_type=F32,
    )
    weight = step_size * mask_ref[...].astype(F32)
    running_ref[...] = running
    weight_ref[...] = weight
    total = running[:, tokens - 1 : tokens]
    tail = jnp.exp(total - running) * weight
    block = column_block(width)
    for first in range(0, width, block):
        lanes = slice(first, first + block)
        heads_map = head_of_lane(heads, block, 6, first // HEAD_DIM)
        scaled = (signal_ref[:, lanes].astype(F32) * spread_tokens(tail, heads_map)).astype(BF16)
        state_ref[:, lanes] = dot_rows(write_ref[...], scaled)
    own = pl.multiple_of(core * HALF, HALF)
    other = pl.multiple_of((1 - core) * HALF, HALF)
    keep_ref[...] = state_ref[pl.ds(own, HALF), :]
    send_ref[:, :width] = state_ref[pl.ds(other, HALF), :].astype(BF16)
    row = jnp.sum(jnp.where(diagonal(heads, LANES), jnp.exp(total), 0.0), axis=0, keepdims=True)
    send_ref[:, width:] = decay_block(row, HALF)
    decay_ref[...] = decay_block(row, 16)


def local_kernel(
    running_ref,
    weight_ref,
    skip_ref,
    write_ref,
    read_ref,
    signal_ref,
    gate_ref,
    base_ref,
    factor_ref,
    scores_ref,
):
    heads, tokens = running_ref.shape
    block = signal_ref.shape[1]
    pairs = block // LANES
    at = pl.program_id(0)
    half = tokens // 2

    @pl.when(at == 0)
    def _():
        scores = lax.dot_general(
            read_ref[...], write_ref[...], (((1,), (1,)), ((), ())), preferred_element_type=F32
        )
        row = lax.broadcasted_iota(jnp.int32, scores.shape, 0)
        lane = lax.broadcasted_iota(jnp.int32, scores.shape, 1)
        scores_ref[...] = jnp.where(row >= lane, scores, 0.0)

    running = running_ref[...]
    first_head = at * (block // HEAD_DIM)
    wide = spread_tokens(running, head_of_lane(heads, block * 2, 7, first_head))
    heads_map = head_of_lane(heads, block, 6, first_head)
    gate = gate_ref[...].astype(F32)
    gate = gate / (1.0 + jnp.exp(-gate))
    factor_ref[...] = spread_tokens(jnp.exp(running), heads_map) * gate
    skip = spread_heads(skip_ref[...], heads_map)
    low_lanes = lax.broadcasted_iota(jnp.int32, (half, LANES), 1) < HEAD_DIM
    for pair in range(pairs):
        lanes = slice(pair * LANES, (pair + 1) * LANES)
        values = signal_ref[:, lanes]
        top, bottom = [], []
        for k in (2 * pair, 2 * pair + 1):
            row = running_ref[pl.ds(first_head + k, 1), :]
            weight = weight_ref[pl.ds(first_head + k, 1), :]
            column = wide[:, k * LANES : (k + 1) * LANES]

            def mixing(rows, cols):
                span = jnp.minimum(column[rows] - row[:, cols], 0.0)
                return (jnp.exp(span) * scores_ref[rows, cols] * weight[:, cols]).astype(BF16)

            early, late = slice(0, half), slice(half, tokens)
            top.append(dot(mixing(early, early), values[early]))
            bottom.append(
                dot(mixing(late, early), values[early]) + dot(mixing(late, late), values[late])
            )
        wide_values = values.astype(F32) * skip[:, lanes]
        base_ref[:half, lanes] = (
            jnp.where(low_lanes, top[0], top[1]) + wide_values[:half]
        ) * gate[:half, lanes]
        base_ref[half:, lanes] = (
            jnp.where(low_lanes, bottom[0], bottom[1]) + wide_values[half:]
        ) * gate[half:, lanes]


def local_part(running, weight, skip_gain, write_proj, read_proj, signal, gate_branch):
    tokens, width = signal.shape
    heads = running.shape[0]
    block = column_block(width)
    whole = lambda a: pl.BlockSpec(a.shape, lambda i: (0, 0))
    cols = pl.BlockSpec((tokens, block), lambda i: (0, i))
    return pl.pallas_call(
        local_kernel,
        name="local_part",
        out_shape=[jax.ShapeDtypeStruct((tokens, width), F32)] * 2,
        grid=(width // block,),
        in_specs=[whole(a) for a in (running, weight, skip_gain, write_proj, read_proj)] + [cols, cols],
        out_specs=[cols, cols],
        scratch_shapes=[pltpu.VMEM((tokens, tokens), F32)],
        compiler_params=pltpu.CompilerParams(vmem_limit_bytes=24 * MIB),
        cost_estimate=pl.CostEstimate(
            flops=6 * heads * tokens * tokens * HEAD_DIM,
            bytes_accessed=tokens * width * 12,
            transcendentals=heads * tokens * tokens,
        ),
    )(running, weight, skip_gain, write_proj, read_proj, signal, gate_branch)


def chip_kernel(keep_ref, got_ref, decay_ref, state_ref, first_ref, second_ref):
    width = keep_ref.shape[1]
    core = lax.axis_index("band")
    chip = lax.axis_index("scan")
    heads_map = head_of_lane(LANES, width, 6)
    got_decay = got_ref[:16, width:]
    mine = decay_ref[...]
    later = jnp.where(core == 0, got_decay.astype(F32), mine.astype(F32)).astype(BF16)
    lanes = decay_lanes(later, heads_map)
    got = got_ref[:, :width].astype(F32)
    keep = keep_ref[...]
    early, late = jnp.where(core == 0, keep, got), jnp.where(core == 0, got, keep)
    state_ref[:, :width] = (early * lanes + late).astype(BF16)
    block = decay_block(decay_row(got_decay) * decay_row(mine), PART)
    state_ref[:PART, width:] = block
    state_ref[PART:, width:] = block
    second_ref[...] = state_ref[PART:, :]
    first_ref[...] = state_ref[pl.ds(pl.multiple_of(jnp.where(chip == 1, PART, 0), PART), PART), :]


def middle_kernel(state_ref, near_ref, far_ref, out_ref):
    width = out_ref.shape[1]
    chip = lax.axis_index("scan")

    @pl.when(chip == 0)
    def _():
        out_ref[...] = state_ref[PART:, :width]

    @pl.when(chip == 1)
    def _():
        lanes = decay_lanes(state_ref[:16, width:], head_of_lane(LANES, width, 6))
        out_ref[...] = (
            lanes * near_ref[:, :width].astype(F32) + state_ref[:PART, :width].astype(F32)
        ).astype(BF16)

    @pl.when(chip == 2)
    def _():
        heads_map = head_of_lane(LANES, width, 6)
        lanes = decay_lanes(near_ref[:16, width:], heads_map)
        entered = lanes * far_ref[:, :width].astype(F32) + near_ref[:, :width].astype(F32)
        own = decay_lanes(state_ref[:16, width:], heads_map)
        out_ref[...] = (own * entered + state_ref[PART:, :width].astype(F32)).astype(BF16)

    @pl.when(chip == 3)
    def _():
        out_ref[...] = jnp.zeros(out_ref.shape, BF16)


def enter_kernel(
    near_ref, far_ref, next_ref, skip_ref, keep_ref, got_ref, decay_ref, mine_ref, send_ref, enter_ref
):
    width = keep_ref.shape[1]
    core = lax.axis_index("band")
    chip = lax.axis_index("scan")
    near = near_ref[:, :width]

    @pl.when(chip == 0)
    def _():
        enter_ref[...] = jnp.zeros(enter_ref.shape, F32)

    @pl.when(chip == 1)
    def _():
        enter_ref[:PART, :] = near.astype(F32)
        enter_ref[PART:, :] = next_ref[...].astype(F32)

    @pl.when(chip > 1)
    def _():
        lanes = decay_lanes(near_ref[:16, width:], head_of_lane(LANES, width, 6))

        @pl.when(chip == 2)
        def _():
            enter_ref[:PART, :] = next_ref[...].astype(F32)
            enter_ref[PART:, :] = lanes * far_ref[:, :width].astype(F32) + near.astype(F32)

        @pl.when(chip == 3)
        def _():
            enter_ref[:PART, :] = lanes * skip_ref[...].astype(F32) + near.astype(F32)
            enter_ref[PART:, :] = next_ref[...].astype(F32)

    share_enter(enter_ref, keep_ref, got_ref, decay_ref, mine_ref, send_ref)


def share_enter(enter_ref, keep_ref, got_ref, decay_ref, mine_ref, send_ref):
    width = keep_ref.shape[1]
    core = lax.axis_index("band")
    heads_map = head_of_lane(LANES, width, 6)
    enter = enter_ref[...]

    @pl.when(core == 0)
    def _():
        mine_ref[...] = enter.astype(BF16)
        send_ref[...] = (decay_lanes(decay_ref[...], heads_map) * enter + keep_ref[...]).astype(BF16)

    @pl.when(core == 1)
    def _():
        send_ref[...] = enter.astype(BF16)
        lanes = decay_lanes(got_ref[:16, width:], heads_map)
        mine_ref[...] = (lanes * enter + got_ref[:, :width].astype(F32)).astype(BF16)


def gathered_kernel(all_ref, keep_ref, got_ref, decay_ref, mine_ref, send_ref, enter_ref):
    width = keep_ref.shape[1]
    chip = lax.axis_index("scan")
    heads_map = head_of_lane(LANES, width, 6)
    enter_ref[...] = jnp.zeros(enter_ref.shape, F32)
    for source in range(all_ref.shape[0]):

        @pl.when(source < chip)
        def _():
            lanes = decay_lanes(all_ref[source, :16, width:], heads_map)
            enter_ref[...] = lanes * enter_ref[...] + all_ref[source, :, :width].astype(F32)

    share_enter(enter_ref, keep_ref, got_ref, decay_ref, mine_ref, send_ref)


def entering_state(keep, got, decay, chips):
    width = keep.shape[1]
    half = jax.ShapeDtypeStruct((HALF, width), BF16)
    state, first, second = local_call(
        chip_kernel,
        "chip_state",
        [
            jax.ShapeDtypeStruct((HALF, width + LANES), BF16),
            jax.ShapeDtypeStruct((PART, width + LANES), BF16),
            jax.ShapeDtypeStruct((PART, width + LANES), BF16),
        ],
        (keep, got, decay),
    )
    enter = pltpu.VMEM((HALF, width), F32)
    if chips != 4:
        gathered = lax.all_gather(state, "scan", axis=0)
        return local_call(
            gathered_kernel, "enter_state", [half, half], (gathered, keep, got, decay), (enter,)
        )
    near = lax.ppermute(first, "scan", [(0, 1), (1, 2), (2, 3)])
    far = lax.ppermute(second, "scan", [(0, 2)])
    (middle,) = local_call(
        middle_kernel, "middle_state", [jax.ShapeDtypeStruct((PART, width), BF16)], (state, near, far)
    )
    following = lax.ppermute(middle, "scan", [(0, 1), (1, 2), (2, 3)])
    skipping = lax.ppermute(middle, "scan", [(1, 3)])
    return local_call(
        enter_kernel,
        "enter_state",
        [half, half],
        (near, far, following, skipping, keep, got, decay),
        (enter,),
    )


def gated_kernel(mine_ref, other_ref, read_ref, gain_ref, base_ref, factor_ref, out_ref, square_ref, sum_ref):
    core = lax.axis_index("band")
    at = pl.program_id(0)
    mine, other = mine_ref[...], other_ref[...]
    is_first = core == 0
    low = jnp.where(is_first, mine.astype(F32), other.astype(F32)).astype(BF16)
    high = jnp.where(is_first, other.astype(F32), mine.astype(F32)).astype(BF16)
    carried = dot(read_ref[...], jnp.concatenate([low, high], axis=0))
    gated = base_ref[...] + factor_ref[...] * carried
    out_ref[...] = (gated * gain_ref[...]).astype(BF16)
    squares = gated * gated
    total = sum(squares[:, k : k + LANES] for k in range(0, squares.shape[1], LANES))

    @pl.when(at == 0)
    def _():
        sum_ref[...] = total

    @pl.when(at > 0)
    def _():
        sum_ref[...] += total

    @pl.when(at == pl.num_programs(0) - 1)
    def _():
        square_ref[...] = jnp.broadcast_to(
            jnp.sum(sum_ref[...].T, axis=0, keepdims=True), square_ref.shape
        )


def gated_part(mine, other, read_proj, norm_gain, base, factor):
    tokens, width = base.shape
    block = column_block(width)
    cols = lambda rows: pl.BlockSpec((rows, block), lambda i: (0, i))
    return pl.pallas_call(
        gated_kernel,
        name="gated_part",
        out_shape=[
            jax.ShapeDtypeStruct((tokens, width), BF16),
            jax.ShapeDtypeStruct((8, tokens), F32),
        ],
        grid=(width // block,),
        in_specs=[
            cols(HALF),
            cols(HALF),
            pl.BlockSpec(read_proj.shape, lambda i: (0, 0)),
            cols(1),
            cols(tokens),
            cols(tokens),
        ],
        out_specs=[cols(tokens), pl.BlockSpec((8, tokens), lambda i: (0, 0))],
        scratch_shapes=[pltpu.VMEM((tokens, LANES), F32)],
        compiler_params=pltpu.CompilerParams(vmem_limit_bytes=24 * MIB),
        cost_estimate=pl.CostEstimate(
            flops=2 * tokens * width * STATE, bytes_accessed=tokens * width * 10, transcendentals=0
        ),
    )(mine, other, read_proj, norm_gain, base, factor)


def project_kernel(where_ref, gated_ref, weight_ref, out_ref):
    out_ref[...] = dot(gated_ref[...], weight_ref[...]).astype(out_ref.dtype)


def project(where, gated, out_weight, count, dtype):
    tokens, width = gated.shape
    return pl.pallas_call(
        project_kernel,
        name="project",
        out_shape=jax.ShapeDtypeStruct((tokens, count * CHUNK), dtype),
        grid_spec=pltpu.PrefetchScalarGridSpec(
            num_scalar_prefetch=1,
            grid=(count,),
            in_specs=[
                pl.BlockSpec((tokens, width), lambda i, where: (0, 0)),
                pl.BlockSpec((width, CHUNK), lambda i, where: (0, where[0] + i)),
            ],
            out_specs=pl.BlockSpec((tokens, CHUNK), lambda i, where: (0, i)),
        ),
        compiler_params=pltpu.CompilerParams(vmem_limit_bytes=16 * MIB),
        cost_estimate=pl.CostEstimate(
            flops=2 * tokens * width * count * CHUNK,
            bytes_accessed=(tokens + count * CHUNK) * width * 2,
            transcendentals=0,
        ),
    )(where, gated, out_weight)


def finish_kernel(squares_ref, other_squares_ref, own_ref, *refs):
    *got_refs, out_ref = refs
    mean = (squares_ref[...] + other_squares_ref[...]) / INNER
    scale = lax.rsqrt(mean[:1] + EPSILON)
    scale = jnp.broadcast_to(scale, (LANES, scale.shape[1])).T
    first = 0
    for got_ref in got_refs:
        for k in range(0, got_ref.shape[1], LANES):
            lanes = slice(first + k, first + k + LANES)
            total = own_ref[:, lanes] + got_ref[:, k : k + LANES].astype(F32)
            out_ref[:, lanes] = (total * scale).astype(BF16)
        first += got_ref.shape[1]


SENDS = (1, 2, 2)


def layer_columns(gated, squares, out_weight, members):
    tokens = gated.shape[0]
    columns = out_weight.shape[1] // members
    if members != 2 or columns != CHUNK * sum(SENDS):
        mean = lax.psum(squares[0], "tensor") / INNER
        partial = dot(gated, out_weight).astype(BF16)
        total = lax.psum_scatter(partial, "tensor", scatter_dimension=1, tiled=True)
        return (total.astype(F32) * lax.rsqrt(mean + EPSILON)[:, None]).astype(BF16)
    member = lax.axis_index("tensor")
    swap = [(0, 1), (1, 0)]
    blocks = columns // CHUNK
    got, first = [], 0
    for count in SENDS:
        where = ((1 - member) * blocks + first)[None].astype(jnp.int32)
        got.append(lax.ppermute(project(where, gated, out_weight, count, BF16), "tensor", swap))
        first += count
    other_squares = lax.ppermute(squares, "tensor", swap)
    own = project((member * blocks)[None].astype(jnp.int32), gated, out_weight, blocks, F32)
    (result,) = local_call(
        finish_kernel,
        "finish",
        [jax.ShapeDtypeStruct((tokens, columns), BF16)],
        (squares, other_squares, own, *got),
    )
    return result


def on_device(
    chips,
    members,
    signal,
    gate_branch,
    write_proj,
    read_proj,
    step_logits,
    valid_mask,
    stretch_band,
    band_offset,
    decay_log,
    step_offset,
    skip_gain,
    norm_gain,
    out_weight,
):
    tokens, width = signal.shape
    heads = decay_log.shape[0]
    running, weight, decay, keep, send = local_call(
        state_kernel,
        "own_state",
        [
            jax.ShapeDtypeStruct((heads, tokens), F32),
            jax.ShapeDtypeStruct((heads, tokens), F32),
            jax.ShapeDtypeStruct((16, LANES), BF16),
            jax.ShapeDtypeStruct((HALF, width), F32),
            jax.ShapeDtypeStruct((HALF, width + LANES), BF16),
        ],
        (
            stretch_band,
            step_logits,
            valid_mask[None],
            band_offset,
            decay_log[None],
            step_offset[None],
            write_proj,
            signal,
        ),
        (pltpu.VMEM((STATE, width), F32),),
        smem=(0,),
        flops=8 * tokens * width * STATE,
    )
    cores = [(0, 1), (1, 0)]
    got = lax.ppermute(send, "band", cores)
    base, factor = local_part(
        running, weight, skip_gain[None], write_proj, read_proj, signal, gate_branch
    )
    mine, give = entering_state(keep, got, decay, chips)
    other = lax.ppermute(give, "band", cores)
    gated, squares = gated_part(mine, other, read_proj, norm_gain[None], base, factor)
    return layer_columns(gated, squares, out_weight, members)


def solution(mesh):
    placed = (
        P(("group", "scan", "band"), "tensor"),
        P(("group", "scan", "band"), "tensor"),
        P(("group", "scan", "band"), None),
        P(("group", "scan", "band"), None),
        P("tensor", ("group", "scan", "band")),
        P(("group", "scan", "band")),
        P(("group", "scan", "band")),
        P(None, "tensor"),
        P("tensor"),
        P("tensor"),
        P("tensor"),
        P("tensor"),
        P("tensor", None),
    )
    return jax.shard_map(
        functools.partial(on_device, mesh.shape["scan"], mesh.shape["tensor"]),
        mesh=mesh,
        in_specs=placed,
        out_specs=P(("group", "scan", "band"), "tensor"),
        check_vma=False,
    )
```

```python
import functools

import jax
import jax.numpy as jnp
from jax import lax
from jax.experimental import pallas as pl
from jax.experimental.pallas import tpu as pltpu
from jax.sharding import PartitionSpec as P

HEAD_DIM = 64
STATE = 128
HALF = STATE // 2
PART = HALF // 2
STRETCH = 256
BANDS = 12
INNER = 5120
LANES = 128
CHUNK = 256

EPSILON = 1e-05
HIGHEST = lax.Precision.HIGHEST
F32 = jnp.float32
BF16 = jnp.bfloat16
MIB = 1 << 20


def dot(a, b):
    return lax.dot_general(a, b, (((1,), (0,)), ((), ())), preferred_element_type=F32)


def dot_rows(a, b):
    return lax.dot_general(a, b, (((0,), (0,)), ((), ())), preferred_element_type=F32)


def pieces(x):
    high = x.astype(BF16)
    rest = x - high.astype(F32)
    middle = rest.astype(BF16)
    return high, middle, (rest - middle.astype(F32)).astype(BF16)


def head_of_lane(heads, lanes, group, first=0):
    row = lax.broadcasted_iota(jnp.int32, (heads, lanes), 0)
    lane = lax.broadcasted_iota(jnp.int32, (heads, lanes), 1)
    return (row == first + lax.shift_right_logical(lane, group)).astype(F32).astype(BF16)


def spread_tokens(values, heads_map):
    return sum(dot_rows(piece, heads_map) for piece in pieces(values))


def spread_heads(row, heads_map):
    return sum(dot(piece, heads_map) for piece in pieces(jnp.broadcast_to(row, (8, row.shape[1]))))[:1]


def diagonal(rows, lanes):
    return lax.broadcasted_iota(jnp.int32, (rows, lanes), 0) == lax.broadcasted_iota(
        jnp.int32, (rows, lanes), 1
    )


def to_column(row):
    count = row.shape[1]
    return jnp.sum(jnp.where(diagonal(count, count), row, 0.0), axis=1, keepdims=True)


def decay_block(row, rows):
    place = lax.broadcasted_iota(jnp.int32, (rows, LANES), 0)
    high, middle, low = (piece.astype(F32) for piece in pieces(row))
    block = jnp.where(place == 0, high, jnp.where(place == 1, middle, jnp.where(place == 2, low, 0.0)))
    return block.astype(BF16)


def decay_row(block):
    return jnp.sum(block.astype(F32), axis=0, keepdims=True)


def decay_lanes(block, heads_map):
    return jnp.sum(dot(block[:16], heads_map), axis=0, keepdims=True)


def column_block(width):
    return width // 5 if width % (5 * LANES) == 0 else width


def local_call(body, name, outs, args, scratch=(), limit=32 * MIB, flops=0, after=()):
    size = sum(a.size * a.dtype.itemsize for a in args) + sum(o.size * o.dtype.itemsize for o in outs)

    def kernel(*refs):
        body(*refs[: len(args)], *refs[len(args) + len(after) :])

    return pl.pallas_call(
        kernel,
        name=name,
        out_shape=outs,
        in_specs=[pl.BlockSpec(memory_space=pltpu.VMEM)] * len(args)
        + [pl.BlockSpec(memory_space=pl.ANY)] * len(after),
        out_specs=[pl.BlockSpec(memory_space=pltpu.VMEM)] * len(outs),
        scratch_shapes=list(scratch),
        compiler_params=pltpu.CompilerParams(vmem_limit_bytes=limit),
        cost_estimate=pl.CostEstimate(flops=flops, bytes_accessed=size, transcendentals=0),
    )(*args, *after)


def whole(a):
    return pl.BlockSpec(a.shape, lambda i: (0,) * a.ndim)


IN_VMEM = pl.BlockSpec(memory_space=pltpu.VMEM)


def in_hbm(*arrays):
    return [pltpu.with_memory_space_constraint(a, pltpu.HBM) for a in arrays]


def state_kernel(
    band_ref,
    logits_ref,
    mask_ref,
    offset_ref,
    decay_log_ref,
    step_offset_ref,
    write_ref,
    signal_ref,
    running_ref,
    weight_ref,
    decay_ref,
    keep_ref,
    send_ref,
    tail_ref,
    state_ref,
):
    heads, tokens = logits_ref.shape
    block = signal_ref.shape[1]
    width = keep_ref.shape[1]
    core = lax.axis_index("band")
    at = pl.program_id(0)

    @pl.when(at == 0)
    def _():
        offset = to_column(step_offset_ref[...] + offset_ref[pl.ds(band_ref[0], 1), :])
        raw = logits_ref[...] + offset
        step_size = jnp.maximum(raw, 0.0) + jnp.log1p(jnp.exp(-jnp.abs(raw)))
        log_decay = step_size * to_column(-jnp.exp(decay_log_ref[...]))
        earlier = lax.broadcasted_iota(jnp.int32, (tokens, tokens), 0)
        later = lax.broadcasted_iota(jnp.int32, (tokens, tokens), 1)
        running = lax.dot_general(
            log_decay,
            (earlier <= later).astype(F32),
            (((1,), (0,)), ((), ())),
            precision=HIGHEST,
            preferred_element_type=F32,
        )
        weight = step_size * mask_ref[...].astype(F32)
        running_ref[...] = running
        weight_ref[...] = weight
        total = running[:, tokens - 1 : tokens]
        tail_ref[...] = jnp.exp(total - running) * weight
        row = jnp.sum(jnp.where(diagonal(heads, LANES), jnp.exp(total), 0.0), axis=0, keepdims=True)
        send_ref[:, width:] = decay_block(row, HALF)
        decay_ref[...] = decay_block(row, 16)

    heads_map = head_of_lane(heads, block, 6, at * (block // HEAD_DIM))
    scaled = (signal_ref[...].astype(F32) * spread_tokens(tail_ref[...], heads_map)).astype(BF16)
    state_ref[...] = dot_rows(write_ref[...], scaled)
    own = pl.multiple_of(core * HALF, HALF)
    other = pl.multiple_of((1 - core) * HALF, HALF)
    lanes = pl.ds(pl.multiple_of(at * block, LANES), block)
    keep_ref[:, lanes] = state_ref[pl.ds(own, HALF), :]
    send_ref[:, lanes] = state_ref[pl.ds(other, HALF), :].astype(BF16)


def own_state(stretch_band, small, write_proj, signal):
    tokens, width = signal.shape
    heads = small[0].shape[0]
    block = column_block(width)
    return pl.pallas_call(
        state_kernel,
        name="own_state",
        out_shape=[
            jax.ShapeDtypeStruct((heads, tokens), F32),
            jax.ShapeDtypeStruct((heads, tokens), F32),
            jax.ShapeDtypeStruct((16, LANES), BF16),
            jax.ShapeDtypeStruct((HALF, width), F32),
            jax.ShapeDtypeStruct((HALF, width + LANES), BF16),
        ],
        grid=(width // block,),
        in_specs=[pl.BlockSpec(memory_space=pltpu.SMEM)]
        + [whole(a) for a in (*small, write_proj)]
        + [pl.BlockSpec((tokens, block), lambda i: (0, i))],
        out_specs=[IN_VMEM] * 5,
        scratch_shapes=[pltpu.VMEM((heads, tokens), F32), pltpu.VMEM((STATE, block), F32)],
        compiler_params=pltpu.CompilerParams(vmem_limit_bytes=16 * MIB),
        cost_estimate=pl.CostEstimate(
            flops=4 * tokens * width * STATE, bytes_accessed=tokens * width * 2, transcendentals=0
        ),
    )(stretch_band, *in_hbm(*small, write_proj, signal))


def local_kernel(
    running_ref,
    weight_ref,
    decay_ref,
    got_ref,
    after_ref,
    skip_ref,
    write_ref,
    read_ref,
    signal_ref,
    gate_ref,
    base_ref,
    factor_ref,
    lanes_ref,
    scores_ref,
):
    heads, tokens = running_ref.shape
    block = signal_ref.shape[1]
    width = base_ref.shape[1]
    at = pl.program_id(0)
    half = tokens // 2

    @pl.when(at == 0)
    def _():
        scores = lax.dot_general(
            read_ref[...], write_ref[...], (((1,), (1,)), ((), ())), preferred_element_type=F32
        )
        row = lax.broadcasted_iota(jnp.int32, scores.shape, 0)
        lane = lax.broadcasted_iota(jnp.int32, scores.shape, 1)
        scores_ref[...] = jnp.where(row >= lane, scores, 0.0)
        core = lax.axis_index("band")
        mine, got = decay_ref[...].astype(F32), got_ref[:16, width:].astype(F32)
        first = jnp.where(core == 0, mine, got).astype(BF16)
        lanes_ref[...] = jnp.broadcast_to(
            decay_lanes(first, head_of_lane(LANES, width, 6)), lanes_ref.shape
        )

    running = running_ref[...]
    first_head = at * (block // HEAD_DIM)
    wide = spread_tokens(running, head_of_lane(heads, block * 2, 7, first_head))
    heads_map = head_of_lane(heads, block, 6, first_head)
    gate = gate_ref[...].astype(F32)
    gate = gate / (1.0 + jnp.exp(-gate))
    out_lanes = pl.ds(pl.multiple_of(at * block, LANES), block)
    factor_ref[:, out_lanes] = spread_tokens(jnp.exp(running), heads_map) * gate
    skip = spread_heads(skip_ref[...], heads_map)
    low_lanes = lax.broadcasted_iota(jnp.int32, (half, LANES), 1) < HEAD_DIM
    early, late = slice(0, half), slice(half, tokens)
    for pair in range(block // LANES):
        lanes = slice(pair * LANES, (pair + 1) * LANES)
        values = signal_ref[:, lanes]
        top, bottom = [], []
        for k in (2 * pair, 2 * pair + 1):
            row = running_ref[pl.ds(first_head + k, 1), :]
            weight = weight_ref[pl.ds(first_head + k, 1), :]
            column = wide[:, k * LANES : (k + 1) * LANES]

            def mixing(rows, cols):
                span = jnp.minimum(column[rows] - row[:, cols], 0.0)
                return (jnp.exp(span) * scores_ref[rows, cols] * weight[:, cols]).astype(BF16)

            top.append(mixing(early, early))
            bottom.append(jnp.concatenate([mixing(late, early), mixing(late, late)], axis=1))
        top = dot(jnp.concatenate(top, axis=0), values[early])
        bottom = dot(jnp.concatenate(bottom, axis=0), values)
        skipped = values.astype(F32) * skip[:, lanes]
        out_lanes = pl.ds(pl.multiple_of(at * block + pair * LANES, LANES), LANES)
        base_ref[early, out_lanes] = (
            jnp.where(low_lanes, top[:half], top[half:]) + skipped[early]
        ) * gate[early, lanes]
        base_ref[late, out_lanes] = (
            jnp.where(low_lanes, bottom[:half], bottom[half:]) + skipped[late]
        ) * gate[late, lanes]


def local_part(running, weight, decay, got, after, skip_gain, write_proj, read_proj, signal, gate_branch):
    tokens, width = signal.shape
    heads = running.shape[0]
    block = column_block(width)
    cols = pl.BlockSpec((tokens, block), lambda i: (0, i))
    return pl.pallas_call(
        local_kernel,
        name="local_part",
        out_shape=[jax.ShapeDtypeStruct((tokens, width), F32)] * 2
        + [jax.ShapeDtypeStruct((8, width), F32)],
        grid=(width // block,),
        in_specs=[IN_VMEM] * 4
        + [pl.BlockSpec(memory_space=pl.ANY)]
        + [whole(a) for a in (skip_gain, write_proj, read_proj)]
        + [cols, cols],
        out_specs=[IN_VMEM] * 3,
        scratch_shapes=[pltpu.VMEM((tokens, tokens), F32)],
        compiler_params=pltpu.CompilerParams(vmem_limit_bytes=24 * MIB),
        cost_estimate=pl.CostEstimate(
            flops=6 * heads * tokens * tokens * HEAD_DIM,
            bytes_accessed=tokens * width * 12,
            transcendentals=heads * tokens * tokens,
        ),
    )(
        running,
        weight,
        decay,
        got,
        after,
        *in_hbm(skip_gain, write_proj, read_proj, signal, gate_branch),
    )


def stage_kernel(*refs):
    count = (len(refs) - 2) // 2
    copies = [
        pltpu.make_async_copy(refs[i], refs[count + 1 + i], refs[-1].at[i]) for i in range(count)
    ]
    for copy in copies:
        copy.start()
    for copy in copies:
        copy.wait()


def stage(arrays, after):
    size = sum(a.size * a.dtype.itemsize for a in arrays)
    return pl.pallas_call(
        stage_kernel,
        name="stage",
        out_shape=[jax.ShapeDtypeStruct(a.shape, a.dtype) for a in arrays],
        in_specs=[pl.BlockSpec(memory_space=pltpu.HBM)] * len(arrays) + [pl.BlockSpec(memory_space=pl.ANY)],
        out_specs=[IN_VMEM] * len(arrays),
        scratch_shapes=[pltpu.SemaphoreType.DMA((len(arrays),))],
        compiler_params=pltpu.CompilerParams(vmem_limit_bytes=4 * MIB),
        cost_estimate=pl.CostEstimate(flops=0, bytes_accessed=2 * size, transcendentals=0),
    )(*in_hbm(*arrays), after)


def chip_kernel(keep_ref, got_ref, decay_ref, state_ref, first_ref, second_ref):
    width = keep_ref.shape[1]
    core = lax.axis_index("band")
    chip = lax.axis_index("scan")
    heads_map = head_of_lane(LANES, width, 6)
    got_decay = got_ref[:16, width:]
    mine = decay_ref[...]
    later = jnp.where(core == 0, got_decay.astype(F32), mine.astype(F32)).astype(BF16)
    lanes = decay_lanes(later, heads_map)
    got = got_ref[:, :width].astype(F32)
    keep = keep_ref[...]
    early, late = jnp.where(core == 0, keep, got), jnp.where(core == 0, got, keep)
    state_ref[:, :width] = (early * lanes + late).astype(BF16)
    block = decay_block(decay_row(got_decay) * decay_row(mine), PART)
    state_ref[:PART, width:] = block
    state_ref[PART:, width:] = block
    second_ref[...] = state_ref[PART:, :]
    first_ref[...] = state_ref[pl.ds(pl.multiple_of(jnp.where(chip == 1, PART, 0), PART), PART), :]


def middle_kernel(state_ref, near_ref, far_ref, out_ref, lanes_ref):
    width = out_ref.shape[1]
    chip = lax.axis_index("scan")

    @pl.when(chip == 0)
    def _():
        out_ref[...] = state_ref[PART:, :width]

    @pl.when(chip == 1)
    def _():
        lanes = decay_lanes(state_ref[:16, width:], head_of_lane(LANES, width, 6))
        out_ref[...] = (
            lanes * near_ref[:, :width].astype(F32) + state_ref[:PART, :width].astype(F32)
        ).astype(BF16)

    @pl.when(chip > 1)
    def _():
        heads_map = head_of_lane(LANES, width, 6)
        lanes = decay_lanes(near_ref[:16, width:], heads_map)
        lanes_ref[...] = jnp.broadcast_to(lanes, lanes_ref.shape)

        @pl.when(chip == 2)
        def _():
            entered = lanes * far_ref[:, :width].astype(F32) + near_ref[:, :width].astype(F32)
            own = decay_lanes(state_ref[:16, width:], heads_map)
            out_ref[...] = (own * entered + state_ref[PART:, :width].astype(F32)).astype(BF16)


def enter_kernel(
    near_ref, far_ref, next_ref, skip_ref, near_lanes_ref, keep_ref, got_ref, lanes_ref, mine_ref, send_ref
):
    width = keep_ref.shape[1]
    chip = lax.axis_index("scan")

    def parts(first, second):
        enter = jnp.concatenate([first.astype(F32), second.astype(F32)], axis=0)
        share_enter(enter, keep_ref, got_ref, lanes_ref, mine_ref, send_ref)

    @pl.when(chip == 0)
    def _():
        share_enter(jnp.zeros((HALF, width), F32), keep_ref, got_ref, lanes_ref, mine_ref, send_ref)

    @pl.when(chip == 1)
    def _():
        parts(near_ref[:, :width], next_ref[...])

    @pl.when(chip == 2)
    def _():
        near = near_ref[:, :width].astype(F32)
        parts(next_ref[...], near_lanes_ref[:1] * far_ref[:, :width].astype(F32) + near)

    @pl.when(chip == 3)
    def _():
        near = near_ref[:, :width].astype(F32)
        parts(near_lanes_ref[:1] * skip_ref[...].astype(F32) + near, next_ref[...])


def share_enter(enter, keep_ref, got_ref, lanes_ref, mine_ref, send_ref):
    width = keep_ref.shape[1]
    core = lax.axis_index("band")

    @pl.when(core == 0)
    def _():
        mine_ref[...] = enter.astype(BF16)
        send_ref[...] = (lanes_ref[:1] * enter + keep_ref[...]).astype(BF16)

    @pl.when(core == 1)
    def _():
        send_ref[...] = enter.astype(BF16)
        mine_ref[...] = (lanes_ref[:1] * enter + got_ref[:, :width].astype(F32)).astype(BF16)


def gathered_kernel(all_ref, keep_ref, got_ref, lanes_ref, mine_ref, send_ref, enter_ref):
    width = keep_ref.shape[1]
    chip = lax.axis_index("scan")
    heads_map = head_of_lane(LANES, width, 6)
    enter_ref[...] = jnp.zeros(enter_ref.shape, F32)
    for source in range(all_ref.shape[0]):

        @pl.when(source < chip)
        def _():
            lanes = decay_lanes(all_ref[source, :16, width:], heads_map)
            enter_ref[...] = lanes * enter_ref[...] + all_ref[source, :, :width].astype(F32)

    share_enter(enter_ref[...], keep_ref, got_ref, lanes_ref, mine_ref, send_ref)


def chip_state(keep, got, decay):
    width = keep.shape[1]
    return local_call(
        chip_kernel,
        "chip_state",
        [
            jax.ShapeDtypeStruct((HALF, width + LANES), BF16),
            jax.ShapeDtypeStruct((PART, width + LANES), BF16),
            jax.ShapeDtypeStruct((PART, width + LANES), BF16),
        ],
        (keep, got, decay),
    )


def entering_state(chips, state, first, second, keep, got, local, constants):
    width = keep.shape[1]
    half = jax.ShapeDtypeStruct((HALF, width), BF16)
    if chips != 4:
        gathered = lax.all_gather(state, "scan", axis=0)
        base, factor, lanes = local(first)
        mine, give = local_call(
            gathered_kernel,
            "enter_state",
            [half, half],
            (gathered, keep, got, lanes),
            (pltpu.VMEM((HALF, width), F32),),
        )
        return mine, give, base, factor, stage(constants, lanes)
    near = lax.ppermute(first, "scan", [(0, 1), (1, 2), (2, 3)])
    far = lax.ppermute(second, "scan", [(0, 2)])
    base, factor, lanes = local(first)
    middle, near_lanes = local_call(
        middle_kernel,
        "middle_state",
        [jax.ShapeDtypeStruct((PART, width), BF16), jax.ShapeDtypeStruct((8, width), F32)],
        (state, near, far),
        after=(lanes,),
    )
    following = lax.ppermute(middle, "scan", [(0, 1), (1, 2), (2, 3)])
    skipping = lax.ppermute(middle, "scan", [(1, 3)])
    staged = stage(constants, middle)
    mine, give = local_call(
        enter_kernel,
        "enter_state",
        [half, half],
        (near, far, following, skipping, near_lanes, keep, got, lanes),
        after=(staged[0],),
    )
    return mine, give, base, factor, staged


def gated_kernel(mine_ref, other_ref, base_ref, factor_ref, read_ref, gain_ref, out_ref, square_ref):
    core = lax.axis_index("band")
    tokens, width = base_ref.shape
    block = column_block(width)
    is_first = core == 0
    read = read_ref[...]
    sums = jnp.zeros((tokens, LANES), F32)
    for first in range(0, width, block):
        lanes = slice(first, first + block)
        mine, other = mine_ref[:, lanes].astype(F32), other_ref[:, lanes].astype(F32)
        low = jnp.where(is_first, mine, other).astype(BF16)
        high = jnp.where(is_first, other, mine).astype(BF16)
        carried = dot(read, jnp.concatenate([low, high], axis=0))
        gated = base_ref[:, lanes] + factor_ref[:, lanes] * carried
        out_ref[:, lanes] = (gated * gain_ref[:, lanes]).astype(BF16)
        squares = gated * gated
        sums += sum(squares[:, k : k + LANES] for k in range(0, block, LANES))
    square_ref[...] = jnp.broadcast_to(jnp.sum(sums.T, axis=0, keepdims=True), square_ref.shape)


def gated_part(mine, other, base, factor, read_proj, norm_gain):
    tokens, width = base.shape
    return local_call(
        gated_kernel,
        "gated_part",
        [
            jax.ShapeDtypeStruct((tokens, width), BF16),
            jax.ShapeDtypeStruct((8, tokens), F32),
        ],
        (mine, other, base, factor, read_proj, norm_gain),
        flops=2 * tokens * width * STATE,
    )


def project_kernel(other, first, gated_ref, weight_ref, out_ref):
    columns = weight_ref.shape[1] // 2
    member = lax.axis_index("tensor")
    start = (1 - member if other else member) * columns + first
    for k in range(0, out_ref.shape[1], CHUNK):
        lanes = pl.ds(pl.multiple_of(start + k, LANES), CHUNK)
        out_ref[:, k : k + CHUNK] = dot(gated_ref[...], weight_ref[:, lanes]).astype(out_ref.dtype)


def project(other, first, count, dtype, gated, weight, after=()):
    tokens, width = gated.shape
    (result,) = local_call(
        functools.partial(project_kernel, other, first * CHUNK),
        "project",
        [jax.ShapeDtypeStruct((tokens, count * CHUNK), dtype)],
        (gated, weight),
        flops=2 * tokens * width * count * CHUNK,
        after=after,
    )
    return result


def finish_kernel(squares_ref, other_squares_ref, own_ref, *refs):
    *got_refs, out_ref = refs
    mean = (squares_ref[...] + other_squares_ref[...]) / INNER
    scale = lax.rsqrt(mean[:1] + EPSILON)
    scale = jnp.broadcast_to(scale, (LANES, scale.shape[1])).T
    first = 0
    for got_ref in got_refs:
        for k in range(0, got_ref.shape[1], LANES):
            lanes = slice(first + k, first + k + LANES)
            total = own_ref[:, lanes] + got_ref[:, k : k + LANES].astype(F32)
            out_ref[:, lanes] = (total * scale).astype(BF16)
        first += got_ref.shape[1]


SENDS = (1, 2, 2)


def layer_columns(members, gated, squares, weight):
    tokens = gated.shape[0]
    columns = weight.shape[1] // members
    if members != 2 or columns != CHUNK * sum(SENDS):
        mean = lax.psum(squares[0], "tensor") / INNER
        partial = dot(gated, weight).astype(BF16)
        total = lax.psum_scatter(partial, "tensor", scatter_dimension=1, tiled=True)
        return (total.astype(F32) * lax.rsqrt(mean + EPSILON)[:, None]).astype(BF16)
    swap = [(0, 1), (1, 0)]
    got, first, done = [], 0, ()
    for count in SENDS:
        part = project(True, first, count, BF16, gated, weight, done)
        got.append(lax.ppermute(part, "tensor", swap))
        first, done = first + count, (part,)
    other_squares = lax.ppermute(squares, "tensor", swap)
    own = project(False, 0, first, F32, gated, weight, done)
    (result,) = local_call(
        finish_kernel,
        "finish",
        [jax.ShapeDtypeStruct((tokens, columns), BF16)],
        (squares, other_squares, own, *got),
    )
    return result


def on_device(
    chips,
    members,
    signal,
    gate_branch,
    write_proj,
    read_proj,
    step_logits,
    valid_mask,
    stretch_band,
    band_offset,
    decay_log,
    step_offset,
    skip_gain,
    norm_gain,
    out_weight,
):
    small = (step_logits, valid_mask[None], band_offset, decay_log[None], step_offset[None])
    running, weight, decay, keep, send = own_state(stretch_band, small, write_proj, signal)
    cores = [(0, 1), (1, 0)]
    got = lax.ppermute(send, "band", cores)
    state, first, second = chip_state(keep, got, decay)

    def local(after):
        return local_part(
            running,
            weight,
            decay,
            got,
            after,
            skip_gain[None],
            write_proj,
            read_proj,
            signal,
            gate_branch,
        )

    mine, give, base, factor, staged = entering_state(
        chips, state, first, second, keep, got, local, (out_weight, read_proj, norm_gain[None])
    )
    other = lax.ppermute(give, "band", cores)
    weight, read, gain = staged
    gated, squares = gated_part(mine, other, base, factor, read, gain)
    return layer_columns(members, gated, squares, weight)


def solution(mesh):
    placed = (
        P(("group", "scan", "band"), "tensor"),
        P(("group", "scan", "band"), "tensor"),
        P(("group", "scan", "band"), None),
        P(("group", "scan", "band"), None),
        P("tensor", ("group", "scan", "band")),
        P(("group", "scan", "band")),
        P(("group", "scan", "band")),
        P(None, "tensor"),
        P("tensor"),
        P("tensor"),
        P("tensor"),
        P("tensor"),
        P("tensor", None),
    )
    return jax.shard_map(
        functools.partial(on_device, mesh.shape["scan"], mesh.shape["tensor"]),
        mesh=mesh,
        in_specs=placed,
        out_specs=P(("group", "scan", "band"), "tensor"),
        check_vma=False,
    )
```

```python
import functools

import jax
import jax.numpy as jnp
from jax import lax
from jax.experimental import pallas as pl
from jax.experimental.pallas import tpu as pltpu
from jax.sharding import PartitionSpec as P

HEAD_DIM = 64
STATE = 128
HALF = STATE // 2
PART = HALF // 2
STRETCH = 256
BANDS = 12
INNER = 5120
LANES = 128

EPSILON = 1e-05
HIGHEST = lax.Precision.HIGHEST
F32 = jnp.float32
BF16 = jnp.bfloat16
MIB = 1 << 20


def dot(a, b):
    return lax.dot_general(a, b, (((1,), (0,)), ((), ())), preferred_element_type=F32)


def pieces(x):
    high = x.astype(BF16)
    rest = x - high.astype(F32)
    middle = rest.astype(BF16)
    return high, middle, (rest - middle.astype(F32)).astype(BF16)


def head_of_lane(heads, lanes, group, first=0):
    row = lax.broadcasted_iota(jnp.int32, (heads, lanes), 0)
    lane = lax.broadcasted_iota(jnp.int32, (heads, lanes), 1)
    return (row == first + lax.shift_right_logical(lane, group)).astype(F32).astype(BF16)


def slot_of(heads):
    return -(-heads // 8) * 8


def piece_rows(values, ref):
    heads = values.shape[0]
    ref[...] = jnp.zeros(ref.shape, F32)
    for k, piece in enumerate(pieces(values)):
        first = k * slot_of(heads)
        ref[first : first + heads, :] = piece.astype(F32)
    return ref[...]


def piece_map(heads, lanes, group, first=0):
    away = (
        lax.broadcasted_iota(jnp.int32, (LANES, lanes), 0)
        - lax.shift_right_logical(lax.broadcasted_iota(jnp.int32, (LANES, lanes), 1), group)
        - first
    )
    slot = slot_of(heads)
    hit = (away == 0) | (away == slot) | (away == 2 * slot)
    return jnp.where(hit, 1.0, 0.0).astype(BF16)


def spread_heads(row, heads_map):
    return sum(dot(piece, heads_map) for piece in pieces(jnp.broadcast_to(row, (8, row.shape[1]))))[:1]


def diagonal(rows, lanes):
    return lax.broadcasted_iota(jnp.int32, (rows, lanes), 0) == lax.broadcasted_iota(
        jnp.int32, (rows, lanes), 1
    )


def to_column(row):
    count = row.shape[1]
    return jnp.sum(jnp.where(diagonal(count, count), row, 0.0), axis=1, keepdims=True)


def decay_block(row, rows):
    place = lax.broadcasted_iota(jnp.int32, (rows, LANES), 0)
    high, middle, low = (piece.astype(F32) for piece in pieces(row))
    block = jnp.where(place == 0, high, jnp.where(place == 1, middle, jnp.where(place == 2, low, 0.0)))
    return block.astype(BF16)


def decay_row(block):
    return jnp.sum(block.astype(F32), axis=0, keepdims=True)


def decay_lanes(block, heads_map):
    return jnp.sum(dot(block[:16], heads_map), axis=0, keepdims=True)


def column_block(width):
    return width // 5 if width % (5 * LANES) == 0 else width


def local_call(body, name, outs, args, scratch=(), limit=8 * MIB, flops=0, after=()):
    size = sum(a.size * a.dtype.itemsize for a in args) + sum(o.size * o.dtype.itemsize for o in outs)

    def kernel(*refs):
        body(*refs[: len(args)], *refs[len(args) + len(after) :])

    return pl.pallas_call(
        kernel,
        name=name,
        out_shape=outs,
        in_specs=[pl.BlockSpec(memory_space=pltpu.VMEM)] * len(args)
        + [pl.BlockSpec(memory_space=pl.ANY)] * len(after),
        out_specs=[pl.BlockSpec(memory_space=pltpu.VMEM)] * len(outs),
        scratch_shapes=list(scratch),
        compiler_params=pltpu.CompilerParams(vmem_limit_bytes=limit),
        cost_estimate=pl.CostEstimate(flops=flops, bytes_accessed=size, transcendentals=0),
    )(*args, *after)


IN_VMEM = pl.BlockSpec(memory_space=pltpu.VMEM)
IN_HBM = pl.BlockSpec(memory_space=pltpu.HBM)
ANYWHERE = pl.BlockSpec(memory_space=pl.ANY)


def in_hbm(*arrays):
    return [pltpu.with_memory_space_constraint(a, pltpu.HBM) for a in arrays]


def state_kernel(
    band_ref,
    logits_hbm,
    mask_hbm,
    offset_hbm,
    decay_log_hbm,
    step_offset_hbm,
    write_hbm,
    read_hbm,
    signal_hbm,
    gate_hbm,
    running_ref,
    weight_ref,
    decay_ref,
    keep_ref,
    send_ref,
    write_ref,
    read_ref,
    signal_ref,
    gate_ref,
    logits_ref,
    mask_ref,
    offset_ref,
    decay_log_ref,
    step_offset_ref,
    rows_ref,
    sems,
    block_sems,
):
    heads, tokens = logits_ref.shape
    width = signal_ref.shape[1]
    block = column_block(width)
    is_first = lax.axis_index("band") == 0
    pairs = (
        (logits_hbm, logits_ref),
        (mask_hbm, mask_ref),
        (offset_hbm, offset_ref),
        (decay_log_hbm, decay_log_ref),
        (step_offset_hbm, step_offset_ref),
        (write_hbm, write_ref),
        (read_hbm, read_ref),
        (gate_hbm, gate_ref),
    )
    copies = [pltpu.make_async_copy(*pair, sems.at[i]) for i, pair in enumerate(pairs)]
    blocks = [
        pltpu.make_async_copy(
            signal_hbm.at[:, pl.ds(first, block)],
            signal_ref.at[:, pl.ds(first, block)],
            block_sems.at[first // block],
        )
        for first in range(0, width, block)
    ]
    for copy in copies[:6] + blocks + copies[6:]:
        copy.start()
    for copy in copies[:6]:
        copy.wait()

    offset = to_column(step_offset_ref[...] + offset_ref[pl.ds(band_ref[0], 1), :])
    raw = logits_ref[...] + offset
    step_size = jnp.maximum(raw, 0.0) + jnp.log1p(jnp.exp(-jnp.abs(raw)))
    log_decay = step_size * to_column(-jnp.exp(decay_log_ref[...]))
    earlier = lax.broadcasted_iota(jnp.int32, (tokens, tokens), 0)
    later = lax.broadcasted_iota(jnp.int32, (tokens, tokens), 1)
    sums = dot(
        piece_rows(log_decay, rows_ref).astype(BF16), jnp.where(earlier <= later, 1.0, 0.0).astype(BF16)
    )
    slot = slot_of(heads)
    running = sums[:heads] + sums[slot : slot + heads] + sums[2 * slot : 2 * slot + heads]
    weight = step_size * mask_ref[...].astype(F32)
    running_ref[...] = running
    weight_ref[...] = weight
    total = running[:, tokens - 1 : tokens]
    row = jnp.sum(jnp.where(diagonal(heads, LANES), jnp.exp(total), 0.0), axis=0, keepdims=True)
    send_ref[:, width:] = decay_block(row, HALF)
    decay_ref[...] = decay_block(row, 16)

    tail = piece_rows(jnp.exp(total - running) * weight, rows_ref).T.astype(BF16)
    write = write_ref[...].astype(F32).T
    low, high = write[:HALF], write[HALF:]
    write = jnp.concatenate(
        [jnp.where(is_first, low, high), jnp.where(is_first, high, low)], axis=0
    ).astype(BF16)
    for copy, first in zip(blocks, range(0, width, block)):
        lanes = slice(first, first + block)
        factors = dot(tail, piece_map(heads, block, 6, first // HEAD_DIM))
        copy.wait()
        state = dot(write, (signal_ref[:, lanes].astype(F32) * factors).astype(BF16))
        keep_ref[:, lanes] = state[:HALF]
        send_ref[:, lanes] = state[HALF:].astype(BF16)
    for copy in copies[6:]:
        copy.wait()


def own_state(stretch_band, small, write_proj, read_proj, signal, gate_branch):
    tokens, width = signal.shape
    heads = small[0].shape[0]
    passed = (write_proj, read_proj, signal, gate_branch)
    return pl.pallas_call(
        state_kernel,
        name="own_state",
        out_shape=[
            jax.ShapeDtypeStruct((heads, tokens), F32),
            jax.ShapeDtypeStruct((heads, tokens), F32),
            jax.ShapeDtypeStruct((16, LANES), BF16),
            jax.ShapeDtypeStruct((HALF, width), F32),
            jax.ShapeDtypeStruct((HALF, width + LANES), BF16),
        ]
        + [jax.ShapeDtypeStruct(a.shape, a.dtype) for a in passed],
        in_specs=[pl.BlockSpec(memory_space=pltpu.SMEM)] + [IN_HBM] * 9,
        out_specs=[IN_VMEM] * 9,
        scratch_shapes=[pltpu.VMEM(a.shape, a.dtype) for a in small]
        + [
            pltpu.VMEM((LANES, tokens), F32),
            pltpu.SemaphoreType.DMA((8,)),
            pltpu.SemaphoreType.DMA((width // column_block(width),)),
        ],
        compiler_params=pltpu.CompilerParams(vmem_limit_bytes=16 * MIB),
        cost_estimate=pl.CostEstimate(
            flops=4 * tokens * width * STATE, bytes_accessed=tokens * width * 2, transcendentals=0
        ),
    )(stretch_band, *in_hbm(*small, *passed))


def local_kernel(
    running_ref,
    weight_ref,
    decay_ref,
    got_ref,
    write_ref,
    read_ref,
    signal_ref,
    gate_ref,
    skip_hbm,
    gain_hbm,
    matrix_hbm,
    after_ref,
    base_ref,
    factor_ref,
    lanes_ref,
    gain_ref,
    matrix_ref,
    scores_ref,
    rows_ref,
    running_pieces_ref,
    decay_pieces_ref,
    skip_ref,
    sems,
):
    heads, tokens = running_ref.shape
    width = base_ref.shape[1]
    block = column_block(width)
    half = tokens // 2
    copies = [
        pltpu.make_async_copy(*pair, sems.at[i])
        for i, pair in enumerate(((skip_hbm, skip_ref), (gain_hbm, gain_ref), (matrix_hbm, matrix_ref)))
    ]
    for copy in copies:
        copy.start()

    scores = lax.dot_general(
        read_ref[...], write_ref[...], (((1,), (1,)), ((), ())), preferred_element_type=F32
    )
    row = lax.broadcasted_iota(jnp.int32, scores.shape, 0)
    lane = lax.broadcasted_iota(jnp.int32, scores.shape, 1)
    scores_ref[...] = jnp.where(row >= lane, scores, 0.0)
    running = running_ref[...]
    running_pieces_ref[...] = piece_rows(running, rows_ref).T.astype(BF16)
    decay_pieces_ref[...] = piece_rows(jnp.exp(running), rows_ref).T.astype(BF16)
    is_first = lax.axis_index("band") == 0
    mine, got = decay_ref[...].astype(F32), got_ref[:16, width:].astype(F32)
    first_core = jnp.where(is_first, mine, got).astype(BF16)
    lanes_ref[...] = jnp.broadcast_to(
        decay_lanes(first_core, head_of_lane(LANES, width, 6)), lanes_ref.shape
    )
    copies[0].wait()
    low_lanes = lax.broadcasted_iota(jnp.int32, (half, LANES), 1) < HEAD_DIM
    early, late = slice(0, half), slice(half, tokens)

    def heads_block(at, _):
        first_head = at * (block // HEAD_DIM)
        out_lanes = pl.ds(pl.multiple_of(at * block, LANES), block)
        wide = dot(running_pieces_ref[...], piece_map(heads, block * 2, 7, first_head))
        gate = gate_ref[:, out_lanes].astype(F32)
        gate = gate / (1.0 + jnp.exp(-gate))
        factor_ref[:, out_lanes] = (
            dot(decay_pieces_ref[...], piece_map(heads, block, 6, first_head)) * gate
        )
        skip = spread_heads(skip_ref[...], head_of_lane(heads, block, 6, first_head))
        for pair in range(block // LANES):
            lanes = slice(pair * LANES, (pair + 1) * LANES)
            out_lanes = pl.ds(pl.multiple_of(at * block + pair * LANES, LANES), LANES)
            values = signal_ref[:, out_lanes]
            top, bottom = [], []
            for k in (2 * pair, 2 * pair + 1):
                row = running_ref[pl.ds(first_head + k, 1), :]
                weight = weight_ref[pl.ds(first_head + k, 1), :]
                column = wide[:, k * LANES : (k + 1) * LANES]

                def mixing(rows, cols):
                    span = jnp.minimum(column[rows] - row[:, cols], 0.0)
                    return (jnp.exp(span) * scores_ref[rows, cols] * weight[:, cols]).astype(BF16)

                top.append(mixing(early, early))
                bottom.append(jnp.concatenate([mixing(late, early), mixing(late, late)], axis=1))
            top = dot(jnp.concatenate(top, axis=0), values[early])
            bottom = dot(jnp.concatenate(bottom, axis=0), values)
            skipped = values.astype(F32) * skip[:, lanes]
            base_ref[early, out_lanes] = (
                jnp.where(low_lanes, top[:half], top[half:]) + skipped[early]
            ) * gate[early, lanes]
            base_ref[late, out_lanes] = (
                jnp.where(low_lanes, bottom[:half], bottom[half:]) + skipped[late]
            ) * gate[late, lanes]
        return 0

    lax.fori_loop(0, width // block, heads_block, 0)
    for copy in copies[1:]:
        copy.wait()


def local_part(resident, constants, after):
    running, signal = resident[0], resident[6]
    skip_gain, norm_gain, out_weight = constants
    tokens, width = signal.shape
    heads = running.shape[0]
    return pl.pallas_call(
        local_kernel,
        name="local_part",
        out_shape=[jax.ShapeDtypeStruct((tokens, width), F32)] * 2
        + [jax.ShapeDtypeStruct((8, width), F32)]
        + [jax.ShapeDtypeStruct(a.shape, a.dtype) for a in (norm_gain, out_weight)],
        in_specs=[IN_VMEM] * len(resident) + [IN_HBM] * len(constants) + [ANYWHERE],
        out_specs=[IN_VMEM] * 5,
        scratch_shapes=[
            pltpu.VMEM((tokens, tokens), F32),
            pltpu.VMEM((LANES, tokens), F32),
            pltpu.VMEM((tokens, LANES), BF16),
            pltpu.VMEM((tokens, LANES), BF16),
            pltpu.VMEM(skip_gain.shape, F32),
            pltpu.SemaphoreType.DMA((3,)),
        ],
        compiler_params=pltpu.CompilerParams(vmem_limit_bytes=16 * MIB),
        cost_estimate=pl.CostEstimate(
            flops=6 * heads * tokens * tokens * HEAD_DIM,
            bytes_accessed=tokens * width * 12,
            transcendentals=heads * tokens * tokens,
        ),
    )(*resident, *in_hbm(*constants), after)


def chip_kernel(keep_ref, got_ref, decay_ref, state_ref, first_ref, second_ref):
    width = keep_ref.shape[1]
    core = lax.axis_index("band")
    chip = lax.axis_index("scan")
    heads_map = head_of_lane(LANES, width, 6)
    got_decay = got_ref[:16, width:]
    mine = decay_ref[...]
    later = jnp.where(core == 0, got_decay.astype(F32), mine.astype(F32)).astype(BF16)
    lanes = decay_lanes(later, heads_map)
    got = got_ref[:, :width].astype(F32)
    keep = keep_ref[...]
    early, late = jnp.where(core == 0, keep, got), jnp.where(core == 0, got, keep)
    state_ref[:, :width] = (early * lanes + late).astype(BF16)
    block = decay_block(decay_row(got_decay) * decay_row(mine), PART)
    state_ref[:PART, width:] = block
    state_ref[PART:, width:] = block
    second_ref[...] = state_ref[PART:, :]
    first_ref[...] = state_ref[pl.ds(pl.multiple_of(jnp.where(chip == 1, PART, 0), PART), PART), :]


def middle_kernel(state_ref, near_ref, far_ref, out_ref, lanes_ref):
    width = out_ref.shape[1]
    chip = lax.axis_index("scan")

    @pl.when(chip == 0)
    def _():
        out_ref[...] = state_ref[PART:, :width]

    @pl.when(chip == 1)
    def _():
        lanes = decay_lanes(state_ref[:16, width:], head_of_lane(LANES, width, 6))
        out_ref[...] = (
            lanes * near_ref[:, :width].astype(F32) + state_ref[:PART, :width].astype(F32)
        ).astype(BF16)

    @pl.when(chip > 1)
    def _():
        heads_map = head_of_lane(LANES, width, 6)
        lanes = decay_lanes(near_ref[:16, width:], heads_map)
        lanes_ref[...] = jnp.broadcast_to(lanes, lanes_ref.shape)

        @pl.when(chip == 2)
        def _():
            entered = lanes * far_ref[:, :width].astype(F32) + near_ref[:, :width].astype(F32)
            own = decay_lanes(state_ref[:16, width:], heads_map)
            out_ref[...] = (own * entered + state_ref[PART:, :width].astype(F32)).astype(BF16)


def enter_kernel(
    near_ref, far_ref, next_ref, skip_ref, near_lanes_ref, keep_ref, got_ref, lanes_ref, mine_ref, send_ref
):
    width = keep_ref.shape[1]
    chip = lax.axis_index("scan")

    def parts(first, second):
        enter = jnp.concatenate([first.astype(F32), second.astype(F32)], axis=0)
        share_enter(enter, keep_ref, got_ref, lanes_ref, mine_ref, send_ref)

    @pl.when(chip == 0)
    def _():
        share_enter(jnp.zeros((HALF, width), F32), keep_ref, got_ref, lanes_ref, mine_ref, send_ref)

    @pl.when(chip == 1)
    def _():
        parts(near_ref[:, :width], next_ref[...])

    @pl.when(chip == 2)
    def _():
        near = near_ref[:, :width].astype(F32)
        parts(next_ref[...], near_lanes_ref[:1] * far_ref[:, :width].astype(F32) + near)

    @pl.when(chip == 3)
    def _():
        near = near_ref[:, :width].astype(F32)
        parts(near_lanes_ref[:1] * skip_ref[...].astype(F32) + near, next_ref[...])


def share_enter(enter, keep_ref, got_ref, lanes_ref, mine_ref, send_ref):
    width = keep_ref.shape[1]
    core = lax.axis_index("band")

    @pl.when(core == 0)
    def _():
        mine_ref[...] = enter.astype(BF16)
        send_ref[...] = (lanes_ref[:1] * enter + keep_ref[...]).astype(BF16)

    @pl.when(core == 1)
    def _():
        send_ref[...] = enter.astype(BF16)
        mine_ref[...] = (lanes_ref[:1] * enter + got_ref[:, :width].astype(F32)).astype(BF16)


def gathered_kernel(all_ref, keep_ref, got_ref, lanes_ref, mine_ref, send_ref, enter_ref):
    width = keep_ref.shape[1]
    chip = lax.axis_index("scan")
    heads_map = head_of_lane(LANES, width, 6)
    enter_ref[...] = jnp.zeros(enter_ref.shape, F32)
    for source in range(all_ref.shape[0]):

        @pl.when(source < chip)
        def _():
            lanes = decay_lanes(all_ref[source, :16, width:], heads_map)
            enter_ref[...] = lanes * enter_ref[...] + all_ref[source, :, :width].astype(F32)

    share_enter(enter_ref[...], keep_ref, got_ref, lanes_ref, mine_ref, send_ref)


def chip_state(keep, got, decay):
    width = keep.shape[1]
    return local_call(
        chip_kernel,
        "chip_state",
        [
            jax.ShapeDtypeStruct((HALF, width + LANES), BF16),
            jax.ShapeDtypeStruct((PART, width + LANES), BF16),
            jax.ShapeDtypeStruct((PART, width + LANES), BF16),
        ],
        (keep, got, decay),
    )


def entering_state(chips, state, first, second, keep, got, local):
    width = keep.shape[1]
    half = jax.ShapeDtypeStruct((HALF, width), BF16)
    if chips != 4:
        gathered = lax.all_gather(state, "scan", axis=0)
        base, factor, lanes, gain, weight = local(first)
        mine, give = local_call(
            gathered_kernel,
            "enter_state",
            [half, half],
            (gathered, keep, got, lanes),
            (pltpu.VMEM((HALF, width), F32),),
        )
        return mine, give, base, factor, gain, weight
    near = lax.ppermute(first, "scan", [(0, 1), (1, 2), (2, 3)])
    far = lax.ppermute(second, "scan", [(0, 2)])
    base, factor, lanes, gain, weight = local(first)
    middle, near_lanes = local_call(
        middle_kernel,
        "middle_state",
        [jax.ShapeDtypeStruct((PART, width), BF16), jax.ShapeDtypeStruct((8, width), F32)],
        (state, near, far),
        after=(lanes,),
    )
    following = lax.ppermute(middle, "scan", [(0, 1), (1, 2), (2, 3)])
    skipping = lax.ppermute(middle, "scan", [(1, 3)])
    mine, give = local_call(
        enter_kernel,
        "enter_state",
        [half, half],
        (near, far, following, skipping, near_lanes, keep, got, lanes),
    )
    return mine, give, base, factor, gain, weight


def gated_kernel(
    mine_ref, other_ref, base_ref, factor_ref, read_ref, gain_ref, weight_ref, out_ref, square_ref, *first_refs
):
    tokens, width = base_ref.shape
    block = column_block(width)
    is_first = lax.axis_index("band") == 0
    read = read_ref[...]
    sums = jnp.zeros((tokens, LANES), F32)
    for first in range(0, width, block):
        lanes = slice(first, first + block)
        mine, other = mine_ref[:, lanes].astype(F32), other_ref[:, lanes].astype(F32)
        low = jnp.where(is_first, mine, other).astype(BF16)
        high = jnp.where(is_first, other, mine).astype(BF16)
        carried = dot(read, jnp.concatenate([low, high], axis=0))
        gated = base_ref[:, lanes] + factor_ref[:, lanes] * carried
        for k in range(0, block, LANES):
            column = gated[:, k : k + LANES]
            row = (first + k) // LANES
            out_ref[:, first + k : first + k + LANES] = (column * gain_ref[row : row + 1, :]).astype(BF16)
            sums += column * column
    for first_ref in first_refs:
        send_kernel(0, out_ref, weight_ref, first_ref)
    square_ref[...] = jnp.broadcast_to(jnp.sum(sums.T, axis=0, keepdims=True), square_ref.shape)


def gated_part(mine, other, base, factor, read_proj, gain, weight, first):
    tokens, width = base.shape
    return local_call(
        gated_kernel,
        "gated_part",
        [
            jax.ShapeDtypeStruct((tokens, width), BF16),
            jax.ShapeDtypeStruct((8, tokens), F32),
        ]
        + [jax.ShapeDtypeStruct((tokens, first), BF16)] * (first > 0),
        (mine, other, base, factor, read_proj, gain, weight),
        flops=2 * tokens * width * STATE,
    )


SENDS = (512, 384, 384)


def columns_of(weight_ref, other, first, count):
    columns = weight_ref.shape[1] // 2
    member = lax.axis_index("tensor")
    start = (1 - member if other else member) * columns + first
    return weight_ref[:, pl.ds(pl.multiple_of(start, LANES), count)]


def send_kernel(first, gated_ref, weight_ref, *refs):
    out_ref = refs[-1]
    tokens, count = gated_ref.shape[0], out_ref.shape[1]
    out_ref[:tokens, :] = dot(gated_ref[...], columns_of(weight_ref, True, first, count)).astype(BF16)
    for square_ref in refs[:-1]:
        out_ref[tokens:, :] = jnp.zeros((16, count), BF16)
        for lane in range(0, tokens, LANES):
            lanes = slice(lane, lane + LANES)
            out_ref[tokens:, lanes] = decay_block(square_ref[:1, lanes], 16)


def own_kernel(gated_ref, weight_ref, out_ref):
    gated, count = gated_ref[...], out_ref.shape[1] // 5
    for first in range(0, out_ref.shape[1], count):
        out_ref[:, first : first + count] = dot(gated, columns_of(weight_ref, False, first, count))


def finish_kernel(squares_ref, own_ref, *refs):
    *got_refs, out_ref, sent_ref, sems = refs
    tokens = own_ref.shape[0]
    other_squares = got_refs[-1][tokens:, :tokens].astype(F32)
    mean = (squares_ref[:1] + jnp.sum(other_squares, axis=0, keepdims=True)) / INNER
    scale = lax.rsqrt(mean + EPSILON)
    scale = jnp.broadcast_to(scale, (LANES, tokens)).T
    first, copies = 0, []
    for got_ref in got_refs:
        count = got_ref.shape[1]
        for lane in range(0, count, LANES):
            lanes = slice(first + lane, first + lane + LANES)
            total = own_ref[:, lanes] + got_ref[:tokens, lane : lane + LANES].astype(F32)
            sent_ref[:, lanes] = (total * scale).astype(BF16)
        lanes = pl.ds(first, count)
        copies.append(
            pltpu.make_async_copy(sent_ref.at[:, lanes], out_ref.at[:, lanes], sems.at[len(copies)])
        )
        copies[-1].start()
        first += count
    for copy in copies:
        copy.wait()


def finish(squares, own, got):
    args = (squares, own, *got)
    return pl.pallas_call(
        finish_kernel,
        name="finish",
        out_shape=jax.ShapeDtypeStruct(own.shape, BF16),
        in_specs=[IN_VMEM] * len(args),
        out_specs=IN_HBM,
        scratch_shapes=[
            pltpu.VMEM(own.shape, BF16),
            pltpu.SemaphoreType.DMA((len(got),)),
        ],
        compiler_params=pltpu.CompilerParams(vmem_limit_bytes=8 * MIB),
    )(*args)


def direct(members, columns):
    return members == 2 and columns == sum(SENDS)


def layer_columns(members, gated, squares, weight, ready):
    columns = weight.shape[1] // members
    if not direct(members, columns):
        mean = lax.psum(squares[0], "tensor") / INNER
        partial = dot(gated, weight).astype(BF16)
        total = lax.psum_scatter(partial, "tensor", scatter_dimension=1, tiled=True)
        return (total.astype(F32) * lax.rsqrt(mean + EPSILON)[:, None]).astype(BF16)
    swap = [(0, 1), (1, 0)]
    tokens = gated.shape[0]
    parts, first = [ready[0]], SENDS[0]
    for count in SENDS[1:]:
        last = first + count == columns
        parts += local_call(
            functools.partial(send_kernel, first),
            "project_other",
            [jax.ShapeDtypeStruct((tokens + 16 * last, count), BF16)],
            (gated, weight) + (squares,) * last,
            after=parts[-1:],
        )
        first += count
    got = [lax.ppermute(part, "tensor", swap) for part in parts]
    (own,) = local_call(
        own_kernel,
        "project_own",
        [jax.ShapeDtypeStruct((tokens, columns), F32)],
        (gated, weight),
        after=parts[-1:],
    )
    return finish(squares, own, got)


def on_device(
    chips,
    members,
    signal,
    gate_branch,
    write_proj,
    read_proj,
    step_logits,
    valid_mask,
    stretch_band,
    band_offset,
    decay_log,
    step_offset,
    skip_gain,
    norm_gain,
    out_weight,
):
    small = (step_logits, valid_mask[None], band_offset, decay_log[None], step_offset[None])
    running, weight, decay, keep, send, *passed = own_state(
        stretch_band, small, write_proj, read_proj, signal, gate_branch
    )
    cores = [(0, 1), (1, 0)]
    got = lax.ppermute(send, "band", cores)
    state, first, second = chip_state(keep, got, decay)
    constants = (skip_gain[None], norm_gain.reshape(-1, LANES), out_weight)

    def local(after):
        return local_part((running, weight, decay, got, *passed), constants, after)

    mine, give, base, factor, gain, matrix = entering_state(
        chips, state, first, second, keep, got, local
    )
    other = lax.ppermute(give, "band", cores)
    ahead = SENDS[0] if direct(members, matrix.shape[1] // members) else 0
    gated, squares, *ready = gated_part(
        mine, other, base, factor, passed[1], gain, matrix, ahead
    )
    return layer_columns(members, gated, squares, matrix, ready)


def solution(mesh):
    placed = (
        P(("group", "scan", "band"), "tensor"),
        P(("group", "scan", "band"), "tensor"),
        P(("group", "scan", "band"), None),
        P(("group", "scan", "band"), None),
        P("tensor", ("group", "scan", "band")),
        P(("group", "scan", "band")),
        P(("group", "scan", "band")),
        P(None, "tensor"),
        P("tensor"),
        P("tensor"),
        P("tensor"),
        P("tensor"),
        P("tensor", None),
    )
    return jax.shard_map(
        functools.partial(on_device, mesh.shape["scan"], mesh.shape["tensor"]),
        mesh=mesh,
        in_specs=placed,
        out_specs=P(("group", "scan", "band"), "tensor"),
        check_vma=False,
    )
```

```python
import functools

import jax
import jax.numpy as jnp
from jax import lax
from jax.experimental import pallas as pl
from jax.experimental.pallas import tpu as pltpu
from jax.sharding import PartitionSpec as P

HEAD_DIM = 64
STATE = 128
HALF = STATE // 2
PART = HALF // 2
STRETCH = 256
BANDS = 12
INNER = 5120
LANES = 128

EPSILON = 1e-05
HIGHEST = lax.Precision.HIGHEST
F32 = jnp.float32
BF16 = jnp.bfloat16
MIB = 1 << 20


def dot(a, b):
    return lax.dot_general(a, b, (((1,), (0,)), ((), ())), preferred_element_type=F32)


def pieces(x):
    high = x.astype(BF16)
    rest = x - high.astype(F32)
    middle = rest.astype(BF16)
    return high, middle, (rest - middle.astype(F32)).astype(BF16)


def head_of_lane(heads, lanes, group, first=0):
    row = lax.broadcasted_iota(jnp.int32, (heads, lanes), 0)
    lane = lax.broadcasted_iota(jnp.int32, (heads, lanes), 1)
    return (row == first + lax.shift_right_logical(lane, group)).astype(F32).astype(BF16)


def slot_of(heads):
    return -(-heads // 8) * 8


def piece_rows(values, ref):
    heads = values.shape[0]
    ref[...] = jnp.zeros(ref.shape, F32)
    for k, piece in enumerate(pieces(values)):
        first = k * slot_of(heads)
        ref[first : first + heads, :] = piece.astype(F32)
    return ref[...]


def piece_map(heads, lanes, group, first=0):
    away = (
        lax.broadcasted_iota(jnp.int32, (LANES, lanes), 0)
        - lax.shift_right_logical(lax.broadcasted_iota(jnp.int32, (LANES, lanes), 1), group)
        - first
    )
    slot = slot_of(heads)
    hit = (away == 0) | (away == slot) | (away == 2 * slot)
    return jnp.where(hit, 1.0, 0.0).astype(BF16)


def spread_heads(row, heads_map):
    return sum(dot(piece, heads_map) for piece in pieces(jnp.broadcast_to(row, (8, row.shape[1]))))[:1]


def diagonal(rows, lanes):
    return lax.broadcasted_iota(jnp.int32, (rows, lanes), 0) == lax.broadcasted_iota(
        jnp.int32, (rows, lanes), 1
    )


def to_column(row):
    count = row.shape[1]
    return jnp.sum(jnp.where(diagonal(count, count), row, 0.0), axis=1, keepdims=True)


def decay_block(row, rows):
    place = lax.broadcasted_iota(jnp.int32, (rows, LANES), 0)
    high, middle, low = (piece.astype(F32) for piece in pieces(row))
    block = jnp.where(place == 0, high, jnp.where(place == 1, middle, jnp.where(place == 2, low, 0.0)))
    return block.astype(BF16)


def decay_row(block):
    return jnp.sum(block.astype(F32), axis=0, keepdims=True)


def decay_lanes(block, heads_map):
    return jnp.sum(dot(block[:16], heads_map), axis=0, keepdims=True)


def column_block(width):
    return width // 5 if width % (5 * LANES) == 0 else width


def local_call(body, name, outs, args, scratch=(), limit=8 * MIB, flops=0, after=()):
    size = sum(a.size * a.dtype.itemsize for a in args) + sum(o.size * o.dtype.itemsize for o in outs)

    def kernel(*refs):
        body(*refs[: len(args)], *refs[len(args) + len(after) :])

    return pl.pallas_call(
        kernel,
        name=name,
        out_shape=outs,
        in_specs=[pl.BlockSpec(memory_space=pltpu.VMEM)] * len(args)
        + [pl.BlockSpec(memory_space=pl.ANY)] * len(after),
        out_specs=[pl.BlockSpec(memory_space=pltpu.VMEM)] * len(outs),
        scratch_shapes=list(scratch),
        compiler_params=pltpu.CompilerParams(vmem_limit_bytes=limit),
        cost_estimate=pl.CostEstimate(flops=flops, bytes_accessed=size, transcendentals=0),
    )(*args, *after)


IN_VMEM = pl.BlockSpec(memory_space=pltpu.VMEM)
IN_HBM = pl.BlockSpec(memory_space=pltpu.HBM)
ANYWHERE = pl.BlockSpec(memory_space=pl.ANY)


def in_hbm(*arrays):
    return [pltpu.with_memory_space_constraint(a, pltpu.HBM) for a in arrays]


def state_kernel(
    band_ref,
    logits_hbm,
    mask_hbm,
    offset_hbm,
    decay_log_hbm,
    step_offset_hbm,
    write_hbm,
    read_hbm,
    signal_hbm,
    gate_hbm,
    running_ref,
    weight_ref,
    decay_ref,
    keep_ref,
    send_ref,
    write_ref,
    read_ref,
    signal_ref,
    gate_ref,
    logits_ref,
    mask_ref,
    offset_ref,
    decay_log_ref,
    step_offset_ref,
    rows_ref,
    sems,
    block_sems,
):
    heads, tokens = logits_ref.shape
    width = signal_ref.shape[1]
    block = column_block(width)
    is_first = lax.axis_index("band") == 0
    pairs = (
        (logits_hbm, logits_ref),
        (mask_hbm, mask_ref),
        (offset_hbm, offset_ref),
        (decay_log_hbm, decay_log_ref),
        (step_offset_hbm, step_offset_ref),
        (write_hbm, write_ref),
        (read_hbm, read_ref),
        (gate_hbm, gate_ref),
    )
    copies = [pltpu.make_async_copy(*pair, sems.at[i]) for i, pair in enumerate(pairs)]
    blocks = [
        pltpu.make_async_copy(
            signal_hbm.at[:, pl.ds(first, block)],
            signal_ref.at[:, pl.ds(first, block)],
            block_sems.at[first // block],
        )
        for first in range(0, width, block)
    ]
    for copy in copies[:6] + blocks + copies[6:]:
        copy.start()
    for copy in copies[:6]:
        copy.wait()

    offset = to_column(step_offset_ref[...] + offset_ref[pl.ds(band_ref[0], 1), :])
    raw = logits_ref[...] + offset
    step_size = jnp.maximum(raw, 0.0) + jnp.log1p(jnp.exp(-jnp.abs(raw)))
    log_decay = step_size * to_column(-jnp.exp(decay_log_ref[...]))
    earlier = lax.broadcasted_iota(jnp.int32, (tokens, tokens), 0)
    later = lax.broadcasted_iota(jnp.int32, (tokens, tokens), 1)
    sums = dot(
        piece_rows(log_decay, rows_ref).astype(BF16), jnp.where(earlier <= later, 1.0, 0.0).astype(BF16)
    )
    slot = slot_of(heads)
    running = sums[:heads] + sums[slot : slot + heads] + sums[2 * slot : 2 * slot + heads]
    weight = step_size * mask_ref[...].astype(F32)
    running_ref[...] = running
    weight_ref[...] = weight
    total = running[:, tokens - 1 : tokens]
    row = jnp.sum(jnp.where(diagonal(heads, LANES), jnp.exp(total), 0.0), axis=0, keepdims=True)
    send_ref[:, width:] = decay_block(row, HALF)
    decay_ref[...] = decay_block(row, 16)

    tail = piece_rows(jnp.exp(total - running) * weight, rows_ref).T.astype(BF16)
    write = write_ref[...].astype(F32).T
    low, high = write[:HALF], write[HALF:]
    write = jnp.concatenate(
        [jnp.where(is_first, low, high), jnp.where(is_first, high, low)], axis=0
    ).astype(BF16)
    for copy, first in zip(blocks, range(0, width, block)):
        lanes = slice(first, first + block)
        factors = dot(tail, piece_map(heads, block, 6, first // HEAD_DIM))
        copy.wait()
        state = dot(write, (signal_ref[:, lanes].astype(F32) * factors).astype(BF16))
        keep_ref[:, lanes] = state[:HALF]
        send_ref[:, lanes] = state[HALF:].astype(BF16)
    for copy in copies[6:]:
        copy.wait()


def own_state(stretch_band, small, write_proj, read_proj, signal, gate_branch):
    tokens, width = signal.shape
    heads = small[0].shape[0]
    passed = (write_proj, read_proj, signal, gate_branch)
    return pl.pallas_call(
        state_kernel,
        name="own_state",
        out_shape=[
            jax.ShapeDtypeStruct((heads, tokens), F32),
            jax.ShapeDtypeStruct((heads, tokens), F32),
            jax.ShapeDtypeStruct((16, LANES), BF16),
            jax.ShapeDtypeStruct((HALF, width), F32),
            jax.ShapeDtypeStruct((HALF, width + LANES), BF16),
        ]
        + [jax.ShapeDtypeStruct(a.shape, a.dtype) for a in passed],
        in_specs=[pl.BlockSpec(memory_space=pltpu.SMEM)] + [IN_HBM] * 9,
        out_specs=[IN_VMEM] * 9,
        scratch_shapes=[pltpu.VMEM(a.shape, a.dtype) for a in small]
        + [
            pltpu.VMEM((LANES, tokens), F32),
            pltpu.SemaphoreType.DMA((8,)),
            pltpu.SemaphoreType.DMA((width // column_block(width),)),
        ],
        compiler_params=pltpu.CompilerParams(vmem_limit_bytes=16 * MIB),
        cost_estimate=pl.CostEstimate(
            flops=4 * tokens * width * STATE, bytes_accessed=tokens * width * 2, transcendentals=0
        ),
    )(stretch_band, *in_hbm(*small, *passed))


def prepare_local(
    running_ref, write_ref, read_ref, decay_ref, got_ref, scores_ref, running_pieces_ref, decay_pieces_ref, lanes_ref, rows_ref
):
    width = lanes_ref.shape[1]
    scores = lax.dot_general(
        read_ref[...], write_ref[...], (((1,), (1,)), ((), ())), preferred_element_type=F32
    )
    row = lax.broadcasted_iota(jnp.int32, scores.shape, 0)
    lane = lax.broadcasted_iota(jnp.int32, scores.shape, 1)
    scores_ref[...] = jnp.where(row >= lane, scores, 0.0)
    running = running_ref[...]
    running_pieces_ref[...] = piece_rows(running, rows_ref).T.astype(BF16)
    decay_pieces_ref[...] = piece_rows(jnp.exp(running), rows_ref).T.astype(BF16)
    mine, got = decay_ref[...].astype(F32), got_ref[:16, width:].astype(F32)
    first_core = jnp.where(lax.axis_index("band") == 0, mine, got).astype(BF16)
    lanes_ref[...] = jnp.broadcast_to(
        decay_lanes(first_core, head_of_lane(LANES, width, 6)), lanes_ref.shape
    )


def local_heads(
    first_block,
    running_ref,
    weight_ref,
    signal_ref,
    gate_ref,
    scores_ref,
    running_pieces_ref,
    decay_pieces_ref,
    skip_ref,
    base_ref,
    factor_ref,
):
    heads, tokens = running_ref.shape
    block = column_block(signal_ref.shape[1])
    half = tokens // 2
    low_lanes = lax.broadcasted_iota(jnp.int32, (half, LANES), 1) < HEAD_DIM
    early, late = slice(0, half), slice(half, tokens)

    def heads_block(at, _):
        first_head = (first_block + at) * (block // HEAD_DIM)

        def whole_lanes(lane, count):
            return pl.ds(pl.multiple_of((first_block + at) * block + lane, LANES), count)

        def part_lanes(lane, count):
            return pl.ds(pl.multiple_of(at * block + lane, LANES), count)

        wide = dot(running_pieces_ref[...], piece_map(heads, block * 2, 7, first_head))
        gate = gate_ref[:, whole_lanes(0, block)].astype(F32)
        gate = gate / (1.0 + jnp.exp(-gate))
        factor_ref[:, part_lanes(0, block)] = (
            dot(decay_pieces_ref[...], piece_map(heads, block, 6, first_head)) * gate
        )
        skip = spread_heads(skip_ref[...], head_of_lane(heads, block, 6, first_head))
        for pair in range(block // LANES):
            lanes = slice(pair * LANES, (pair + 1) * LANES)
            values = signal_ref[:, whole_lanes(pair * LANES, LANES)]
            top, bottom = [], []
            for k in (2 * pair, 2 * pair + 1):
                row = running_ref[pl.ds(first_head + k, 1), :]
                weight = weight_ref[pl.ds(first_head + k, 1), :]
                column = wide[:, k * LANES : (k + 1) * LANES]

                def mixing(rows, cols):
                    span = jnp.minimum(column[rows] - row[:, cols], 0.0)
                    return (jnp.exp(span) * scores_ref[rows, cols] * weight[:, cols]).astype(BF16)

                top.append(mixing(early, early))
                bottom.append(jnp.concatenate([mixing(late, early), mixing(late, late)], axis=1))
            top = dot(jnp.concatenate(top, axis=0), values[early])
            bottom = dot(jnp.concatenate(bottom, axis=0), values)
            skipped = values.astype(F32) * skip[:, lanes]
            out_lanes = part_lanes(pair * LANES, LANES)
            base_ref[early, out_lanes] = (
                jnp.where(low_lanes, top[:half], top[half:]) + skipped[early]
            ) * gate[early, lanes]
            base_ref[late, out_lanes] = (
                jnp.where(low_lanes, bottom[:half], bottom[half:]) + skipped[late]
            ) * gate[late, lanes]
        return 0

    lax.fori_loop(0, base_ref.shape[1] // block, heads_block, 0)


def local_first_kernel(
    running_ref,
    weight_ref,
    signal_ref,
    gate_ref,
    write_ref,
    read_ref,
    decay_ref,
    got_ref,
    skip_hbm,
    gain_hbm,
    matrix_hbm,
    after_ref,
    base_ref,
    factor_ref,
    matrix_ref,
    gain_ref,
    scores_ref,
    running_pieces_ref,
    decay_pieces_ref,
    skip_ref,
    lanes_ref,
    rows_ref,
    sems,
):
    rows = matrix_ref.shape[0]
    pairs = (
        (skip_hbm, skip_ref),
        (gain_hbm, gain_ref),
        (matrix_hbm.at[pl.ds(0, rows), :], matrix_ref),
    )
    copies = [pltpu.make_async_copy(*pair, sems.at[i]) for i, pair in enumerate(pairs)]
    for copy in copies:
        copy.start()
    prepared = (scores_ref, running_pieces_ref, decay_pieces_ref)
    prepare_local(running_ref, write_ref, read_ref, decay_ref, got_ref, *prepared, lanes_ref, rows_ref)
    copies[0].wait()
    local_heads(
        0, running_ref, weight_ref, signal_ref, gate_ref, *prepared, skip_ref, base_ref, factor_ref
    )
    for copy in copies[1:]:
        copy.wait()


def local_rest_kernel(
    running_ref,
    weight_ref,
    signal_ref,
    gate_ref,
    scores_ref,
    running_pieces_ref,
    decay_pieces_ref,
    skip_ref,
    matrix_hbm,
    after_ref,
    base_ref,
    factor_ref,
    matrix_ref,
    sem,
):
    rows = matrix_ref.shape[0]
    copy = pltpu.make_async_copy(
        matrix_hbm.at[pl.ds(matrix_hbm.shape[0] - rows, rows), :], matrix_ref, sem
    )
    copy.start()
    local_heads(
        (signal_ref.shape[1] - rows) // column_block(signal_ref.shape[1]),
        running_ref,
        weight_ref,
        signal_ref,
        gate_ref,
        scores_ref,
        running_pieces_ref,
        decay_pieces_ref,
        skip_ref,
        base_ref,
        factor_ref,
    )
    copy.wait()


def first_columns(width):
    return 4 * (width // 5) if width % (5 * LANES) == 0 else width // 2


def local_call_of(kernel, name, heads, columns, outs, resident, passed, after, scratch):
    tokens = resident[0].shape[1]
    matrix = passed[-1]
    return pl.pallas_call(
        kernel,
        name=name,
        out_shape=[jax.ShapeDtypeStruct((tokens, columns), F32)] * 2
        + [jax.ShapeDtypeStruct((columns, matrix.shape[1]), BF16)]
        + outs,
        in_specs=[IN_VMEM] * len(resident) + [IN_HBM] * len(passed) + [ANYWHERE],
        out_specs=[IN_VMEM] * (3 + len(outs)),
        scratch_shapes=scratch,
        compiler_params=pltpu.CompilerParams(vmem_limit_bytes=16 * MIB),
        cost_estimate=pl.CostEstimate(
            flops=6 * columns * tokens * tokens,
            bytes_accessed=tokens * columns * 12,
            transcendentals=columns // HEAD_DIM * tokens * tokens,
        ),
    )(*resident, *in_hbm(*passed), after)


def local_first(values, constants, after):
    running, signal = values[0], values[2]
    skip_gain, norm_gain, _ = constants
    heads, tokens = running.shape
    width = signal.shape[1]
    pieces_shape = jax.ShapeDtypeStruct((tokens, LANES), BF16)
    return local_call_of(
        local_first_kernel,
        "local_first",
        heads,
        first_columns(width),
        [
            jax.ShapeDtypeStruct(norm_gain.shape, F32),
            jax.ShapeDtypeStruct((tokens, tokens), F32),
            pieces_shape,
            pieces_shape,
            jax.ShapeDtypeStruct(skip_gain.shape, F32),
            jax.ShapeDtypeStruct((8, width), F32),
        ],
        values,
        constants,
        after,
        [pltpu.VMEM((LANES, tokens), F32), pltpu.SemaphoreType.DMA((3,))],
    )


def local_rest(values, prepared, out_weight, after):
    running, signal = values[0], values[2]
    width = signal.shape[1]
    return local_call_of(
        local_rest_kernel,
        "local_rest",
        running.shape[0],
        width - first_columns(width),
        [],
        (*values, *prepared),
        (out_weight,),
        after,
        [pltpu.SemaphoreType.DMA(())],
    )


def chip_kernel(keep_ref, got_ref, decay_ref, state_ref, first_ref, second_ref):
    width = keep_ref.shape[1]
    core = lax.axis_index("band")
    chip = lax.axis_index("scan")
    heads_map = head_of_lane(LANES, width, 6)
    got_decay = got_ref[:16, width:]
    mine = decay_ref[...]
    later = jnp.where(core == 0, got_decay.astype(F32), mine.astype(F32)).astype(BF16)
    lanes = decay_lanes(later, heads_map)
    got = got_ref[:, :width].astype(F32)
    keep = keep_ref[...]
    early, late = jnp.where(core == 0, keep, got), jnp.where(core == 0, got, keep)
    state_ref[:, :width] = (early * lanes + late).astype(BF16)
    block = decay_block(decay_row(got_decay) * decay_row(mine), PART)
    state_ref[:PART, width:] = block
    state_ref[PART:, width:] = block

    def rows(second):
        return state_ref[pl.ds(pl.multiple_of(jnp.where(second, PART, 0), PART), PART), :]

    first_ref[:, : width + LANES] = rows(chip == 1)
    first_ref[:, width + LANES :] = jnp.zeros((PART, LANES), BF16)
    second_ref[...] = rows(chip != 2)


def early_kernel(state_ref, near_ref, out_ref):
    width = out_ref.shape[1] - LANES
    chip = lax.axis_index("scan")
    out_ref[:, width:] = jnp.zeros((PART, LANES), BF16)

    @pl.when(chip == 0)
    def _():
        out_ref[:, :width] = state_ref[PART:, :width]

    @pl.when(chip == 1)
    def _():
        lanes = decay_lanes(state_ref[:16, width : width + LANES], head_of_lane(LANES, width, 6))
        out_ref[:, :width] = (
            lanes * near_ref[:, :width].astype(F32) + state_ref[:PART, :width].astype(F32)
        ).astype(BF16)


def middle_kernel(state_ref, near_ref, far_ref, early_ref, out_ref, lanes_ref):
    width = out_ref.shape[1]
    chip = lax.axis_index("scan")
    decays = slice(width, width + LANES)

    @pl.when(chip < 2)
    def _():
        out_ref[...] = early_ref[:, :width]

    @pl.when(chip == 2)
    def _():
        heads_map = head_of_lane(LANES, width, 6)
        lanes = decay_lanes(near_ref[:16, decays], heads_map)
        lanes_ref[...] = jnp.broadcast_to(lanes, lanes_ref.shape)
        entered = lanes * far_ref[:, :width].astype(F32) + near_ref[:, :width].astype(F32)
        own = decay_lanes(state_ref[:16, decays], heads_map)
        out_ref[...] = (own * entered + state_ref[PART:, :width].astype(F32)).astype(BF16)

    @pl.when(chip == 3)
    def _():
        lanes = decay_lanes(far_ref[:16, decays], head_of_lane(LANES, width, 6))
        lanes_ref[...] = jnp.broadcast_to(lanes, lanes_ref.shape)


def enter_kernel(
    near_ref, far_ref, early_ref, last_ref, far_lanes_ref, keep_ref, got_ref, lanes_ref, mine_ref, send_ref
):
    width = keep_ref.shape[1]
    chip = lax.axis_index("scan")
    near, far, early = (ref.at[:, pl.ds(0, width)] for ref in (near_ref, far_ref, early_ref))

    def parts(first, second):
        enter = jnp.concatenate([first.astype(F32), second.astype(F32)], axis=0)
        share_enter(enter, keep_ref, got_ref, lanes_ref, mine_ref, send_ref)

    @pl.when(chip == 0)
    def _():
        share_enter(jnp.zeros((HALF, width), F32), keep_ref, got_ref, lanes_ref, mine_ref, send_ref)

    @pl.when(chip == 1)
    def _():
        parts(near[...], early[...])

    @pl.when(chip == 2)
    def _():
        parts(last_ref[...], far_lanes_ref[:1] * far[...].astype(F32) + near[...].astype(F32))

    @pl.when(chip == 3)
    def _():
        parts(far_lanes_ref[:1] * early[...].astype(F32) + far[...].astype(F32), last_ref[...])


def share_enter(enter, keep_ref, got_ref, lanes_ref, mine_ref, send_ref):
    width = keep_ref.shape[1]
    core = lax.axis_index("band")

    @pl.when(core == 0)
    def _():
        mine_ref[...] = enter.astype(BF16)
        send_ref[...] = (lanes_ref[:1] * enter + keep_ref[...]).astype(BF16)

    @pl.when(core == 1)
    def _():
        send_ref[...] = enter.astype(BF16)
        mine_ref[...] = (lanes_ref[:1] * enter + got_ref[:, :width].astype(F32)).astype(BF16)


def gathered_kernel(all_ref, keep_ref, got_ref, lanes_ref, mine_ref, send_ref, enter_ref):
    width = keep_ref.shape[1]
    chip = lax.axis_index("scan")
    heads_map = head_of_lane(LANES, width, 6)
    enter_ref[...] = jnp.zeros(enter_ref.shape, F32)
    for source in range(all_ref.shape[0]):

        @pl.when(source < chip)
        def _():
            lanes = decay_lanes(all_ref[source, :16, width:], heads_map)
            enter_ref[...] = lanes * enter_ref[...] + all_ref[source, :, :width].astype(F32)

    share_enter(enter_ref[...], keep_ref, got_ref, lanes_ref, mine_ref, send_ref)


def chip_state(keep, got, decay):
    width = keep.shape[1]
    return local_call(
        chip_kernel,
        "chip_state",
        [
            jax.ShapeDtypeStruct((HALF, width + LANES), BF16),
            jax.ShapeDtypeStruct((PART, width + 2 * LANES), BF16),
            jax.ShapeDtypeStruct((PART, width + LANES), BF16),
        ],
        (keep, got, decay),
    )


def entering_state(chips, state, first, second, keep, got, local_one, local_two):
    width = keep.shape[1]
    half = jax.ShapeDtypeStruct((HALF, width), BF16)
    if chips != 4:
        gathered = lax.all_gather(state, "scan", axis=0)
        locals_one, lanes = local_one(first)
        locals_two = local_two(locals_one[0])
        mine, give = local_call(
            gathered_kernel,
            "enter_state",
            [half, half],
            (gathered, keep, got, lanes),
            (pltpu.VMEM((HALF, width), F32),),
        )
        return mine, give, locals_one, locals_two
    near = lax.ppermute(first, "scan", [(0, 1), (1, 2)])
    far = lax.ppermute(second, "scan", [(0, 2), (2, 3)])
    locals_one, lanes = local_one(first)
    (ahead,) = local_call(
        early_kernel,
        "early_state",
        [jax.ShapeDtypeStruct((PART, width + LANES), BF16)],
        (state, near),
        after=(lanes,),
    )
    early = lax.ppermute(ahead, "scan", [(1, 3), (0, 1)])
    middle, far_lanes = local_call(
        middle_kernel,
        "middle_state",
        [jax.ShapeDtypeStruct((PART, width), BF16), jax.ShapeDtypeStruct((8, width), F32)],
        (state, near, far, ahead),
    )
    locals_two = local_two(middle)
    last = lax.ppermute(middle, "scan", [(1, 2), (2, 3)])
    mine, give = local_call(
        enter_kernel,
        "enter_state",
        [half, half],
        (near, far, early, last, far_lanes, keep, got, lanes),
        after=(locals_two[0],),
    )
    return mine, give, locals_one, locals_two


def gated_kernel(
    mine_ref,
    other_ref,
    base_ref,
    base_rest_ref,
    factor_ref,
    factor_rest_ref,
    read_ref,
    gain_ref,
    weight_ref,
    weight_rest_ref,
    out_ref,
    square_ref,
    *first_refs,
):
    tokens, width = out_ref.shape
    block = column_block(width)
    is_first = lax.axis_index("band") == 0
    read = read_ref[...]
    sums = jnp.zeros((tokens, LANES), F32)
    for first in range(0, width, block):
        lanes = slice(first, first + block)
        mine, other = mine_ref[:, lanes].astype(F32), other_ref[:, lanes].astype(F32)
        low = jnp.where(is_first, mine, other).astype(BF16)
        high = jnp.where(is_first, other, mine).astype(BF16)
        carried = dot(read, jnp.concatenate([low, high], axis=0))
        base, factor, start = base_ref, factor_ref, first
        if first >= base_ref.shape[1]:
            base, factor, start = base_rest_ref, factor_rest_ref, first - base_ref.shape[1]
        gated = base[:, start : start + block] + factor[:, start : start + block] * carried
        for k in range(0, block, LANES):
            column = gated[:, k : k + LANES]
            row = (first + k) // LANES
            out_ref[:, first + k : first + k + LANES] = (column * gain_ref[row : row + 1, :]).astype(BF16)
            sums += column * column
    for first_ref in first_refs:
        send_kernel(0, out_ref, weight_ref, weight_rest_ref, first_ref)
    square_ref[...] = jnp.broadcast_to(jnp.sum(sums.T, axis=0, keepdims=True), square_ref.shape)


def gated_part(mine, other, bases, factors, read_proj, gain, weights, first):
    tokens = read_proj.shape[0]
    width = mine.shape[1]
    return local_call(
        gated_kernel,
        "gated_part",
        [
            jax.ShapeDtypeStruct((tokens, width), BF16),
            jax.ShapeDtypeStruct((8, tokens), F32),
        ]
        + [jax.ShapeDtypeStruct((tokens, first), BF16)] * (first > 0),
        (mine, other, *bases, *factors, read_proj, gain, *weights),
        flops=2 * tokens * width * STATE,
    )


SENDS = (512, 384, 384)


def project(gated_ref, weight_ref, weight_rest_ref, other, first, count):
    columns = weight_ref.shape[1] // 2
    member = lax.axis_index("tensor")
    start = (1 - member if other else member) * columns + first
    lanes = pl.ds(pl.multiple_of(start, LANES), count)
    rows = weight_ref.shape[0]
    return dot(gated_ref[:, :rows], weight_ref[:, lanes]) + dot(
        gated_ref[:, rows:], weight_rest_ref[:, lanes]
    )


def send_kernel(first, gated_ref, weight_ref, weight_rest_ref, *refs):
    out_ref = refs[-1]
    tokens, count = gated_ref.shape[0], out_ref.shape[1]
    out_ref[:tokens, :] = project(
        gated_ref, weight_ref, weight_rest_ref, True, first, count
    ).astype(BF16)
    for square_ref in refs[:-1]:
        out_ref[tokens:, :] = jnp.zeros((16, count), BF16)
        for lane in range(0, tokens, LANES):
            lanes = slice(lane, lane + LANES)
            out_ref[tokens:, lanes] = decay_block(square_ref[:1, lanes], 16)


def own_kernel(gated_ref, weight_ref, weight_rest_ref, out_ref):
    count = out_ref.shape[1] // 5
    for first in range(0, out_ref.shape[1], count):
        out_ref[:, first : first + count] = project(
            gated_ref, weight_ref, weight_rest_ref, False, first, count
        )


def finish_kernel(squares_ref, own_ref, *refs):
    *got_refs, out_ref, sent_ref, sems = refs
    tokens = own_ref.shape[0]
    other_squares = got_refs[-1][tokens:, :tokens].astype(F32)
    mean = (squares_ref[:1] + jnp.sum(other_squares, axis=0, keepdims=True)) / INNER
    scale = lax.rsqrt(mean + EPSILON)
    scale = jnp.broadcast_to(scale, (LANES, tokens)).T
    first, copies = 0, []
    for got_ref in got_refs:
        count = got_ref.shape[1]
        for lane in range(0, count, LANES):
            lanes = slice(first + lane, first + lane + LANES)
            total = own_ref[:, lanes] + got_ref[:tokens, lane : lane + LANES].astype(F32)
            sent_ref[:, lanes] = (total * scale).astype(BF16)
        lanes = pl.ds(first, count)
        copies.append(
            pltpu.make_async_copy(sent_ref.at[:, lanes], out_ref.at[:, lanes], sems.at[len(copies)])
        )
        copies[-1].start()
        first += count
    for copy in copies:
        copy.wait()


def finish(squares, own, got):
    args = (squares, own, *got)
    return pl.pallas_call(
        finish_kernel,
        name="finish",
        out_shape=jax.ShapeDtypeStruct(own.shape, BF16),
        in_specs=[IN_VMEM] * len(args),
        out_specs=IN_HBM,
        scratch_shapes=[
            pltpu.VMEM(own.shape, BF16),
            pltpu.SemaphoreType.DMA((len(got),)),
        ],
        compiler_params=pltpu.CompilerParams(vmem_limit_bytes=8 * MIB),
    )(*args)


def direct(members, columns):
    return members == 2 and columns == sum(SENDS)


def layer_columns(members, gated, squares, weights, ready):
    columns = weights[0].shape[1] // members
    if not direct(members, columns):
        mean = lax.psum(squares[0], "tensor") / INNER
        partial = dot(gated, jnp.concatenate(weights, axis=0)).astype(BF16)
        total = lax.psum_scatter(partial, "tensor", scatter_dimension=1, tiled=True)
        return (total.astype(F32) * lax.rsqrt(mean + EPSILON)[:, None]).astype(BF16)
    swap = [(0, 1), (1, 0)]
    tokens = gated.shape[0]
    parts, first = [ready[0]], SENDS[0]
    for count in SENDS[1:]:
        last = first + count == columns
        parts += local_call(
            functools.partial(send_kernel, first),
            "project_other",
            [jax.ShapeDtypeStruct((tokens + 16 * last, count), BF16)],
            (gated, *weights) + (squares,) * last,
            after=parts[-1:],
        )
        first += count
    got = [lax.ppermute(part, "tensor", swap) for part in parts]
    (own,) = local_call(
        own_kernel,
        "project_own",
        [jax.ShapeDtypeStruct((tokens, columns), F32)],
        (gated, *weights),
        after=parts[-1:],
    )
    return finish(squares, own, got)


def on_device(
    chips,
    members,
    signal,
    gate_branch,
    write_proj,
    read_proj,
    step_logits,
    valid_mask,
    stretch_band,
    band_offset,
    decay_log,
    step_offset,
    skip_gain,
    norm_gain,
    out_weight,
):
    small = (step_logits, valid_mask[None], band_offset, decay_log[None], step_offset[None])
    running, weight, decay, keep, send, *passed = own_state(
        stretch_band, small, write_proj, read_proj, signal, gate_branch
    )
    cores = [(0, 1), (1, 0)]
    got = lax.ppermute(send, "band", cores)
    state, first, second = chip_state(keep, got, decay)
    constants = (skip_gain[None], norm_gain.reshape(-1, LANES), out_weight)
    write, read, *streams = passed
    values = (running, weight, *streams)
    prepared = []

    def local_one(after):
        base, factor, matrix, gain, *rest, lanes = local_first(
            (*values, write, read, decay, got), constants, after
        )
        prepared.extend(rest)
        return (base, factor, matrix, gain), lanes

    def local_two(after):
        return local_rest(values, prepared, out_weight, after)

    mine, give, (base, factor, matrix, gain), rest = entering_state(
        chips, state, first, second, keep, got, local_one, local_two
    )
    other = lax.ppermute(give, "band", cores)
    ahead = SENDS[0] if direct(members, matrix.shape[1] // members) else 0
    weights = (matrix, rest[2])
    gated, squares, *ready = gated_part(
        mine, other, (base, rest[0]), (factor, rest[1]), read, gain, weights, ahead
    )
    return layer_columns(members, gated, squares, weights, ready)


def solution(mesh):
    placed = (
        P(("group", "scan", "band"), "tensor"),
        P(("group", "scan", "band"), "tensor"),
        P(("group", "scan", "band"), None),
        P(("group", "scan", "band"), None),
        P("tensor", ("group", "scan", "band")),
        P(("group", "scan", "band")),
        P(("group", "scan", "band")),
        P(None, "tensor"),
        P("tensor"),
        P("tensor"),
        P("tensor"),
        P("tensor"),
        P("tensor", None),
    )
    return jax.shard_map(
        functools.partial(on_device, mesh.shape["scan"], mesh.shape["tensor"]),
        mesh=mesh,
        in_specs=placed,
        out_specs=P(("group", "scan", "band"), "tensor"),
        check_vma=False,
    )
```

```python
import functools

import jax
import jax.numpy as jnp
from jax import lax
from jax.experimental import pallas as pl
from jax.experimental.pallas import tpu as pltpu
from jax.sharding import PartitionSpec as P

HEAD_DIM = 64
STATE = 128
HALF = STATE // 2
PART = HALF // 2
STRETCH = 256
BANDS = 12
INNER = 5120
LANES = 128

EPSILON = 1e-05
HIGHEST = lax.Precision.HIGHEST
F32 = jnp.float32
BF16 = jnp.bfloat16
MIB = 1 << 20


def dot(a, b):
    return lax.dot_general(a, b, (((1,), (0,)), ((), ())), preferred_element_type=F32)


def pieces(x):
    high = x.astype(BF16)
    rest = x - high.astype(F32)
    middle = rest.astype(BF16)
    return high, middle, (rest - middle.astype(F32)).astype(BF16)


def head_of_lane(heads, lanes, group, first=0):
    row = lax.broadcasted_iota(jnp.int32, (heads, lanes), 0)
    lane = lax.broadcasted_iota(jnp.int32, (heads, lanes), 1)
    return (row == first + lax.shift_right_logical(lane, group)).astype(F32).astype(BF16)


def slot_of(heads):
    return -(-heads // 8) * 8


def piece_rows(values, ref):
    heads = values.shape[0]
    ref[...] = jnp.zeros(ref.shape, F32)
    for k, piece in enumerate(pieces(values)):
        first = k * slot_of(heads)
        ref[first : first + heads, :] = piece.astype(F32)
    return ref[...]


def piece_map(heads, lanes, group, first=0):
    away = (
        lax.broadcasted_iota(jnp.int32, (LANES, lanes), 0)
        - lax.shift_right_logical(lax.broadcasted_iota(jnp.int32, (LANES, lanes), 1), group)
        - first
    )
    slot = slot_of(heads)
    hit = (away == 0) | (away == slot) | (away == 2 * slot)
    return jnp.where(hit, 1.0, 0.0).astype(BF16)


def spread_heads(row, heads_map):
    return sum(dot(piece, heads_map) for piece in pieces(jnp.broadcast_to(row, (8, row.shape[1]))))[:1]


def diagonal(rows, lanes):
    return lax.broadcasted_iota(jnp.int32, (rows, lanes), 0) == lax.broadcasted_iota(
        jnp.int32, (rows, lanes), 1
    )


def to_column(row):
    count = row.shape[1]
    return jnp.sum(jnp.where(diagonal(count, count), row, 0.0), axis=1, keepdims=True)


def decay_block(row, rows):
    place = lax.broadcasted_iota(jnp.int32, (rows, LANES), 0)
    high, middle, low = (piece.astype(F32) for piece in pieces(row))
    block = jnp.where(place == 0, high, jnp.where(place == 1, middle, jnp.where(place == 2, low, 0.0)))
    return block.astype(BF16)


def decay_row(block):
    return jnp.sum(block.astype(F32), axis=0, keepdims=True)


def decay_lanes(block, heads_map):
    return jnp.sum(dot(block[:16], heads_map), axis=0, keepdims=True)


def column_block(width):
    return width // 5 if width % (5 * LANES) == 0 else width


def local_call(body, name, outs, args, scratch=(), limit=8 * MIB, flops=0, after=(), aliases=None):
    size = sum(a.size * a.dtype.itemsize for a in args) + sum(o.size * o.dtype.itemsize for o in outs)

    def kernel(*refs):
        body(*refs[: len(args)], *refs[len(args) + len(after) :])

    return pl.pallas_call(
        kernel,
        name=name,
        out_shape=outs,
        in_specs=[pl.BlockSpec(memory_space=pltpu.VMEM)] * len(args)
        + [pl.BlockSpec(memory_space=pl.ANY)] * len(after),
        out_specs=[pl.BlockSpec(memory_space=pltpu.VMEM)] * len(outs),
        scratch_shapes=list(scratch),
        input_output_aliases=aliases or {},
        compiler_params=pltpu.CompilerParams(vmem_limit_bytes=limit),
        cost_estimate=pl.CostEstimate(flops=flops, bytes_accessed=size, transcendentals=0),
    )(*args, *after)


IN_VMEM = pl.BlockSpec(memory_space=pltpu.VMEM)
IN_HBM = pl.BlockSpec(memory_space=pltpu.HBM)
ANYWHERE = pl.BlockSpec(memory_space=pl.ANY)


def in_hbm(*arrays):
    return [pltpu.with_memory_space_constraint(a, pltpu.HBM) for a in arrays]


def state_kernel(
    band_ref,
    logits_hbm,
    mask_hbm,
    offset_hbm,
    decay_log_hbm,
    step_offset_hbm,
    write_hbm,
    read_hbm,
    signal_hbm,
    gate_hbm,
    running_ref,
    weight_ref,
    decay_ref,
    keep_ref,
    send_ref,
    write_ref,
    read_ref,
    signal_ref,
    gate_ref,
    logits_ref,
    mask_ref,
    offset_ref,
    decay_log_ref,
    step_offset_ref,
    rows_ref,
    sems,
    block_sems,
):
    heads, tokens = logits_ref.shape
    width = signal_ref.shape[1]
    block = column_block(width)
    is_first = lax.axis_index("band") == 0
    pairs = (
        (logits_hbm, logits_ref),
        (mask_hbm, mask_ref),
        (offset_hbm, offset_ref),
        (decay_log_hbm, decay_log_ref),
        (step_offset_hbm, step_offset_ref),
        (write_hbm, write_ref),
        (read_hbm, read_ref),
        (gate_hbm, gate_ref),
    )
    copies = [pltpu.make_async_copy(*pair, sems.at[i]) for i, pair in enumerate(pairs)]
    blocks = [
        pltpu.make_async_copy(
            signal_hbm.at[:, pl.ds(first, block)],
            signal_ref.at[:, pl.ds(first, block)],
            block_sems.at[first // block],
        )
        for first in range(0, width, block)
    ]
    for copy in copies[:6] + blocks + copies[6:]:
        copy.start()
    for copy in copies[:6]:
        copy.wait()

    offset = to_column(step_offset_ref[...] + offset_ref[pl.ds(band_ref[0], 1), :])
    raw = logits_ref[...] + offset
    step_size = jnp.maximum(raw, 0.0) + jnp.log1p(jnp.exp(-jnp.abs(raw)))
    log_decay = step_size * to_column(-jnp.exp(decay_log_ref[...]))
    earlier = lax.broadcasted_iota(jnp.int32, (tokens, tokens), 0)
    later = lax.broadcasted_iota(jnp.int32, (tokens, tokens), 1)
    sums = dot(
        piece_rows(log_decay, rows_ref).astype(BF16), jnp.where(earlier <= later, 1.0, 0.0).astype(BF16)
    )
    slot = slot_of(heads)
    running = sums[:heads] + sums[slot : slot + heads] + sums[2 * slot : 2 * slot + heads]
    weight = step_size * mask_ref[...].astype(F32)
    running_ref[...] = running
    weight_ref[...] = weight
    total = running[:, tokens - 1 : tokens]
    row = jnp.sum(jnp.where(diagonal(heads, LANES), jnp.exp(total), 0.0), axis=0, keepdims=True)
    send_ref[:, width:] = decay_block(row, HALF)
    decay_ref[...] = decay_block(row, 16)

    tail = piece_rows(jnp.exp(total - running) * weight, rows_ref).T.astype(BF16)
    write = write_ref[...].astype(F32).T
    low, high = write[:HALF], write[HALF:]
    write = jnp.concatenate(
        [jnp.where(is_first, low, high), jnp.where(is_first, high, low)], axis=0
    ).astype(BF16)
    for copy, first in zip(blocks, range(0, width, block)):
        lanes = slice(first, first + block)
        factors = dot(tail, piece_map(heads, block, 6, first // HEAD_DIM))
        copy.wait()
        state = dot(write, (signal_ref[:, lanes].astype(F32) * factors).astype(BF16))
        keep_ref[:, lanes] = state[:HALF]
        send_ref[:, lanes] = state[HALF:].astype(BF16)
    for copy in copies[6:]:
        copy.wait()


def own_state(stretch_band, small, write_proj, read_proj, signal, gate_branch):
    tokens, width = signal.shape
    heads = small[0].shape[0]
    passed = (write_proj, read_proj, signal, gate_branch)
    return pl.pallas_call(
        state_kernel,
        name="own_state",
        out_shape=[
            jax.ShapeDtypeStruct((heads, tokens), F32),
            jax.ShapeDtypeStruct((heads, tokens), F32),
            jax.ShapeDtypeStruct((16, LANES), BF16),
            jax.ShapeDtypeStruct((HALF, width), F32),
            jax.ShapeDtypeStruct((HALF, width + LANES), BF16),
        ]
        + [jax.ShapeDtypeStruct(a.shape, a.dtype) for a in passed],
        in_specs=[pl.BlockSpec(memory_space=pltpu.SMEM)] + [IN_HBM] * 9,
        out_specs=[IN_VMEM] * 9,
        scratch_shapes=[pltpu.VMEM(a.shape, a.dtype) for a in small]
        + [
            pltpu.VMEM((LANES, tokens), F32),
            pltpu.SemaphoreType.DMA((8,)),
            pltpu.SemaphoreType.DMA((width // column_block(width),)),
        ],
        compiler_params=pltpu.CompilerParams(vmem_limit_bytes=16 * MIB),
        cost_estimate=pl.CostEstimate(
            flops=4 * tokens * width * STATE, bytes_accessed=tokens * width * 2, transcendentals=0
        ),
    )(stretch_band, *in_hbm(*small, *passed))


def prepare_local(
    running_ref, write_ref, read_ref, decay_ref, got_ref, scores_ref, running_pieces_ref, decay_pieces_ref, lanes_ref, rows_ref
):
    width = lanes_ref.shape[1]
    scores = lax.dot_general(
        read_ref[...], write_ref[...], (((1,), (1,)), ((), ())), preferred_element_type=F32
    )
    row = lax.broadcasted_iota(jnp.int32, scores.shape, 0)
    lane = lax.broadcasted_iota(jnp.int32, scores.shape, 1)
    scores_ref[...] = jnp.where(row >= lane, scores, 0.0)
    running = running_ref[...]
    running_pieces_ref[...] = piece_rows(running, rows_ref).T.astype(BF16)
    decay_pieces_ref[...] = piece_rows(jnp.exp(running), rows_ref).T.astype(BF16)
    mine, got = decay_ref[...].astype(F32), got_ref[:16, width:].astype(F32)
    first_core = jnp.where(lax.axis_index("band") == 0, mine, got).astype(BF16)
    lanes_ref[...] = jnp.broadcast_to(
        decay_lanes(first_core, head_of_lane(LANES, width, 6)), lanes_ref.shape
    )


def local_heads(
    first_block,
    running_ref,
    weight_ref,
    signal_ref,
    gate_ref,
    scores_ref,
    running_pieces_ref,
    decay_pieces_ref,
    skip_ref,
    base_ref,
    factor_ref,
):
    heads, tokens = running_ref.shape
    block = column_block(signal_ref.shape[1])
    half = tokens // 2
    low_lanes = lax.broadcasted_iota(jnp.int32, (half, LANES), 1) < HEAD_DIM
    early, late = slice(0, half), slice(half, tokens)

    def heads_block(at, _):
        first_head = (first_block + at) * (block // HEAD_DIM)

        def whole_lanes(lane, count):
            return pl.ds(pl.multiple_of((first_block + at) * block + lane, LANES), count)

        def part_lanes(lane, count):
            return pl.ds(pl.multiple_of(at * block + lane, LANES), count)

        wide = dot(running_pieces_ref[...], piece_map(heads, block * 2, 7, first_head))
        gate = gate_ref[:, whole_lanes(0, block)].astype(F32)
        gate = gate / (1.0 + jnp.exp(-gate))
        factor_ref[:, part_lanes(0, block)] = (
            dot(decay_pieces_ref[...], piece_map(heads, block, 6, first_head)) * gate
        )
        skip = spread_heads(skip_ref[...], head_of_lane(heads, block, 6, first_head))
        for pair in range(block // LANES):
            lanes = slice(pair * LANES, (pair + 1) * LANES)
            values = signal_ref[:, whole_lanes(pair * LANES, LANES)]
            top, bottom = [], []
            for k in (2 * pair, 2 * pair + 1):
                row = running_ref[pl.ds(first_head + k, 1), :]
                weight = weight_ref[pl.ds(first_head + k, 1), :]
                column = wide[:, k * LANES : (k + 1) * LANES]

                def mixing(rows, cols):
                    span = jnp.minimum(column[rows] - row[:, cols], 0.0)
                    return (jnp.exp(span) * scores_ref[rows, cols] * weight[:, cols]).astype(BF16)

                top.append(mixing(early, early))
                bottom.append(jnp.concatenate([mixing(late, early), mixing(late, late)], axis=1))
            top = dot(jnp.concatenate(top, axis=0), values[early])
            bottom = dot(jnp.concatenate(bottom, axis=0), values)
            skipped = values.astype(F32) * skip[:, lanes]
            out_lanes = part_lanes(pair * LANES, LANES)
            base_ref[early, out_lanes] = (
                jnp.where(low_lanes, top[:half], top[half:]) + skipped[early]
            ) * gate[early, lanes]
            base_ref[late, out_lanes] = (
                jnp.where(low_lanes, bottom[:half], bottom[half:]) + skipped[late]
            ) * gate[late, lanes]
        return 0

    lax.fori_loop(0, base_ref.shape[1] // block, heads_block, 0)


def local_first_kernel(
    running_ref,
    weight_ref,
    signal_ref,
    gate_ref,
    write_ref,
    read_ref,
    decay_ref,
    got_ref,
    state_ref,
    skip_hbm,
    gain_hbm,
    matrix_hbm,
    after_ref,
    base_ref,
    factor_ref,
    matrix_ref,
    second_ref,
    gain_ref,
    scores_ref,
    running_pieces_ref,
    decay_pieces_ref,
    skip_ref,
    lanes_ref,
    rows_ref,
    sems,
):
    rows = matrix_ref.shape[0]
    pairs = (
        (skip_hbm, skip_ref),
        (gain_hbm, gain_ref),
        (matrix_hbm.at[pl.ds(0, rows), :], matrix_ref),
    )
    copies = [pltpu.make_async_copy(*pair, sems.at[i]) for i, pair in enumerate(pairs)]
    for copy in copies:
        copy.start()
    upper = lax.axis_index("scan") == 2
    second_ref[...] = state_ref[pl.ds(pl.multiple_of(jnp.where(upper, 0, PART), PART), PART), :]
    prepared = (scores_ref, running_pieces_ref, decay_pieces_ref)
    prepare_local(running_ref, write_ref, read_ref, decay_ref, got_ref, *prepared, lanes_ref, rows_ref)
    copies[0].wait()
    local_heads(
        0, running_ref, weight_ref, signal_ref, gate_ref, *prepared, skip_ref, base_ref, factor_ref
    )
    for copy in copies[1:]:
        copy.wait()


def local_rest_kernel(
    first_block,
    first_row,
    running_ref,
    weight_ref,
    signal_ref,
    gate_ref,
    scores_ref,
    running_pieces_ref,
    decay_pieces_ref,
    skip_ref,
    matrix_hbm,
    after_ref,
    base_ref,
    factor_ref,
    matrix_ref,
    sem,
):
    rows = matrix_ref.shape[0]
    copy = pltpu.make_async_copy(matrix_hbm.at[pl.ds(first_row, rows), :], matrix_ref, sem)
    copy.start()
    local_heads(
        first_block,
        running_ref,
        weight_ref,
        signal_ref,
        gate_ref,
        scores_ref,
        running_pieces_ref,
        decay_pieces_ref,
        skip_ref,
        base_ref,
        factor_ref,
    )
    copy.wait()


def local_shares(width):
    if width % (10 * LANES):
        return (width // column_block(width), 0, 0), (width, 0, 0)
    tenth = width // 10
    return (1, 2, 2), (tenth, 3 * tenth, 6 * tenth)


def local_call_of(kernel, name, part, outs, resident, passed, after, scratch):
    tokens, width = resident[2].shape
    matrix = passed[-1]
    blocks, rows = local_shares(width)
    columns = blocks[part] * column_block(width)
    return pl.pallas_call(
        kernel,
        name=name,
        out_shape=[jax.ShapeDtypeStruct((tokens, columns), F32)] * 2
        + [jax.ShapeDtypeStruct((rows[part], matrix.shape[1]), BF16)]
        + outs,
        in_specs=[IN_VMEM] * len(resident) + [IN_HBM] * len(passed) + [ANYWHERE],
        out_specs=[IN_VMEM] * (3 + len(outs)),
        scratch_shapes=scratch,
        compiler_params=pltpu.CompilerParams(vmem_limit_bytes=16 * MIB),
        cost_estimate=pl.CostEstimate(
            flops=6 * columns * tokens * tokens,
            bytes_accessed=tokens * columns * 12,
            transcendentals=columns // HEAD_DIM * tokens * tokens,
        ),
    )(*resident, *in_hbm(*passed), after)


def local_first(values, state, constants, after):
    running, signal = values[0], values[2]
    skip_gain, norm_gain, _ = constants
    tokens, width = signal.shape
    pieces_shape = jax.ShapeDtypeStruct((tokens, LANES), BF16)
    return local_call_of(
        local_first_kernel,
        "local_first",
        0,
        [
            jax.ShapeDtypeStruct((PART, state.shape[1]), BF16),
            jax.ShapeDtypeStruct(norm_gain.shape, F32),
            jax.ShapeDtypeStruct((tokens, tokens), F32),
            pieces_shape,
            pieces_shape,
            jax.ShapeDtypeStruct(skip_gain.shape, F32),
            jax.ShapeDtypeStruct((8, width), F32),
        ],
        (*values, state),
        constants,
        after,
        [pltpu.VMEM((LANES, tokens), F32), pltpu.SemaphoreType.DMA((3,))],
    )


def local_rest(part, values, prepared, out_weight, after):
    blocks, rows = local_shares(values[2].shape[1])
    return local_call_of(
        functools.partial(local_rest_kernel, sum(blocks[:part]), sum(rows[:part])),
        "local_rest",
        part,
        [],
        (*values, *prepared),
        (out_weight,),
        after,
        [pltpu.SemaphoreType.DMA(())],
    )


def chip_kernel(keep_ref, got_ref, decay_ref, state_ref, first_ref):
    width = keep_ref.shape[1]
    core = lax.axis_index("band")
    chip = lax.axis_index("scan")
    heads_map = head_of_lane(LANES, width, 6)
    got_decay = got_ref[:16, width:]
    mine = decay_ref[...]
    later = jnp.where(core == 0, got_decay.astype(F32), mine.astype(F32)).astype(BF16)
    lanes = decay_lanes(later, heads_map)
    got = got_ref[:, :width].astype(F32)
    keep = keep_ref[...]
    early, late = jnp.where(core == 0, keep, got), jnp.where(core == 0, got, keep)
    state_ref[:, :width] = (early * lanes + late).astype(BF16)
    block = decay_block(decay_row(got_decay) * decay_row(mine), PART)
    state_ref[:PART, width:] = block
    state_ref[PART:, width:] = block

    lower = jnp.where(chip == 1, PART, 0)
    first_ref[...] = state_ref[pl.ds(pl.multiple_of(lower, PART), PART), :]


def early_kernel(state_ref, near_ref, out_ref):
    width = out_ref.shape[1]
    chip = lax.axis_index("scan")

    @pl.when(chip == 0)
    def _():
        out_ref[...] = state_ref[PART:, :width]

    @pl.when(chip == 1)
    def _():
        lanes = decay_lanes(state_ref[:16, width:], head_of_lane(LANES, width, 6))
        out_ref[...] = (
            lanes * near_ref[:, :width].astype(F32) + state_ref[:PART, :width].astype(F32)
        ).astype(BF16)


def middle_kernel(state_ref, near_ref, far_ref, out_ref, lanes_ref):
    width = out_ref.shape[1]
    chip = lax.axis_index("scan")

    @pl.when(chip == 2)
    def _():
        heads_map = head_of_lane(LANES, width, 6)
        lanes = decay_lanes(near_ref[:16, width:], heads_map)
        lanes_ref[...] = jnp.broadcast_to(lanes, lanes_ref.shape)
        entered = lanes * far_ref[:, :width].astype(F32) + near_ref[:, :width].astype(F32)
        own = decay_lanes(state_ref[:16, width:], heads_map)
        out_ref[...] = (own * entered + state_ref[PART:, :width].astype(F32)).astype(BF16)

    @pl.when(chip == 3)
    def _():
        lanes = decay_lanes(far_ref[:16, width:], head_of_lane(LANES, width, 6))
        lanes_ref[...] = jnp.broadcast_to(lanes, lanes_ref.shape)


def enter_kernel(
    near_ref,
    far_ref,
    early_ref,
    next_ref,
    far_lanes_ref,
    keep_ref,
    got_ref,
    lanes_ref,
    mine_ref,
    send_ref,
):
    width = keep_ref.shape[1]
    chip = lax.axis_index("scan")
    near, far = (ref.at[:, pl.ds(0, width)] for ref in (near_ref, far_ref))
    refs = (keep_ref, got_ref, lanes_ref, mine_ref, send_ref)

    @pl.when(chip == 0)
    def _():
        share_enter(jnp.zeros((HALF, width), F32), 0, *refs)

    @pl.when(chip == 1)
    def _():
        share_enter(near[...].astype(F32), 0, *refs)
        share_enter(early_ref[...].astype(F32), PART, *refs)

    @pl.when(chip == 2)
    def _():
        share_enter(next_ref[...].astype(F32), 0, *refs)
        share_enter(far_lanes_ref[:1] * far[...].astype(F32) + near[...].astype(F32), PART, *refs)

    @pl.when(chip == 3)
    def _():
        share_enter(far_lanes_ref[:1] * early_ref[...].astype(F32) + far[...].astype(F32), 0, *refs)


def enter_last_kernel(last_ref, keep_ref, got_ref, lanes_ref, old_mine, old_send, mine_ref, send_ref):
    @pl.when(lax.axis_index("scan") == 3)
    def _():
        share_enter(
            last_ref[...].astype(F32), PART, keep_ref, got_ref, lanes_ref, mine_ref, send_ref
        )


def share_enter(enter, first, keep_ref, got_ref, lanes_ref, mine_ref, send_ref):
    width = keep_ref.shape[1]
    core = lax.axis_index("band")
    rows = slice(first, first + enter.shape[0])

    @pl.when(core == 0)
    def _():
        mine_ref[rows, :] = enter.astype(BF16)
        send_ref[rows, :] = (lanes_ref[:1] * enter + keep_ref[rows, :]).astype(BF16)

    @pl.when(core == 1)
    def _():
        send_ref[rows, :] = enter.astype(BF16)
        mine_ref[rows, :] = (lanes_ref[:1] * enter + got_ref[rows, :width].astype(F32)).astype(BF16)


def gathered_kernel(all_ref, keep_ref, got_ref, lanes_ref, mine_ref, send_ref, enter_ref):
    width = keep_ref.shape[1]
    chip = lax.axis_index("scan")
    heads_map = head_of_lane(LANES, width, 6)
    enter_ref[...] = jnp.zeros(enter_ref.shape, F32)
    for source in range(all_ref.shape[0]):

        @pl.when(source < chip)
        def _():
            lanes = decay_lanes(all_ref[source, :16, width:], heads_map)
            enter_ref[...] = lanes * enter_ref[...] + all_ref[source, :, :width].astype(F32)

    share_enter(enter_ref[...], 0, keep_ref, got_ref, lanes_ref, mine_ref, send_ref)


def chip_state(keep, got, decay):
    width = keep.shape[1]
    return local_call(
        chip_kernel,
        "chip_state",
        [
            jax.ShapeDtypeStruct((HALF, width + LANES), BF16),
            jax.ShapeDtypeStruct((PART, width + LANES), BF16),
        ],
        (keep, got, decay),
    )


def entering_state(chips, state, first, keep, got, local):
    width = keep.shape[1]
    half = jax.ShapeDtypeStruct((HALF, width), BF16)
    if chips != 4:
        gathered = lax.all_gather(state, "scan", axis=0)
        second, lanes = local(0, first)
        local(1, second)
        local(2, second)
        return local_call(
            gathered_kernel,
            "enter_state",
            [half, half],
            (gathered, keep, got, lanes),
            (pltpu.VMEM((HALF, width), F32),),
        )
    near = lax.ppermute(first, "scan", [(0, 1), (1, 2)])
    second, lanes = local(0, first)
    far = lax.ppermute(second, "scan", [(0, 2), (2, 3)])
    done = local(1, second)
    (ahead,) = local_call(
        early_kernel,
        "early_state",
        [jax.ShapeDtypeStruct((PART, width), BF16)],
        (state, near),
        after=(done,),
    )
    early = lax.ppermute(ahead, "scan", [(1, 3), (0, 1)])
    following = lax.ppermute(ahead, "scan", [(1, 2)])
    middle, far_lanes = local_call(
        middle_kernel,
        "middle_state",
        [jax.ShapeDtypeStruct((PART, width), BF16), jax.ShapeDtypeStruct((8, width), F32)],
        (state, near, far),
        after=(ahead,),
    )
    last = lax.ppermute(middle, "scan", [(2, 3)])
    done = local(2, middle)
    mine, give = local_call(
        enter_kernel,
        "enter_state",
        [half, half],
        (near, far, early, following, far_lanes, keep, got, lanes),
        after=(done,),
    )
    return local_call(
        enter_last_kernel,
        "enter_last",
        [half, half],
        (last, keep, got, lanes, mine, give),
        aliases={4: 0, 5: 1},
    )


def gated_kernel(parts, mine_ref, other_ref, read_ref, gain_ref, *refs):
    bases, factors, weights = refs[:parts], refs[parts : 2 * parts], refs[2 * parts : 3 * parts]
    out_ref, square_ref, *first_refs = refs[3 * parts :]
    tokens, width = out_ref.shape
    block = column_block(width)
    is_first = lax.axis_index("band") == 0
    read = read_ref[...]
    sums = jnp.zeros((tokens, LANES), F32)
    first = 0
    for base_ref, factor_ref in zip(bases, factors):
        for start in range(0, base_ref.shape[1], block):
            lanes = slice(first, first + block)
            mine, other = mine_ref[:, lanes].astype(F32), other_ref[:, lanes].astype(F32)
            low = jnp.where(is_first, mine, other).astype(BF16)
            high = jnp.where(is_first, other, mine).astype(BF16)
            carried = dot(read, jnp.concatenate([low, high], axis=0))
            lanes = slice(start, start + block)
            gated = base_ref[:, lanes] + factor_ref[:, lanes] * carried
            for k in range(0, block, LANES):
                column = gated[:, k : k + LANES]
                row = (first + k) // LANES
                out_ref[:, first + k : first + k + LANES] = (
                    column * gain_ref[row : row + 1, :]
                ).astype(BF16)
                sums += column * column
            first += block
    for first_ref in first_refs:
        send_kernel(0, out_ref, *weights, first_ref)
    square_ref[...] = jnp.broadcast_to(jnp.sum(sums.T, axis=0, keepdims=True), square_ref.shape)


def gated_part(mine, other, read_proj, gain, bases, factors, weights, first):
    tokens = read_proj.shape[0]
    width = mine.shape[1]
    return local_call(
        functools.partial(gated_kernel, len(bases)),
        "gated_part",
        [
            jax.ShapeDtypeStruct((tokens, width), BF16),
            jax.ShapeDtypeStruct((8, tokens), F32),
        ]
        + [jax.ShapeDtypeStruct((tokens, first), BF16)] * (first > 0),
        (mine, other, read_proj, gain, *bases, *factors, *weights),
        flops=2 * tokens * width * STATE,
    )


SENDS = (512, 384, 384)


def project(gated_ref, weights, other, first, count):
    columns = weights[0].shape[1] // 2
    member = lax.axis_index("tensor")
    start = (1 - member if other else member) * columns + first
    lanes = pl.ds(pl.multiple_of(start, LANES), count)
    row, total = 0, None
    for weight_ref in weights:
        rows = weight_ref.shape[0]
        term = dot(gated_ref[:, row : row + rows], weight_ref[:, lanes])
        row, total = row + rows, term if total is None else total + term
    return total


def send_kernel(first, gated_ref, *refs, squares=False):
    *refs, out_ref = refs
    weights = refs[:-1] if squares else refs
    tokens, count = gated_ref.shape[0], out_ref.shape[1]
    out_ref[:tokens, :] = project(gated_ref, weights, True, first, count).astype(BF16)
    if squares:
        out_ref[tokens:, :] = jnp.zeros((16, count), BF16)
        for lane in range(0, tokens, LANES):
            lanes = slice(lane, lane + LANES)
            out_ref[tokens:, lanes] = decay_block(refs[-1][:1, lanes], 16)


def own_kernel(gated_ref, *refs):
    *weights, out_ref = refs
    count = out_ref.shape[1] // 5
    for first in range(0, out_ref.shape[1], count):
        out_ref[:, first : first + count] = project(gated_ref, weights, False, first, count)


def finish_kernel(squares_ref, own_ref, *refs):
    *got_refs, out_ref, sent_ref, sems = refs
    tokens = own_ref.shape[0]
    other_squares = got_refs[-1][tokens:, :tokens].astype(F32)
    mean = (squares_ref[:1] + jnp.sum(other_squares, axis=0, keepdims=True)) / INNER
    scale = lax.rsqrt(mean + EPSILON)
    scale = jnp.broadcast_to(scale, (LANES, tokens)).T
    first, copies = 0, []
    for got_ref in got_refs:
        count = got_ref.shape[1]
        for lane in range(0, count, LANES):
            lanes = slice(first + lane, first + lane + LANES)
            total = own_ref[:, lanes] + got_ref[:tokens, lane : lane + LANES].astype(F32)
            sent_ref[:, lanes] = (total * scale).astype(BF16)
        lanes = pl.ds(first, count)
        copies.append(
            pltpu.make_async_copy(sent_ref.at[:, lanes], out_ref.at[:, lanes], sems.at[len(copies)])
        )
        copies[-1].start()
        first += count
    for copy in copies:
        copy.wait()


def finish(squares, own, got):
    args = (squares, own, *got)
    return pl.pallas_call(
        finish_kernel,
        name="finish",
        out_shape=jax.ShapeDtypeStruct(own.shape, BF16),
        in_specs=[IN_VMEM] * len(args),
        out_specs=IN_HBM,
        scratch_shapes=[
            pltpu.VMEM(own.shape, BF16),
            pltpu.SemaphoreType.DMA((len(got),)),
        ],
        compiler_params=pltpu.CompilerParams(vmem_limit_bytes=8 * MIB),
    )(*args)


def direct(members, columns):
    return members == 2 and columns == sum(SENDS)


def layer_columns(members, gated, squares, weights, ready):
    columns = weights[0].shape[1] // members
    if not direct(members, columns):
        mean = lax.psum(squares[0], "tensor") / INNER
        partial = dot(gated, jnp.concatenate(weights, axis=0)).astype(BF16)
        total = lax.psum_scatter(partial, "tensor", scatter_dimension=1, tiled=True)
        return (total.astype(F32) * lax.rsqrt(mean + EPSILON)[:, None]).astype(BF16)
    swap = [(0, 1), (1, 0)]
    tokens = gated.shape[0]
    parts, first = [ready[0]], SENDS[0]
    for count in SENDS[1:]:
        last = first + count == columns
        parts += local_call(
            functools.partial(send_kernel, first, squares=last),
            "project_other",
            [jax.ShapeDtypeStruct((tokens + 16 * last, count), BF16)],
            (gated, *weights) + (squares,) * last,
            after=parts[-1:],
        )
        first += count
    got = [lax.ppermute(part, "tensor", swap) for part in parts]
    (own,) = local_call(
        own_kernel,
        "project_own",
        [jax.ShapeDtypeStruct((tokens, columns), F32)],
        (gated, *weights),
        after=parts[-1:],
    )
    return finish(squares, own, got)


def on_device(
    chips,
    members,
    signal,
    gate_branch,
    write_proj,
    read_proj,
    step_logits,
    valid_mask,
    stretch_band,
    band_offset,
    decay_log,
    step_offset,
    skip_gain,
    norm_gain,
    out_weight,
):
    small = (step_logits, valid_mask[None], band_offset, decay_log[None], step_offset[None])
    running, weight, decay, keep, send, *passed = own_state(
        stretch_band, small, write_proj, read_proj, signal, gate_branch
    )
    cores = [(0, 1), (1, 0)]
    got = lax.ppermute(send, "band", cores)
    state, first = chip_state(keep, got, decay)
    constants = (skip_gain[None], norm_gain.reshape(-1, LANES), out_weight)
    write, read, *streams = passed
    values = (running, weight, *streams)
    bases, factors, weights, prepared, gains = [], [], [], [], []

    def local(part, after):
        if not local_shares(signal.shape[1])[0][part]:
            return after
        if part:
            base, factor, matrix = local_rest(part, values, prepared, out_weight, after)
        else:
            base, factor, matrix, second, gain, *rest, lanes = local_first(
                (*values, write, read, decay, got), state, constants, after
            )
            prepared.extend(rest)
            gains.append(gain)
        bases.append(base)
        factors.append(factor)
        weights.append(matrix)
        return base if part else (second, lanes)

    mine, give = entering_state(chips, state, first, keep, got, local)
    other = lax.ppermute(give, "band", cores)
    ahead = SENDS[0] if direct(members, out_weight.shape[1] // members) else 0
    gated, squares, *ready = gated_part(
        mine, other, read, gains[0], bases, factors, weights, ahead
    )
    return layer_columns(members, gated, squares, weights, ready)


def solution(mesh):
    placed = (
        P(("group", "scan", "band"), "tensor"),
        P(("group", "scan", "band"), "tensor"),
        P(("group", "scan", "band"), None),
        P(("group", "scan", "band"), None),
        P("tensor", ("group", "scan", "band")),
        P(("group", "scan", "band")),
        P(("group", "scan", "band")),
        P(None, "tensor"),
        P("tensor"),
        P("tensor"),
        P("tensor"),
        P("tensor"),
        P("tensor", None),
    )
    return jax.shard_map(
        functools.partial(on_device, mesh.shape["scan"], mesh.shape["tensor"]),
        mesh=mesh,
        in_specs=placed,
        out_specs=P(("group", "scan", "band"), "tensor"),
        check_vma=False,
    )
```

```python
import functools

import jax
import jax.numpy as jnp
from jax import lax
from jax.experimental import pallas as pl
from jax.experimental.pallas import tpu as pltpu
from jax.sharding import PartitionSpec as P

HEAD_DIM = 64
STATE = 128
HALF = STATE // 2
PART = HALF // 2
STRETCH = 256
BANDS = 12
INNER = 5120
LANES = 128

EPSILON = 1e-05
HIGHEST = lax.Precision.HIGHEST
F32 = jnp.float32
BF16 = jnp.bfloat16
MIB = 1 << 20


def dot(a, b):
    return lax.dot_general(a, b, (((1,), (0,)), ((), ())), preferred_element_type=F32)


def pieces(x):
    high = x.astype(BF16)
    rest = x - high.astype(F32)
    middle = rest.astype(BF16)
    return high, middle, (rest - middle.astype(F32)).astype(BF16)


def head_of_lane(heads, lanes, group, first=0):
    row = lax.broadcasted_iota(jnp.int32, (heads, lanes), 0)
    lane = lax.broadcasted_iota(jnp.int32, (heads, lanes), 1)
    return (row == first + lax.shift_right_logical(lane, group)).astype(F32).astype(BF16)


def slot_of(heads):
    return -(-heads // 8) * 8


def piece_rows(values, ref):
    heads = values.shape[0]
    ref[...] = jnp.zeros(ref.shape, F32)
    for k, piece in enumerate(pieces(values)):
        first = k * slot_of(heads)
        ref[first : first + heads, :] = piece.astype(F32)
    return ref[...]


def piece_away(heads, lanes, group):
    slot = slot_of(heads)
    row = lax.broadcasted_iota(jnp.int32, (LANES, lanes), 0)
    head = row - jnp.where(row >= 2 * slot, 2 * slot, jnp.where(row >= slot, slot, 0))
    head = jnp.where(row < 3 * slot, head, -LANES)
    return head - lax.shift_right_logical(lax.broadcasted_iota(jnp.int32, (LANES, lanes), 1), group)


def piece_map(away, first):
    return jnp.where(away == first, 1.0, 0.0).astype(BF16)


def spread_heads(row, heads_map):
    return sum(dot(piece, heads_map) for piece in pieces(jnp.broadcast_to(row, (8, row.shape[1]))))[:1]


def diagonal(rows, lanes):
    return lax.broadcasted_iota(jnp.int32, (rows, lanes), 0) == lax.broadcasted_iota(
        jnp.int32, (rows, lanes), 1
    )


def to_column(row):
    count = row.shape[1]
    return jnp.sum(jnp.where(diagonal(count, count), row, 0.0), axis=1, keepdims=True)


def decay_block(row, rows):
    place = lax.broadcasted_iota(jnp.int32, (rows, LANES), 0)
    high, middle, low = (piece.astype(F32) for piece in pieces(row))
    block = jnp.where(place == 0, high, jnp.where(place == 1, middle, jnp.where(place == 2, low, 0.0)))
    return block.astype(BF16)


def decay_row(block):
    return jnp.sum(block.astype(F32), axis=0, keepdims=True)


def decay_map(heads, width):
    return head_of_lane(-(-heads // 16) * 16, width, 6)


def decay_lanes(block, heads_map):
    return jnp.sum(dot(block[:16, : heads_map.shape[0]], heads_map), axis=0, keepdims=True)


def column_block(width):
    return width // 5 if width % (5 * LANES) == 0 else width


def local_call(body, name, outs, args, scratch=(), limit=8 * MIB, flops=0, after=(), aliases=None):
    size = sum(a.size * a.dtype.itemsize for a in args) + sum(o.size * o.dtype.itemsize for o in outs)

    def kernel(*refs):
        body(*refs[: len(args)], *refs[len(args) + len(after) :])

    return pl.pallas_call(
        kernel,
        name=name,
        out_shape=outs,
        in_specs=[pl.BlockSpec(memory_space=pltpu.VMEM)] * len(args)
        + [pl.BlockSpec(memory_space=pl.ANY)] * len(after),
        out_specs=[pl.BlockSpec(memory_space=pltpu.VMEM)] * len(outs),
        scratch_shapes=list(scratch),
        input_output_aliases=aliases or {},
        compiler_params=pltpu.CompilerParams(vmem_limit_bytes=limit),
        cost_estimate=pl.CostEstimate(flops=flops, bytes_accessed=size, transcendentals=0),
    )(*args, *after)


IN_VMEM = pl.BlockSpec(memory_space=pltpu.VMEM)
IN_HBM = pl.BlockSpec(memory_space=pltpu.HBM)
ANYWHERE = pl.BlockSpec(memory_space=pl.ANY)


def in_hbm(*arrays):
    return [pltpu.with_memory_space_constraint(a, pltpu.HBM) for a in arrays]


def state_kernel(
    band_ref,
    logits_hbm,
    mask_hbm,
    offset_hbm,
    decay_log_hbm,
    step_offset_hbm,
    write_hbm,
    read_hbm,
    signal_hbm,
    gate_hbm,
    running_ref,
    weight_ref,
    decay_ref,
    keep_ref,
    send_ref,
    write_ref,
    read_ref,
    signal_ref,
    gate_ref,
    logits_ref,
    mask_ref,
    offset_ref,
    decay_log_ref,
    step_offset_ref,
    rows_ref,
    factors_ref,
    sems,
    block_sems,
):
    heads, tokens = logits_ref.shape
    width = signal_ref.shape[1]
    block = column_block(width)
    is_first = lax.axis_index("band") == 0
    pairs = (
        (logits_hbm, logits_ref),
        (mask_hbm, mask_ref),
        (offset_hbm, offset_ref),
        (decay_log_hbm, decay_log_ref),
        (step_offset_hbm, step_offset_ref),
        (write_hbm, write_ref),
        (read_hbm, read_ref),
        (gate_hbm, gate_ref),
    )
    copies = [pltpu.make_async_copy(*pair, sems.at[i]) for i, pair in enumerate(pairs)]
    blocks = [
        pltpu.make_async_copy(
            signal_hbm.at[:, pl.ds(first, block)],
            signal_ref.at[:, pl.ds(first, block)],
            block_sems.at[first // block],
        )
        for first in range(0, width, block)
    ]
    for copy in copies[:6] + blocks + copies[6:]:
        copy.start()
    for copy in copies[:6]:
        copy.wait()

    offset = to_column(step_offset_ref[...] + offset_ref[pl.ds(band_ref[0], 1), :])
    raw = logits_ref[...] + offset
    step_size = jnp.maximum(raw, 0.0) + jnp.log1p(jnp.exp(-jnp.abs(raw)))
    log_decay = step_size * to_column(-jnp.exp(decay_log_ref[...]))
    earlier = lax.broadcasted_iota(jnp.int32, (tokens, tokens), 0)
    later = lax.broadcasted_iota(jnp.int32, (tokens, tokens), 1)
    sums = dot(
        piece_rows(log_decay, rows_ref).astype(BF16), jnp.where(earlier <= later, 1.0, 0.0).astype(BF16)
    )
    slot = slot_of(heads)
    running = sums[:heads] + sums[slot : slot + heads] + sums[2 * slot : 2 * slot + heads]
    weight = step_size * mask_ref[...].astype(F32)
    running_ref[...] = running
    weight_ref[...] = weight
    total = running[:, tokens - 1 : tokens]
    row = jnp.sum(jnp.where(diagonal(heads, LANES), jnp.exp(total), 0.0), axis=0, keepdims=True)
    send_ref[:, width:] = decay_block(row, HALF)
    decay_ref[...] = decay_block(row, 16)

    tail = piece_rows(jnp.exp(total - running) * weight, rows_ref).T.astype(BF16)
    write = write_ref[...].astype(F32).T
    low, high = write[:HALF], write[HALF:]
    write = jnp.concatenate(
        [jnp.where(is_first, low, high), jnp.where(is_first, high, low)], axis=0
    ).astype(BF16)
    away = piece_away(heads, block, 6)
    for first in range(0, width, block):
        factors_ref[:, first : first + block] = dot(tail, piece_map(away, first // HEAD_DIM))
    for copy in blocks:
        copy.wait()
    for first in range(0, width, block):
        lanes = slice(first, first + block)
        scaled = (signal_ref[:, lanes].astype(F32) * factors_ref[:, lanes]).astype(BF16)
        state = dot(write, scaled)
        keep_ref[:, lanes] = state[:HALF]
        send_ref[:, lanes] = state[HALF:].astype(BF16)
    for copy in copies[6:]:
        copy.wait()


def own_state(stretch_band, small, write_proj, read_proj, signal, gate_branch):
    tokens, width = signal.shape
    heads = small[0].shape[0]
    passed = (write_proj, read_proj, signal, gate_branch)
    return pl.pallas_call(
        state_kernel,
        name="own_state",
        out_shape=[
            jax.ShapeDtypeStruct((heads, tokens), F32),
            jax.ShapeDtypeStruct((heads, tokens), F32),
            jax.ShapeDtypeStruct((16, LANES), BF16),
            jax.ShapeDtypeStruct((HALF, width), F32),
            jax.ShapeDtypeStruct((HALF, width + LANES), BF16),
        ]
        + [jax.ShapeDtypeStruct(a.shape, a.dtype) for a in passed],
        in_specs=[pl.BlockSpec(memory_space=pltpu.SMEM)] + [IN_HBM] * 9,
        out_specs=[IN_VMEM] * 9,
        scratch_shapes=[pltpu.VMEM(a.shape, a.dtype) for a in small]
        + [
            pltpu.VMEM((LANES, tokens), F32),
            pltpu.VMEM((tokens, width), F32),
            pltpu.SemaphoreType.DMA((8,)),
            pltpu.SemaphoreType.DMA((width // column_block(width),)),
        ],
        compiler_params=pltpu.CompilerParams(vmem_limit_bytes=16 * MIB),
        cost_estimate=pl.CostEstimate(
            flops=4 * tokens * width * STATE, bytes_accessed=tokens * width * 2, transcendentals=0
        ),
    )(stretch_band, *in_hbm(*small, *passed))


def prepare_local(
    running_ref, write_ref, read_ref, decay_ref, got_ref, scores_ref, running_pieces_ref, decay_pieces_ref, lanes_ref, rows_ref
):
    width = lanes_ref.shape[1]
    scores = lax.dot_general(
        read_ref[...], write_ref[...], (((1,), (1,)), ((), ())), preferred_element_type=F32
    )
    row = lax.broadcasted_iota(jnp.int32, scores.shape, 0)
    lane = lax.broadcasted_iota(jnp.int32, scores.shape, 1)
    scores_ref[...] = jnp.where(row >= lane, scores, 0.0)
    running = running_ref[...]
    running_pieces_ref[...] = piece_rows(running, rows_ref).T.astype(BF16)
    decay_pieces_ref[...] = piece_rows(jnp.exp(running), rows_ref).T.astype(BF16)
    mine, got = decay_ref[...].astype(F32), got_ref[:16, width:].astype(F32)
    first_core = jnp.where(lax.axis_index("band") == 0, mine, got).astype(BF16)
    lanes_ref[...] = jnp.broadcast_to(
        decay_lanes(first_core, decay_map(width // HEAD_DIM, width)), lanes_ref.shape
    )


def local_heads(
    first_block,
    running_ref,
    weight_ref,
    signal_ref,
    gate_ref,
    scores_ref,
    running_pieces_ref,
    decay_pieces_ref,
    skip_ref,
    base_ref,
    factor_ref,
):
    heads, tokens = running_ref.shape
    block = column_block(signal_ref.shape[1])
    half = tokens // 2
    low_lanes = lax.broadcasted_iota(jnp.int32, (half, LANES), 1) < HEAD_DIM
    early, late = slice(0, half), slice(half, tokens)

    wide_away, away = piece_away(heads, 2 * block, 7), piece_away(heads, block, 6)

    def heads_block(at, _):
        first_head = (first_block + at) * (block // HEAD_DIM)

        def whole_lanes(lane, count):
            return pl.ds(pl.multiple_of((first_block + at) * block + lane, LANES), count)

        def part_lanes(lane, count):
            return pl.ds(pl.multiple_of(at * block + lane, LANES), count)

        wide = dot(running_pieces_ref[...], piece_map(wide_away, first_head))
        gate = gate_ref[:, whole_lanes(0, block)].astype(F32)
        gate = gate / (1.0 + jnp.exp(-gate))
        factor_ref[:, part_lanes(0, block)] = (
            dot(decay_pieces_ref[...], piece_map(away, first_head)) * gate
        )
        skip = spread_heads(skip_ref[...], head_of_lane(heads, block, 6, first_head))
        for pair in range(block // LANES):
            lanes = slice(pair * LANES, (pair + 1) * LANES)
            values = signal_ref[:, whole_lanes(pair * LANES, LANES)]
            top, bottom = [], []
            for k in (2 * pair, 2 * pair + 1):
                row = running_ref[pl.ds(first_head + k, 1), :]
                weight = weight_ref[pl.ds(first_head + k, 1), :]
                column = wide[:, k * LANES : (k + 1) * LANES]

                def mixing(rows, cols):
                    span = jnp.minimum(column[rows] - row[:, cols], 0.0)
                    return (jnp.exp(span) * scores_ref[rows, cols] * weight[:, cols]).astype(BF16)

                top.append(mixing(early, early))
                bottom.append(jnp.concatenate([mixing(late, early), mixing(late, late)], axis=1))
            top = dot(jnp.concatenate(top, axis=0), values[early])
            bottom = dot(jnp.concatenate(bottom, axis=0), values)
            skipped = values.astype(F32) * skip[:, lanes]
            out_lanes = part_lanes(pair * LANES, LANES)
            base_ref[early, out_lanes] = (
                jnp.where(low_lanes, top[:half], top[half:]) + skipped[early]
            ) * gate[early, lanes]
            base_ref[late, out_lanes] = (
                jnp.where(low_lanes, bottom[:half], bottom[half:]) + skipped[late]
            ) * gate[late, lanes]
        return 0

    lax.fori_loop(0, base_ref.shape[1] // block, heads_block, 0)


def local_first_kernel(
    running_ref,
    weight_ref,
    signal_ref,
    gate_ref,
    write_ref,
    read_ref,
    decay_ref,
    got_ref,
    state_ref,
    skip_hbm,
    gain_hbm,
    matrix_hbm,
    after_ref,
    base_ref,
    factor_ref,
    matrix_ref,
    second_ref,
    gain_ref,
    scores_ref,
    running_pieces_ref,
    decay_pieces_ref,
    skip_ref,
    lanes_ref,
    rows_ref,
    sems,
):
    rows = matrix_ref.shape[0]
    pairs = (
        (skip_hbm, skip_ref),
        (gain_hbm, gain_ref),
        (matrix_hbm.at[pl.ds(0, rows), :], matrix_ref),
    )
    copies = [pltpu.make_async_copy(*pair, sems.at[i]) for i, pair in enumerate(pairs)]
    for copy in copies:
        copy.start()
    upper = lax.axis_index("scan") == 2
    second_ref[...] = state_ref[pl.ds(pl.multiple_of(jnp.where(upper, 0, PART), PART), PART), :]
    prepared = (scores_ref, running_pieces_ref, decay_pieces_ref)
    prepare_local(running_ref, write_ref, read_ref, decay_ref, got_ref, *prepared, lanes_ref, rows_ref)
    copies[0].wait()
    local_heads(
        0, running_ref, weight_ref, signal_ref, gate_ref, *prepared, skip_ref, base_ref, factor_ref
    )
    for copy in copies[1:]:
        copy.wait()


def local_rest_kernel(
    first_block,
    first_row,
    running_ref,
    weight_ref,
    signal_ref,
    gate_ref,
    scores_ref,
    running_pieces_ref,
    decay_pieces_ref,
    skip_ref,
    matrix_hbm,
    after_ref,
    base_ref,
    factor_ref,
    matrix_ref,
    sem,
):
    rows = matrix_ref.shape[0]
    copy = pltpu.make_async_copy(matrix_hbm.at[pl.ds(first_row, rows), :], matrix_ref, sem)
    copy.start()
    local_heads(
        first_block,
        running_ref,
        weight_ref,
        signal_ref,
        gate_ref,
        scores_ref,
        running_pieces_ref,
        decay_pieces_ref,
        skip_ref,
        base_ref,
        factor_ref,
    )
    copy.wait()


def local_shares(width):
    if width % (10 * LANES):
        return (width // column_block(width), 0, 0), (width, 0, 0)
    tenth = width // 10
    return (1, 2, 2), (tenth, 3 * tenth, 6 * tenth)


def local_call_of(kernel, name, part, outs, resident, passed, after, scratch):
    tokens, width = resident[2].shape
    matrix = passed[-1]
    blocks, rows = local_shares(width)
    columns = blocks[part] * column_block(width)
    return pl.pallas_call(
        kernel,
        name=name,
        out_shape=[jax.ShapeDtypeStruct((tokens, columns), F32)] * 2
        + [jax.ShapeDtypeStruct((rows[part], matrix.shape[1]), BF16)]
        + outs,
        in_specs=[IN_VMEM] * len(resident) + [IN_HBM] * len(passed) + [ANYWHERE],
        out_specs=[IN_VMEM] * (3 + len(outs)),
        scratch_shapes=scratch,
        compiler_params=pltpu.CompilerParams(vmem_limit_bytes=16 * MIB),
        cost_estimate=pl.CostEstimate(
            flops=6 * columns * tokens * tokens,
            bytes_accessed=tokens * columns * 12,
            transcendentals=columns // HEAD_DIM * tokens * tokens,
        ),
    )(*resident, *in_hbm(*passed), after)


def local_first(values, state, constants, after):
    running, signal = values[0], values[2]
    skip_gain, norm_gain, _ = constants
    tokens, width = signal.shape
    pieces_shape = jax.ShapeDtypeStruct((tokens, LANES), BF16)
    return local_call_of(
        local_first_kernel,
        "local_first",
        0,
        [
            jax.ShapeDtypeStruct((PART, state.shape[1]), BF16),
            jax.ShapeDtypeStruct(norm_gain.shape, F32),
            jax.ShapeDtypeStruct((tokens, tokens), F32),
            pieces_shape,
            pieces_shape,
            jax.ShapeDtypeStruct(skip_gain.shape, F32),
            jax.ShapeDtypeStruct((8, width), F32),
        ],
        (*values, state),
        constants,
        after,
        [pltpu.VMEM((LANES, tokens), F32), pltpu.SemaphoreType.DMA((3,))],
    )


def local_rest(part, values, prepared, out_weight, after):
    blocks, rows = local_shares(values[2].shape[1])
    return local_call_of(
        functools.partial(local_rest_kernel, sum(blocks[:part]), sum(rows[:part])),
        "local_rest",
        part,
        [],
        (*values, *prepared),
        (out_weight,),
        after,
        [pltpu.SemaphoreType.DMA(())],
    )


def chip_kernel(keep_ref, got_ref, decay_ref, state_ref, first_ref):
    width = keep_ref.shape[1]
    core = lax.axis_index("band")
    chip = lax.axis_index("scan")
    heads_map = decay_map(width // HEAD_DIM, width)
    got_decay = got_ref[:16, width:]
    mine = decay_ref[...]
    later = jnp.where(core == 0, got_decay.astype(F32), mine.astype(F32)).astype(BF16)
    lanes = decay_lanes(later, heads_map)
    got = got_ref[:, :width].astype(F32)
    keep = keep_ref[...]
    early, late = jnp.where(core == 0, keep, got), jnp.where(core == 0, got, keep)
    state_ref[:, :width] = (early * lanes + late).astype(BF16)
    block = decay_block(decay_row(got_decay) * decay_row(mine), PART)
    state_ref[:PART, width:] = block
    state_ref[PART:, width:] = block

    lower = jnp.where(chip == 1, PART, 0)
    first_ref[...] = state_ref[pl.ds(pl.multiple_of(lower, PART), PART), :]


def early_kernel(state_ref, near_ref, out_ref):
    width = out_ref.shape[1]
    chip = lax.axis_index("scan")

    @pl.when(chip == 0)
    def _():
        out_ref[...] = state_ref[PART:, :width]

    @pl.when(chip == 1)
    def _():
        lanes = decay_lanes(state_ref[:16, width:], decay_map(width // HEAD_DIM, width))
        out_ref[...] = (
            lanes * near_ref[:, :width].astype(F32) + state_ref[:PART, :width].astype(F32)
        ).astype(BF16)


def middle_kernel(state_ref, near_ref, far_ref, out_ref, lanes_ref):
    width = out_ref.shape[1]
    chip = lax.axis_index("scan")

    @pl.when(chip == 2)
    def _():
        heads_map = decay_map(width // HEAD_DIM, width)
        lanes = decay_lanes(near_ref[:16, width:], heads_map)
        lanes_ref[...] = jnp.broadcast_to(lanes, lanes_ref.shape)
        entered = lanes * far_ref[:, :width].astype(F32) + near_ref[:, :width].astype(F32)
        own = decay_lanes(state_ref[:16, width:], heads_map)
        out_ref[...] = (own * entered + state_ref[PART:, :width].astype(F32)).astype(BF16)

    @pl.when(chip == 3)
    def _():
        lanes = decay_lanes(far_ref[:16, width:], decay_map(width // HEAD_DIM, width))
        lanes_ref[...] = jnp.broadcast_to(lanes, lanes_ref.shape)


def enter_kernel(
    near_ref,
    far_ref,
    early_ref,
    next_ref,
    far_lanes_ref,
    keep_ref,
    got_ref,
    lanes_ref,
    mine_ref,
    send_ref,
):
    width = keep_ref.shape[1]
    chip = lax.axis_index("scan")
    near, far = (ref.at[:, pl.ds(0, width)] for ref in (near_ref, far_ref))
    refs = (keep_ref, got_ref, lanes_ref, mine_ref, send_ref)

    @pl.when(chip == 0)
    def _():
        share_enter(jnp.zeros((HALF, width), F32), 0, *refs)

    @pl.when(chip == 1)
    def _():
        share_enter(near[...].astype(F32), 0, *refs)
        share_enter(early_ref[...].astype(F32), PART, *refs)

    @pl.when(chip == 2)
    def _():
        share_enter(next_ref[...].astype(F32), 0, *refs)
        share_enter(far_lanes_ref[:1] * far[...].astype(F32) + near[...].astype(F32), PART, *refs)

    @pl.when(chip == 3)
    def _():
        share_enter(far_lanes_ref[:1] * early_ref[...].astype(F32) + far[...].astype(F32), 0, *refs)


def enter_last_kernel(last_ref, keep_ref, got_ref, lanes_ref, old_mine, old_send, mine_ref, send_ref):
    @pl.when(lax.axis_index("scan") == 3)
    def _():
        share_enter(
            last_ref[...].astype(F32), PART, keep_ref, got_ref, lanes_ref, mine_ref, send_ref
        )


def share_enter(enter, first, keep_ref, got_ref, lanes_ref, mine_ref, send_ref):
    width = keep_ref.shape[1]
    core = lax.axis_index("band")
    rows = slice(first, first + enter.shape[0])

    @pl.when(core == 0)
    def _():
        mine_ref[rows, :] = enter.astype(BF16)
        send_ref[rows, :] = (lanes_ref[:1] * enter + keep_ref[rows, :]).astype(BF16)

    @pl.when(core == 1)
    def _():
        send_ref[rows, :] = enter.astype(BF16)
        mine_ref[rows, :] = (lanes_ref[:1] * enter + got_ref[rows, :width].astype(F32)).astype(BF16)


def gathered_kernel(all_ref, keep_ref, got_ref, lanes_ref, mine_ref, send_ref, enter_ref):
    width = keep_ref.shape[1]
    chip = lax.axis_index("scan")
    heads_map = decay_map(width // HEAD_DIM, width)
    enter_ref[...] = jnp.zeros(enter_ref.shape, F32)
    for source in range(all_ref.shape[0]):

        @pl.when(source < chip)
        def _():
            lanes = decay_lanes(all_ref[source, :16, width:], heads_map)
            enter_ref[...] = lanes * enter_ref[...] + all_ref[source, :, :width].astype(F32)

    share_enter(enter_ref[...], 0, keep_ref, got_ref, lanes_ref, mine_ref, send_ref)


def chip_state(keep, got, decay):
    width = keep.shape[1]
    return local_call(
        chip_kernel,
        "chip_state",
        [
            jax.ShapeDtypeStruct((HALF, width + LANES), BF16),
            jax.ShapeDtypeStruct((PART, width + LANES), BF16),
        ],
        (keep, got, decay),
    )


def entering_state(chips, state, first, keep, got, local):
    width = keep.shape[1]
    half = jax.ShapeDtypeStruct((HALF, width), BF16)
    if chips != 4:
        gathered = lax.all_gather(state, "scan", axis=0)
        second, lanes = local(0, first)
        local(1, second)
        local(2, second)
        return local_call(
            gathered_kernel,
            "enter_state",
            [half, half],
            (gathered, keep, got, lanes),
            (pltpu.VMEM((HALF, width), F32),),
        )
    near = lax.ppermute(first, "scan", [(0, 1), (1, 2)])
    second, lanes = local(0, first)
    far = lax.ppermute(second, "scan", [(0, 2), (2, 3)])
    done = local(1, second)
    (ahead,) = local_call(
        early_kernel,
        "early_state",
        [jax.ShapeDtypeStruct((PART, width), BF16)],
        (state, near),
        after=(done,),
    )
    early = lax.ppermute(ahead, "scan", [(1, 3), (0, 1)])
    following = lax.ppermute(ahead, "scan", [(1, 2)])
    middle, far_lanes = local_call(
        middle_kernel,
        "middle_state",
        [jax.ShapeDtypeStruct((PART, width), BF16), jax.ShapeDtypeStruct((8, width), F32)],
        (state, near, far),
        after=(ahead,),
    )
    last = lax.ppermute(middle, "scan", [(2, 3)])
    done = local(2, middle)
    mine, give = local_call(
        enter_kernel,
        "enter_state",
        [half, half],
        (near, far, early, following, far_lanes, keep, got, lanes),
        after=(done,),
    )
    return local_call(
        enter_last_kernel,
        "enter_last",
        [half, half],
        (last, keep, got, lanes, mine, give),
        aliases={4: 0, 5: 1},
    )


def gated_kernel(parts, mine_ref, other_ref, read_ref, gain_ref, *refs):
    bases, factors, weights = refs[:parts], refs[parts : 2 * parts], refs[2 * parts : 3 * parts]
    out_ref, square_ref, *first_refs = refs[3 * parts :]
    tokens, width = out_ref.shape
    block = column_block(width)
    is_first = lax.axis_index("band") == 0
    read = read_ref[...]
    sums = jnp.zeros((tokens, LANES), F32)
    first = 0
    for base_ref, factor_ref in zip(bases, factors):
        for start in range(0, base_ref.shape[1], block):
            lanes = slice(first, first + block)
            mine, other = mine_ref[:, lanes].astype(F32), other_ref[:, lanes].astype(F32)
            low = jnp.where(is_first, mine, other).astype(BF16)
            high = jnp.where(is_first, other, mine).astype(BF16)
            carried = dot(read, jnp.concatenate([low, high], axis=0))
            lanes = slice(start, start + block)
            gated = base_ref[:, lanes] + factor_ref[:, lanes] * carried
            for k in range(0, block, LANES):
                column = gated[:, k : k + LANES]
                row = (first + k) // LANES
                out_ref[:, first + k : first + k + LANES] = (
                    column * gain_ref[row : row + 1, :]
                ).astype(BF16)
                sums += column * column
            first += block
    square_ref[...] = jnp.broadcast_to(jnp.sum(sums.T, axis=0, keepdims=True), square_ref.shape)
    for first_ref in first_refs:
        send_kernel(0, out_ref, *weights, first_ref)
        first_ref[tokens:, :] = jnp.zeros((16, first_ref.shape[1]), BF16)
        for lane in range(0, tokens, LANES):
            lanes = slice(lane, lane + LANES)
            first_ref[tokens:, lanes] = decay_block(square_ref[:1, lanes], 16)


def gated_part(mine, other, read_proj, gain, bases, factors, weights, first):
    tokens = read_proj.shape[0]
    width = mine.shape[1]
    return local_call(
        functools.partial(gated_kernel, len(bases)),
        "gated_part",
        [
            jax.ShapeDtypeStruct((tokens, width), BF16),
            jax.ShapeDtypeStruct((8, tokens), F32),
        ]
        + [jax.ShapeDtypeStruct((tokens + 16, first), BF16)] * (first > 0),
        (mine, other, read_proj, gain, *bases, *factors, *weights),
        flops=2 * tokens * width * STATE,
    )


SENDS = (512, 384, 384)


def project(gated_ref, weights, other, first, count):
    columns = weights[0].shape[1] // 2
    member = lax.axis_index("tensor")
    start = (1 - member if other else member) * columns + first
    lanes = pl.ds(pl.multiple_of(start, LANES), count)
    row, total = 0, None
    for weight_ref in weights:
        rows = weight_ref.shape[0]
        term = dot(gated_ref[:, row : row + rows], weight_ref[:, lanes])
        row, total = row + rows, term if total is None else total + term
    return total


def send_kernel(first, gated_ref, *refs):
    *weights, out_ref = refs
    tokens, count = gated_ref.shape[0], out_ref.shape[1]
    out_ref[:tokens, :] = project(gated_ref, weights, True, first, count).astype(BF16)


def own_kernel(gated_ref, *refs):
    *weights, out_ref = refs
    count = out_ref.shape[1] // 5
    for first in range(0, out_ref.shape[1], count):
        out_ref[:, first : first + count] = project(gated_ref, weights, False, first, count)


def finish_columns(first, got_refs, own_ref, scale, out_ref, sent_ref, sems):
    tokens = own_ref.shape[0]
    copies, place = [], 0
    for got_ref in got_refs:
        count = got_ref.shape[1]
        for lane in range(0, count, LANES):
            own_lanes = slice(first + place + lane, first + place + lane + LANES)
            total = own_ref[:, own_lanes] + got_ref[:tokens, lane : lane + LANES].astype(F32)
            sent_ref[:, place + lane : place + lane + LANES] = (total * scale).astype(BF16)
        copies.append(
            pltpu.make_async_copy(
                sent_ref.at[:, pl.ds(place, count)],
                out_ref.at[:, pl.ds(first + place, count)],
                sems.at[len(copies)],
            )
        )
        copies[-1].start()
        place += count
    for copy in copies:
        copy.wait()


def finish_first_kernel(squares_ref, own_ref, got_ref, out_ref, scale_ref, sent_ref, sems):
    tokens = own_ref.shape[0]
    other_squares = got_ref[tokens:, :tokens].astype(F32)
    mean = (squares_ref[:1] + jnp.sum(other_squares, axis=0, keepdims=True)) / INNER
    scale = lax.rsqrt(mean + EPSILON)
    scale_ref[...] = jnp.broadcast_to(scale, (LANES, tokens)).T
    finish_columns(0, [got_ref], own_ref, scale_ref[...], out_ref, sent_ref, sems)


def finish_rest_kernel(scale_ref, own_ref, *refs):
    *got_refs, old_ref, out_ref, sent_ref, sems = refs
    first = own_ref.shape[1] - sent_ref.shape[1]
    finish_columns(first, got_refs, own_ref, scale_ref[...], out_ref, sent_ref, sems)


def finish(squares, own, got):
    tokens, columns = own.shape
    first = got[0].shape[1]
    shape = jax.ShapeDtypeStruct(own.shape, BF16)
    params = pltpu.CompilerParams(vmem_limit_bytes=8 * MIB)
    begun, scale = pl.pallas_call(
        finish_first_kernel,
        name="finish_first",
        out_shape=[shape, jax.ShapeDtypeStruct((tokens, LANES), F32)],
        in_specs=[IN_VMEM] * 3,
        out_specs=[IN_HBM, IN_VMEM],
        scratch_shapes=[pltpu.VMEM((tokens, first), BF16), pltpu.SemaphoreType.DMA((1,))],
        compiler_params=params,
    )(squares, own, got[0])
    args = (scale, own, *got[1:])
    return pl.pallas_call(
        finish_rest_kernel,
        name="finish_rest",
        out_shape=shape,
        in_specs=[IN_VMEM] * len(args) + [IN_HBM],
        out_specs=IN_HBM,
        input_output_aliases={len(args): 0},
        scratch_shapes=[
            pltpu.VMEM((tokens, columns - first), BF16),
            pltpu.SemaphoreType.DMA((len(got) - 1,)),
        ],
        compiler_params=params,
    )(*args, begun)


def direct(members, columns):
    return members == 2 and columns == sum(SENDS)


def layer_columns(members, gated, squares, weights, ready):
    columns = weights[0].shape[1] // members
    if not direct(members, columns):
        mean = lax.psum(squares[0], "tensor") / INNER
        partial = dot(gated, jnp.concatenate(weights, axis=0)).astype(BF16)
        total = lax.psum_scatter(partial, "tensor", scatter_dimension=1, tiled=True)
        return (total.astype(F32) * lax.rsqrt(mean + EPSILON)[:, None]).astype(BF16)
    swap = [(0, 1), (1, 0)]
    tokens = gated.shape[0]
    parts, first = [ready[0]], SENDS[0]
    for count in SENDS[1:]:
        parts += local_call(
            functools.partial(send_kernel, first),
            "project_other",
            [jax.ShapeDtypeStruct((tokens, count), BF16)],
            (gated, *weights),
            after=parts[-1:],
        )
        first += count
    got = [lax.ppermute(part, "tensor", swap) for part in parts]
    (own,) = local_call(
        own_kernel,
        "project_own",
        [jax.ShapeDtypeStruct((tokens, columns), F32)],
        (gated, *weights),
        after=parts[-1:],
    )
    return finish(squares, own, got)


def on_device(
    chips,
    members,
    signal,
    gate_branch,
    write_proj,
    read_proj,
    step_logits,
    valid_mask,
    stretch_band,
    band_offset,
    decay_log,
    step_offset,
    skip_gain,
    norm_gain,
    out_weight,
):
    small = (step_logits, valid_mask[None], band_offset, decay_log[None], step_offset[None])
    running, weight, decay, keep, send, *passed = own_state(
        stretch_band, small, write_proj, read_proj, signal, gate_branch
    )
    cores = [(0, 1), (1, 0)]
    got = lax.ppermute(send, "band", cores)
    state, first = chip_state(keep, got, decay)
    constants = (skip_gain[None], norm_gain.reshape(-1, LANES), out_weight)
    write, read, *streams = passed
    values = (running, weight, *streams)
    bases, factors, weights, prepared, gains = [], [], [], [], []

    def local(part, after):
        if not local_shares(signal.shape[1])[0][part]:
            return after
        if part:
            base, factor, matrix = local_rest(part, values, prepared, out_weight, after)
        else:
            base, factor, matrix, second, gain, *rest, lanes = local_first(
                (*values, write, read, decay, got), state, constants, after
            )
            prepared.extend(rest)
            gains.append(gain)
        bases.append(base)
        factors.append(factor)
        weights.append(matrix)
        return base if part else (second, lanes)

    mine, give = entering_state(chips, state, first, keep, got, local)
    other = lax.ppermute(give, "band", cores)
    ahead = SENDS[0] if direct(members, out_weight.shape[1] // members) else 0
    gated, squares, *ready = gated_part(
        mine, other, read, gains[0], bases, factors, weights, ahead
    )
    return layer_columns(members, gated, squares, weights, ready)


def solution(mesh):
    placed = (
        P(("group", "scan", "band"), "tensor"),
        P(("group", "scan", "band"), "tensor"),
        P(("group", "scan", "band"), None),
        P(("group", "scan", "band"), None),
        P("tensor", ("group", "scan", "band")),
        P(("group", "scan", "band")),
        P(("group", "scan", "band")),
        P(None, "tensor"),
        P("tensor"),
        P("tensor"),
        P("tensor"),
        P("tensor"),
        P("tensor", None),
    )
    return jax.shard_map(
        functools.partial(on_device, mesh.shape["scan"], mesh.shape["tensor"]),
        mesh=mesh,
        in_specs=placed,
        out_specs=P(("group", "scan", "band"), "tensor"),
        check_vma=False,
    )
```

```python
import functools

import jax
import jax.numpy as jnp
from jax import lax
from jax.experimental import pallas as pl
from jax.experimental.pallas import tpu as pltpu
from jax.sharding import PartitionSpec as P

HEAD_DIM = 64
STATE = 128
HALF = STATE // 2
PART = HALF // 2
STRETCH = 256
BANDS = 12
INNER = 5120
LANES = 128

EPSILON = 1e-05
HIGHEST = lax.Precision.HIGHEST
F32 = jnp.float32
BF16 = jnp.bfloat16
MIB = 1 << 20


def dot(a, b):
    return lax.dot_general(a, b, (((1,), (0,)), ((), ())), preferred_element_type=F32)


def pieces(x):
    high = x.astype(BF16)
    rest = x - high.astype(F32)
    middle = rest.astype(BF16)
    return high, middle, (rest - middle.astype(F32)).astype(BF16)


def head_of_lane(heads, lanes, group, first=0):
    row = lax.broadcasted_iota(jnp.int32, (heads, lanes), 0)
    lane = lax.broadcasted_iota(jnp.int32, (heads, lanes), 1)
    return (row == first + lax.shift_right_logical(lane, group)).astype(F32).astype(BF16)


def slot_of(heads):
    return -(-heads // 8) * 8


def piece_rows(values, ref):
    heads = values.shape[0]
    ref[...] = jnp.zeros(ref.shape, F32)
    for k, piece in enumerate(pieces(values)):
        first = k * slot_of(heads)
        ref[first : first + heads, :] = piece.astype(F32)
    return ref[...]


def piece_away(heads, lanes, group):
    slot = slot_of(heads)
    row = lax.broadcasted_iota(jnp.int32, (LANES, lanes), 0)
    head = row - jnp.where(row >= 2 * slot, 2 * slot, jnp.where(row >= slot, slot, 0))
    head = jnp.where(row < 3 * slot, head, -LANES)
    return head - lax.shift_right_logical(lax.broadcasted_iota(jnp.int32, (LANES, lanes), 1), group)


def piece_map(away, first):
    return jnp.where(away == first, 1.0, 0.0).astype(BF16)


def spread_heads(row, heads_map):
    return sum(dot(piece, heads_map) for piece in pieces(jnp.broadcast_to(row, (8, row.shape[1]))))[:1]


def diagonal(rows, lanes):
    return lax.broadcasted_iota(jnp.int32, (rows, lanes), 0) == lax.broadcasted_iota(
        jnp.int32, (rows, lanes), 1
    )


def to_column(row):
    count = row.shape[1]
    return jnp.sum(jnp.where(diagonal(count, count), row, 0.0), axis=1, keepdims=True)


def decay_block(row, rows):
    place = lax.broadcasted_iota(jnp.int32, (rows, LANES), 0)
    high, middle, low = (piece.astype(F32) for piece in pieces(row))
    block = jnp.where(place == 0, high, jnp.where(place == 1, middle, jnp.where(place == 2, low, 0.0)))
    return block.astype(BF16)


def decay_row(block):
    return jnp.sum(block.astype(F32), axis=0, keepdims=True)


def decay_map(heads, width):
    return head_of_lane(-(-heads // 16) * 16, width, 6)


def decay_lanes(block, heads_map):
    return jnp.sum(dot(block[:16, : heads_map.shape[0]], heads_map), axis=0, keepdims=True)


def column_block(width):
    return width // 5 if width % (5 * LANES) == 0 else width


def local_call(body, name, outs, args, scratch=(), limit=8 * MIB, flops=0, after=(), aliases=None):
    size = sum(a.size * a.dtype.itemsize for a in args) + sum(o.size * o.dtype.itemsize for o in outs)

    def kernel(*refs):
        body(*refs[: len(args)], *refs[len(args) + len(after) :])

    return pl.pallas_call(
        kernel,
        name=name,
        out_shape=outs,
        in_specs=[pl.BlockSpec(memory_space=pltpu.VMEM)] * len(args)
        + [pl.BlockSpec(memory_space=pl.ANY)] * len(after),
        out_specs=[pl.BlockSpec(memory_space=pltpu.VMEM)] * len(outs),
        scratch_shapes=list(scratch),
        input_output_aliases=aliases or {},
        compiler_params=pltpu.CompilerParams(vmem_limit_bytes=limit),
        cost_estimate=pl.CostEstimate(flops=flops, bytes_accessed=size, transcendentals=0),
    )(*args, *after)


IN_VMEM = pl.BlockSpec(memory_space=pltpu.VMEM)
IN_HBM = pl.BlockSpec(memory_space=pltpu.HBM)
ANYWHERE = pl.BlockSpec(memory_space=pl.ANY)


def in_hbm(*arrays):
    return [pltpu.with_memory_space_constraint(a, pltpu.HBM) for a in arrays]


def state_kernel(
    band_ref,
    logits_hbm,
    mask_hbm,
    offset_hbm,
    decay_log_hbm,
    step_offset_hbm,
    write_hbm,
    read_hbm,
    signal_hbm,
    gate_hbm,
    running_ref,
    weight_ref,
    decay_ref,
    keep_ref,
    send_ref,
    write_ref,
    read_ref,
    signal_ref,
    gate_ref,
    logits_ref,
    mask_ref,
    offset_ref,
    decay_log_ref,
    step_offset_ref,
    rows_ref,
    factors_ref,
    sems,
    block_sems,
):
    heads, tokens = logits_ref.shape
    width = signal_ref.shape[1]
    block = column_block(width)
    is_first = lax.axis_index("band") == 0
    pairs = (
        (logits_hbm, logits_ref),
        (mask_hbm, mask_ref),
        (offset_hbm, offset_ref),
        (decay_log_hbm, decay_log_ref),
        (step_offset_hbm, step_offset_ref),
        (write_hbm, write_ref),
        (read_hbm, read_ref),
        (gate_hbm, gate_ref),
    )
    copies = [pltpu.make_async_copy(*pair, sems.at[i]) for i, pair in enumerate(pairs)]
    blocks = [
        pltpu.make_async_copy(
            signal_hbm.at[:, pl.ds(first, block)],
            signal_ref.at[:, pl.ds(first, block)],
            block_sems.at[first // block],
        )
        for first in range(0, width, block)
    ]
    for copy in copies[:6] + blocks + copies[6:]:
        copy.start()
    for copy in copies[:6]:
        copy.wait()

    offset = to_column(step_offset_ref[...] + offset_ref[pl.ds(band_ref[0], 1), :])
    raw = logits_ref[...] + offset
    step_size = jnp.maximum(raw, 0.0) + jnp.log1p(jnp.exp(-jnp.abs(raw)))
    log_decay = step_size * to_column(-jnp.exp(decay_log_ref[...]))
    earlier = lax.broadcasted_iota(jnp.int32, (tokens, tokens), 0)
    later = lax.broadcasted_iota(jnp.int32, (tokens, tokens), 1)
    sums = dot(
        piece_rows(log_decay, rows_ref).astype(BF16), jnp.where(earlier <= later, 1.0, 0.0).astype(BF16)
    )
    slot = slot_of(heads)
    running = sums[:heads] + sums[slot : slot + heads] + sums[2 * slot : 2 * slot + heads]
    weight = step_size * mask_ref[...].astype(F32)
    running_ref[...] = running
    weight_ref[...] = weight
    total = running[:, tokens - 1 : tokens]
    row = jnp.sum(jnp.where(diagonal(heads, LANES), jnp.exp(total), 0.0), axis=0, keepdims=True)
    send_ref[:, width:] = decay_block(row, HALF)
    decay_ref[...] = decay_block(row, 16)

    tail = piece_rows(jnp.exp(total - running) * weight, rows_ref).T.astype(BF16)
    write = write_ref[...].astype(F32).T
    low, high = write[:HALF], write[HALF:]
    write = jnp.concatenate(
        [jnp.where(is_first, low, high), jnp.where(is_first, high, low)], axis=0
    ).astype(BF16)
    away = piece_away(heads, block, 6)
    for first in range(0, width, block):
        factors_ref[:, first : first + block] = dot(tail, piece_map(away, first // HEAD_DIM))
    for copy in blocks:
        copy.wait()
    for first in range(0, width, block):
        lanes = slice(first, first + block)
        scaled = (signal_ref[:, lanes].astype(F32) * factors_ref[:, lanes]).astype(BF16)
        state = dot(write, scaled)
        keep_ref[:, lanes] = state[:HALF]
        send_ref[:, lanes] = state[HALF:].astype(BF16)
    for copy in copies[6:]:
        copy.wait()


def own_state(stretch_band, small, write_proj, read_proj, signal, gate_branch):
    tokens, width = signal.shape
    heads = small[0].shape[0]
    passed = (write_proj, read_proj, signal, gate_branch)
    return pl.pallas_call(
        state_kernel,
        name="own_state",
        out_shape=[
            jax.ShapeDtypeStruct((heads, tokens), F32),
            jax.ShapeDtypeStruct((heads, tokens), F32),
            jax.ShapeDtypeStruct((16, LANES), BF16),
            jax.ShapeDtypeStruct((HALF, width), F32),
            jax.ShapeDtypeStruct((HALF, width + LANES), BF16),
        ]
        + [jax.ShapeDtypeStruct(a.shape, a.dtype) for a in passed],
        in_specs=[pl.BlockSpec(memory_space=pltpu.SMEM)] + [IN_HBM] * 9,
        out_specs=[IN_VMEM] * 9,
        scratch_shapes=[pltpu.VMEM(a.shape, a.dtype) for a in small]
        + [
            pltpu.VMEM((LANES, tokens), F32),
            pltpu.VMEM((tokens, width), F32),
            pltpu.SemaphoreType.DMA((8,)),
            pltpu.SemaphoreType.DMA((width // column_block(width),)),
        ],
        compiler_params=pltpu.CompilerParams(vmem_limit_bytes=16 * MIB),
        cost_estimate=pl.CostEstimate(
            flops=4 * tokens * width * STATE, bytes_accessed=tokens * width * 2, transcendentals=0
        ),
    )(stretch_band, *in_hbm(*small, *passed))


def prepare_local(
    running_ref, write_ref, read_ref, decay_ref, got_ref, scores_ref, running_pieces_ref, decay_pieces_ref, lanes_ref, rows_ref
):
    width = lanes_ref.shape[1]
    scores = lax.dot_general(
        read_ref[...], write_ref[...], (((1,), (1,)), ((), ())), preferred_element_type=F32
    )
    row = lax.broadcasted_iota(jnp.int32, scores.shape, 0)
    lane = lax.broadcasted_iota(jnp.int32, scores.shape, 1)
    scores_ref[...] = jnp.where(row >= lane, scores, 0.0)
    running = running_ref[...]
    running_pieces_ref[...] = piece_rows(running, rows_ref).T.astype(BF16)
    decay_pieces_ref[...] = piece_rows(jnp.exp(running), rows_ref).T.astype(BF16)
    mine, got = decay_ref[...].astype(F32), got_ref[:16, width:].astype(F32)
    first_core = jnp.where(lax.axis_index("band") == 0, mine, got).astype(BF16)
    lanes_ref[...] = jnp.broadcast_to(
        decay_lanes(first_core, decay_map(width // HEAD_DIM, width)), lanes_ref.shape
    )


def local_heads(
    first_block,
    running_ref,
    weight_ref,
    signal_ref,
    gate_ref,
    scores_ref,
    running_pieces_ref,
    decay_pieces_ref,
    skip_ref,
    base_ref,
    factor_ref,
):
    heads, tokens = running_ref.shape
    block = column_block(signal_ref.shape[1])
    half = tokens // 2
    low_lanes = lax.broadcasted_iota(jnp.int32, (half, LANES), 1) < HEAD_DIM
    early, late = slice(0, half), slice(half, tokens)

    wide_away, away = piece_away(heads, 2 * block, 7), piece_away(heads, block, 6)

    def heads_block(at, _):
        first_head = (first_block + at) * (block // HEAD_DIM)

        def whole_lanes(lane, count):
            return pl.ds(pl.multiple_of((first_block + at) * block + lane, LANES), count)

        def part_lanes(lane, count):
            return pl.ds(pl.multiple_of(at * block + lane, LANES), count)

        wide = dot(running_pieces_ref[...], piece_map(wide_away, first_head))
        gate = gate_ref[:, whole_lanes(0, block)].astype(F32)
        gate = gate / (1.0 + jnp.exp(-gate))
        factor_ref[:, part_lanes(0, block)] = (
            dot(decay_pieces_ref[...], piece_map(away, first_head)) * gate
        )
        skip = spread_heads(skip_ref[...], head_of_lane(heads, block, 6, first_head))
        for pair in range(block // LANES):
            lanes = slice(pair * LANES, (pair + 1) * LANES)
            values = signal_ref[:, whole_lanes(pair * LANES, LANES)]
            top, bottom = [], []
            for k in (2 * pair, 2 * pair + 1):
                row = running_ref[pl.ds(first_head + k, 1), :]
                weight = weight_ref[pl.ds(first_head + k, 1), :]
                column = wide[:, k * LANES : (k + 1) * LANES]

                def mixing(rows, cols):
                    span = jnp.minimum(column[rows] - row[:, cols], 0.0)
                    return (jnp.exp(span) * scores_ref[rows, cols] * weight[:, cols]).astype(BF16)

                top.append(mixing(early, early))
                bottom.append(jnp.concatenate([mixing(late, early), mixing(late, late)], axis=1))
            top = dot(jnp.concatenate(top, axis=0), values[early])
            bottom = dot(jnp.concatenate(bottom, axis=0), values)
            skipped = values.astype(F32) * skip[:, lanes]
            out_lanes = part_lanes(pair * LANES, LANES)
            base_ref[early, out_lanes] = (
                jnp.where(low_lanes, top[:half], top[half:]) + skipped[early]
            ) * gate[early, lanes]
            base_ref[late, out_lanes] = (
                jnp.where(low_lanes, bottom[:half], bottom[half:]) + skipped[late]
            ) * gate[late, lanes]
        return 0

    lax.fori_loop(0, base_ref.shape[1] // block, heads_block, 0)


def local_first_kernel(
    running_ref,
    weight_ref,
    signal_ref,
    gate_ref,
    write_ref,
    read_ref,
    decay_ref,
    got_ref,
    state_ref,
    skip_hbm,
    gain_hbm,
    matrix_hbm,
    after_ref,
    base_ref,
    factor_ref,
    matrix_ref,
    second_ref,
    halves_ref,
    gain_ref,
    scores_ref,
    running_pieces_ref,
    decay_pieces_ref,
    skip_ref,
    lanes_ref,
    rows_ref,
    sems,
):
    rows = matrix_ref.shape[0]
    pairs = (
        (skip_hbm, skip_ref),
        (gain_hbm, gain_ref),
        (matrix_hbm.at[pl.ds(0, rows), :], matrix_ref),
    )
    copies = [pltpu.make_async_copy(*pair, sems.at[i]) for i, pair in enumerate(pairs)]
    for copy in copies:
        copy.start()
    read = read_ref[...].astype(F32)
    swapped = jnp.concatenate([read[:, HALF:], read[:, :HALF]], axis=1)
    halves_ref[...] = jnp.where(lax.axis_index("band") == 0, read, swapped).astype(BF16)
    upper = lax.axis_index("scan") == 2
    second_ref[...] = state_ref[pl.ds(pl.multiple_of(jnp.where(upper, 0, PART), PART), PART), :]
    prepared = (scores_ref, running_pieces_ref, decay_pieces_ref)
    prepare_local(running_ref, write_ref, read_ref, decay_ref, got_ref, *prepared, lanes_ref, rows_ref)
    copies[0].wait()
    local_heads(
        0, running_ref, weight_ref, signal_ref, gate_ref, *prepared, skip_ref, base_ref, factor_ref
    )
    for copy in copies[1:]:
        copy.wait()


def local_rest_kernel(
    first_block,
    first_row,
    running_ref,
    weight_ref,
    signal_ref,
    gate_ref,
    scores_ref,
    running_pieces_ref,
    decay_pieces_ref,
    skip_ref,
    matrix_hbm,
    after_ref,
    base_ref,
    factor_ref,
    matrix_ref,
    sem,
):
    rows = matrix_ref.shape[0]
    copy = pltpu.make_async_copy(matrix_hbm.at[pl.ds(first_row, rows), :], matrix_ref, sem)
    copy.start()
    local_heads(
        first_block,
        running_ref,
        weight_ref,
        signal_ref,
        gate_ref,
        scores_ref,
        running_pieces_ref,
        decay_pieces_ref,
        skip_ref,
        base_ref,
        factor_ref,
    )
    copy.wait()


def local_shares(width):
    if width % (10 * LANES):
        return (width // column_block(width), 0, 0), (width, 0, 0)
    tenth = width // 10
    return (1, 2, 2), (tenth, 3 * tenth, 6 * tenth)


def local_call_of(kernel, name, part, outs, resident, passed, after, scratch):
    tokens, width = resident[2].shape
    matrix = passed[-1]
    blocks, rows = local_shares(width)
    columns = blocks[part] * column_block(width)
    return pl.pallas_call(
        kernel,
        name=name,
        out_shape=[jax.ShapeDtypeStruct((tokens, columns), F32)] * 2
        + [jax.ShapeDtypeStruct((rows[part], matrix.shape[1]), BF16)]
        + outs,
        in_specs=[IN_VMEM] * len(resident) + [IN_HBM] * len(passed) + [ANYWHERE],
        out_specs=[IN_VMEM] * (3 + len(outs)),
        scratch_shapes=scratch,
        compiler_params=pltpu.CompilerParams(vmem_limit_bytes=16 * MIB),
        cost_estimate=pl.CostEstimate(
            flops=6 * columns * tokens * tokens,
            bytes_accessed=tokens * columns * 12,
            transcendentals=columns // HEAD_DIM * tokens * tokens,
        ),
    )(*resident, *in_hbm(*passed), after)


def local_first(values, state, constants, after):
    running, signal = values[0], values[2]
    skip_gain, norm_gain, _ = constants
    tokens, width = signal.shape
    pieces_shape = jax.ShapeDtypeStruct((tokens, LANES), BF16)
    return local_call_of(
        local_first_kernel,
        "local_first",
        0,
        [
            jax.ShapeDtypeStruct((PART, state.shape[1]), BF16),
            jax.ShapeDtypeStruct((tokens, STATE), BF16),
            jax.ShapeDtypeStruct(norm_gain.shape, F32),
            jax.ShapeDtypeStruct((tokens, tokens), F32),
            pieces_shape,
            pieces_shape,
            jax.ShapeDtypeStruct(skip_gain.shape, F32),
            jax.ShapeDtypeStruct((8, width), F32),
        ],
        (*values, state),
        constants,
        after,
        [pltpu.VMEM((LANES, tokens), F32), pltpu.SemaphoreType.DMA((3,))],
    )


def local_rest(part, values, prepared, out_weight, after):
    blocks, rows = local_shares(values[2].shape[1])
    return local_call_of(
        functools.partial(local_rest_kernel, sum(blocks[:part]), sum(rows[:part])),
        "local_rest",
        part,
        [],
        (*values, *prepared),
        (out_weight,),
        after,
        [pltpu.SemaphoreType.DMA(())],
    )


def chip_kernel(keep_ref, got_ref, decay_ref, state_ref, first_ref):
    width = keep_ref.shape[1]
    core = lax.axis_index("band")
    chip = lax.axis_index("scan")
    heads_map = decay_map(width // HEAD_DIM, width)
    got_decay = got_ref[:16, width:]
    mine = decay_ref[...]
    later = jnp.where(core == 0, got_decay.astype(F32), mine.astype(F32)).astype(BF16)
    lanes = decay_lanes(later, heads_map)
    got = got_ref[:, :width].astype(F32)
    keep = keep_ref[...]
    early, late = jnp.where(core == 0, keep, got), jnp.where(core == 0, got, keep)
    state_ref[:, :width] = (early * lanes + late).astype(BF16)
    block = decay_block(decay_row(got_decay) * decay_row(mine), PART)
    state_ref[:PART, width:] = block
    state_ref[PART:, width:] = block

    lower = jnp.where(chip == 1, PART, 0)
    first_ref[...] = state_ref[pl.ds(pl.multiple_of(lower, PART), PART), :]


def early_kernel(state_ref, near_ref, out_ref):
    width = out_ref.shape[1]
    chip = lax.axis_index("scan")

    @pl.when(chip == 0)
    def _():
        out_ref[...] = state_ref[PART:, :width]

    @pl.when(chip == 1)
    def _():
        lanes = decay_lanes(state_ref[:16, width:], decay_map(width // HEAD_DIM, width))
        out_ref[...] = (
            lanes * near_ref[:, :width].astype(F32) + state_ref[:PART, :width].astype(F32)
        ).astype(BF16)


def middle_kernel(state_ref, near_ref, far_ref, out_ref, lanes_ref):
    width = out_ref.shape[1]
    chip = lax.axis_index("scan")

    @pl.when(chip == 2)
    def _():
        heads_map = decay_map(width // HEAD_DIM, width)
        lanes = decay_lanes(near_ref[:16, width:], heads_map)
        lanes_ref[...] = jnp.broadcast_to(lanes, lanes_ref.shape)
        entered = lanes * far_ref[:, :width].astype(F32) + near_ref[:, :width].astype(F32)
        own = decay_lanes(state_ref[:16, width:], heads_map)
        out_ref[...] = (own * entered + state_ref[PART:, :width].astype(F32)).astype(BF16)

    @pl.when(chip == 3)
    def _():
        lanes = decay_lanes(far_ref[:16, width:], decay_map(width // HEAD_DIM, width))
        lanes_ref[...] = jnp.broadcast_to(lanes, lanes_ref.shape)


def enter_kernel(
    near_ref,
    far_ref,
    early_ref,
    next_ref,
    far_lanes_ref,
    keep_ref,
    got_ref,
    lanes_ref,
    mine_ref,
    send_ref,
):
    width = keep_ref.shape[1]
    chip = lax.axis_index("scan")
    near, far = (ref.at[:, pl.ds(0, width)] for ref in (near_ref, far_ref))
    refs = (keep_ref, got_ref, lanes_ref, mine_ref, send_ref)

    @pl.when(chip == 0)
    def _():
        share_enter(jnp.zeros((HALF, width), F32), 0, *refs)

    @pl.when(chip == 1)
    def _():
        share_enter(near[...].astype(F32), 0, *refs)
        share_enter(early_ref[...].astype(F32), PART, *refs)

    @pl.when(chip == 2)
    def _():
        share_enter(next_ref[...].astype(F32), 0, *refs)
        share_enter(far_lanes_ref[:1] * far[...].astype(F32) + near[...].astype(F32), PART, *refs)

    @pl.when(chip == 3)
    def _():
        share_enter(far_lanes_ref[:1] * early_ref[...].astype(F32) + far[...].astype(F32), 0, *refs)


def enter_last_kernel(last_ref, keep_ref, got_ref, lanes_ref, old_mine, old_send, mine_ref, send_ref):
    @pl.when(lax.axis_index("scan") == 3)
    def _():
        share_enter(
            last_ref[...].astype(F32), PART, keep_ref, got_ref, lanes_ref, mine_ref, send_ref
        )


def share_enter(enter, first, keep_ref, got_ref, lanes_ref, mine_ref, send_ref):
    width = keep_ref.shape[1]
    core = lax.axis_index("band")
    rows = slice(first, first + enter.shape[0])

    @pl.when(core == 0)
    def _():
        mine_ref[rows, :] = enter.astype(BF16)
        send_ref[rows, :] = (lanes_ref[:1] * enter + keep_ref[rows, :]).astype(BF16)

    @pl.when(core == 1)
    def _():
        send_ref[rows, :] = enter.astype(BF16)
        mine_ref[rows, :] = (lanes_ref[:1] * enter + got_ref[rows, :width].astype(F32)).astype(BF16)


def gathered_kernel(all_ref, keep_ref, got_ref, lanes_ref, mine_ref, send_ref, enter_ref):
    width = keep_ref.shape[1]
    chip = lax.axis_index("scan")
    heads_map = decay_map(width // HEAD_DIM, width)
    enter_ref[...] = jnp.zeros(enter_ref.shape, F32)
    for source in range(all_ref.shape[0]):

        @pl.when(source < chip)
        def _():
            lanes = decay_lanes(all_ref[source, :16, width:], heads_map)
            enter_ref[...] = lanes * enter_ref[...] + all_ref[source, :, :width].astype(F32)

    share_enter(enter_ref[...], 0, keep_ref, got_ref, lanes_ref, mine_ref, send_ref)


def chip_state(keep, got, decay):
    width = keep.shape[1]
    return local_call(
        chip_kernel,
        "chip_state",
        [
            jax.ShapeDtypeStruct((HALF, width + LANES), BF16),
            jax.ShapeDtypeStruct((PART, width + LANES), BF16),
        ],
        (keep, got, decay),
    )


def entering_state(chips, state, first, keep, got, local):
    width = keep.shape[1]
    half = jax.ShapeDtypeStruct((HALF, width), BF16)
    if chips != 4:
        gathered = lax.all_gather(state, "scan", axis=0)
        second, lanes = local(0, first)
        local(1, second)
        local(2, second)
        return local_call(
            gathered_kernel,
            "enter_state",
            [half, half],
            (gathered, keep, got, lanes),
            (pltpu.VMEM((HALF, width), F32),),
        )
    near = lax.ppermute(first, "scan", [(0, 1), (1, 2)])
    second, lanes = local(0, first)
    far = lax.ppermute(second, "scan", [(0, 2), (2, 3)])
    done = local(1, second)
    (ahead,) = local_call(
        early_kernel,
        "early_state",
        [jax.ShapeDtypeStruct((PART, width), BF16)],
        (state, near),
        after=(done,),
    )
    early = lax.ppermute(ahead, "scan", [(1, 3), (0, 1)])
    following = lax.ppermute(ahead, "scan", [(1, 2)])
    middle, far_lanes = local_call(
        middle_kernel,
        "middle_state",
        [jax.ShapeDtypeStruct((PART, width), BF16), jax.ShapeDtypeStruct((8, width), F32)],
        (state, near, far),
        after=(ahead,),
    )
    last = lax.ppermute(middle, "scan", [(2, 3)])
    done = local(2, middle)
    mine, give = local_call(
        enter_kernel,
        "enter_state",
        [half, half],
        (near, far, early, following, far_lanes, keep, got, lanes),
        after=(done,),
    )
    return local_call(
        enter_last_kernel,
        "enter_last",
        [half, half],
        (last, keep, got, lanes, mine, give),
        aliases={4: 0, 5: 1},
    )


def gated_kernel(parts, mine_ref, other_ref, read_ref, gain_ref, *refs):
    bases, factors, weights = refs[:parts], refs[parts : 2 * parts], refs[2 * parts : 3 * parts]
    out_ref, square_ref, *first_refs = refs[3 * parts :]
    tokens, width = out_ref.shape
    block = column_block(width)
    read = read_ref[...]
    sums = jnp.zeros((tokens, LANES), F32)
    first = 0
    for base_ref, factor_ref in zip(bases, factors):
        for start in range(0, base_ref.shape[1], block):
            lanes = slice(first, first + block)
            carried = dot(read, jnp.concatenate([mine_ref[:, lanes], other_ref[:, lanes]], axis=0))
            lanes = slice(start, start + block)
            gated = base_ref[:, lanes] + factor_ref[:, lanes] * carried
            for k in range(0, block, LANES):
                column = gated[:, k : k + LANES]
                row = (first + k) // LANES
                out_ref[:, first + k : first + k + LANES] = (
                    column * gain_ref[row : row + 1, :]
                ).astype(BF16)
                sums += column * column
            first += block
    for first_ref in first_refs:
        send_kernel(0, out_ref, *weights, first_ref)
    squares = jnp.sum(sums.T, axis=0, keepdims=True)
    for row in range(tokens // LANES):
        square_ref[row : row + 1, :] = squares[:, row * LANES : (row + 1) * LANES]


def gated_part(mine, other, read_proj, gain, bases, factors, weights, first):
    tokens = read_proj.shape[0]
    width = mine.shape[1]
    return local_call(
        functools.partial(gated_kernel, len(bases)),
        "gated_part",
        [
            jax.ShapeDtypeStruct((tokens, width), BF16),
            jax.ShapeDtypeStruct((tokens // LANES, LANES), F32),
        ]
        + [jax.ShapeDtypeStruct((tokens, first), BF16)] * (first > 0),
        (mine, other, read_proj, gain, *bases, *factors, *weights),
        flops=2 * tokens * width * STATE,
    )


SENDS = (256, 384, 384, 256)
FINISH_FLOPS = 2 * 10**9


def project(gated_ref, weights, other, first, count):
    columns = weights[0].shape[1] // 2
    member = lax.axis_index("tensor")
    start = (1 - member if other else member) * columns + first
    lanes = pl.ds(pl.multiple_of(start, LANES), count)
    row, total = 0, None
    for weight_ref in weights:
        rows = weight_ref.shape[0]
        term = dot(gated_ref[:, row : row + rows], weight_ref[:, lanes])
        row, total = row + rows, term if total is None else total + term
    return total


def send_kernel(first, gated_ref, *refs):
    *weights, out_ref = refs
    count = out_ref.shape[1]
    out_ref[...] = project(gated_ref, weights, True, first, count).astype(BF16)


def own_kernel(gated_ref, *refs):
    *weights, out_ref = refs
    count = out_ref.shape[1] // 5
    for first in range(0, out_ref.shape[1], count):
        out_ref[:, first : first + count] = project(gated_ref, weights, False, first, count)


def finish_kernel(first, squares_ref, other_squares_ref, own_ref, got_ref, *refs):
    out_ref, sent_ref, sem = refs[-3:]
    tokens, count = got_ref.shape
    mean = (squares_ref[...] + other_squares_ref[...]) / INNER
    scale = lax.rsqrt(mean + EPSILON)
    scale = jnp.concatenate(
        [jnp.broadcast_to(scale[k : k + 1], (LANES, LANES)).T for k in range(tokens // LANES)], axis=0
    )
    for lane in range(0, count, LANES):
        lanes = slice(lane, lane + LANES)
        total = own_ref[:, first + lane : first + lane + LANES] + got_ref[:, lanes].astype(F32)
        sent_ref[:, lanes] = (total * scale).astype(BF16)
    copy = pltpu.make_async_copy(sent_ref, out_ref.at[:, pl.ds(first, count)], sem)
    copy.start()
    copy.wait()


def finish(squares, other_squares, own, got):
    result, first = [], 0
    for part in got:
        args = (squares, other_squares, own, part)
        result = [
            pl.pallas_call(
                functools.partial(finish_kernel, first),
                name="finish",
                out_shape=jax.ShapeDtypeStruct(own.shape, BF16),
                in_specs=[IN_VMEM] * len(args) + [IN_HBM] * len(result),
                out_specs=IN_HBM,
                input_output_aliases={len(args): 0} if result else {},
                scratch_shapes=[pltpu.VMEM(part.shape, BF16), pltpu.SemaphoreType.DMA(())],
                compiler_params=pltpu.CompilerParams(vmem_limit_bytes=8 * MIB),
                cost_estimate=pl.CostEstimate(flops=FINISH_FLOPS, bytes_accessed=0, transcendentals=0),
            )(*args, *result)
        ]
        first += part.shape[1]
    return result[0]


def direct(members, columns):
    return members == 2 and columns == sum(SENDS)


def layer_columns(members, gated, squares, weights, ready):
    columns = weights[0].shape[1] // members
    if not direct(members, columns):
        mean = lax.psum(squares.reshape(-1), "tensor") / INNER
        partial = dot(gated, jnp.concatenate(weights, axis=0)).astype(BF16)
        total = lax.psum_scatter(partial, "tensor", scatter_dimension=1, tiled=True)
        return (total.astype(F32) * lax.rsqrt(mean + EPSILON)[:, None]).astype(BF16)
    swap = [(0, 1), (1, 0)]
    tokens = gated.shape[0]
    parts, first = [ready[0]], SENDS[0]
    for count in SENDS[1:]:
        parts += local_call(
            functools.partial(send_kernel, first),
            "project_other",
            [jax.ShapeDtypeStruct((tokens, count), BF16)],
            (gated, *weights),
            after=parts[-1:],
        )
        first += count
    got = [lax.ppermute(part, "tensor", swap) for part in parts]
    other_squares = lax.ppermute(squares, "tensor", swap)
    (own,) = local_call(
        own_kernel,
        "project_own",
        [jax.ShapeDtypeStruct((tokens, columns), F32)],
        (gated, *weights),
        after=parts[-1:],
    )
    return finish(squares, other_squares, own, got)


def on_device(
    chips,
    members,
    signal,
    gate_branch,
    write_proj,
    read_proj,
    step_logits,
    valid_mask,
    stretch_band,
    band_offset,
    decay_log,
    step_offset,
    skip_gain,
    norm_gain,
    out_weight,
):
    small = (step_logits, valid_mask[None], band_offset, decay_log[None], step_offset[None])
    running, weight, decay, keep, send, *passed = own_state(
        stretch_band, small, write_proj, read_proj, signal, gate_branch
    )
    cores = [(0, 1), (1, 0)]
    got = lax.ppermute(send, "band", cores)
    state, first = chip_state(keep, got, decay)
    constants = (skip_gain[None], norm_gain.reshape(-1, LANES), out_weight)
    write, read, *streams = passed
    values = (running, weight, *streams)
    bases, factors, weights, prepared, halves, gains = [], [], [], [], [], []

    def local(part, after):
        if not local_shares(signal.shape[1])[0][part]:
            return after
        if part:
            base, factor, matrix = local_rest(part, values, prepared, out_weight, after)
        else:
            base, factor, matrix, second, *kept, lanes = local_first(
                (*values, write, read, decay, got), state, constants, after
            )
            halves.append(kept[0])
            gains.append(kept[1])
            prepared.extend(kept[2:])
        bases.append(base)
        factors.append(factor)
        weights.append(matrix)
        return base if part else (second, lanes)

    mine, give = entering_state(chips, state, first, keep, got, local)
    other = lax.ppermute(give, "band", cores)
    ahead = SENDS[0] if direct(members, out_weight.shape[1] // members) else 0
    gated, squares, *ready = gated_part(
        mine, other, halves[0], gains[0], bases, factors, weights, ahead
    )
    return layer_columns(members, gated, squares, weights, ready)


def solution(mesh):
    placed = (
        P(("group", "scan", "band"), "tensor"),
        P(("group", "scan", "band"), "tensor"),
        P(("group", "scan", "band"), None),
        P(("group", "scan", "band"), None),
        P("tensor", ("group", "scan", "band")),
        P(("group", "scan", "band")),
        P(("group", "scan", "band")),
        P(None, "tensor"),
        P("tensor"),
        P("tensor"),
        P("tensor"),
        P("tensor"),
        P("tensor", None),
    )
    return jax.shard_map(
        functools.partial(on_device, mesh.shape["scan"], mesh.shape["tensor"]),
        mesh=mesh,
        in_specs=placed,
        out_specs=P(("group", "scan", "band"), "tensor"),
        check_vma=False,
    )
```

```python
import functools

import jax
import jax.numpy as jnp
from jax import lax
from jax.experimental import pallas as pl
from jax.experimental.pallas import tpu as pltpu
from jax.sharding import PartitionSpec as P

HEAD_DIM = 64
STATE = 128
HALF = STATE // 2
PART = HALF // 2
STRETCH = 256
BANDS = 12
INNER = 5120
LANES = 128

EPSILON = 1e-05
HIGHEST = lax.Precision.HIGHEST
F32 = jnp.float32
BF16 = jnp.bfloat16
MIB = 1 << 20


def dot(a, b):
    return lax.dot_general(a, b, (((1,), (0,)), ((), ())), preferred_element_type=F32)


def pieces(x):
    high = x.astype(BF16)
    rest = x - high.astype(F32)
    middle = rest.astype(BF16)
    return high, middle, (rest - middle.astype(F32)).astype(BF16)


def head_of_lane(heads, lanes, group, first=0):
    row = lax.broadcasted_iota(jnp.int32, (heads, lanes), 0)
    lane = lax.broadcasted_iota(jnp.int32, (heads, lanes), 1)
    return (row == first + lax.shift_right_logical(lane, group)).astype(F32).astype(BF16)


def slot_of(heads):
    return -(-heads // 8) * 8


def piece_rows(values, ref):
    heads = values.shape[0]
    ref[...] = jnp.zeros(ref.shape, F32)
    for k, piece in enumerate(pieces(values)):
        first = k * slot_of(heads)
        ref[first : first + heads, :] = piece.astype(F32)
    return ref[...]


def piece_away(heads, lanes, group):
    slot = slot_of(heads)
    row = lax.broadcasted_iota(jnp.int32, (LANES, lanes), 0)
    head = row - jnp.where(row >= 2 * slot, 2 * slot, jnp.where(row >= slot, slot, 0))
    head = jnp.where(row < 3 * slot, head, -LANES)
    return head - lax.shift_right_logical(lax.broadcasted_iota(jnp.int32, (LANES, lanes), 1), group)


def piece_map(away, first):
    return jnp.where(away == first, 1.0, 0.0).astype(BF16)


def spread_heads(row, heads_map):
    return sum(dot(piece, heads_map) for piece in pieces(jnp.broadcast_to(row, (8, row.shape[1]))))[:1]


def diagonal(rows, lanes):
    return lax.broadcasted_iota(jnp.int32, (rows, lanes), 0) == lax.broadcasted_iota(
        jnp.int32, (rows, lanes), 1
    )


def to_column(row):
    count = row.shape[1]
    return jnp.sum(jnp.where(diagonal(count, count), row, 0.0), axis=1, keepdims=True)


def decay_block(row, rows):
    place = lax.broadcasted_iota(jnp.int32, (rows, LANES), 0)
    high, middle, low = (piece.astype(F32) for piece in pieces(row))
    block = jnp.where(place == 0, high, jnp.where(place == 1, middle, jnp.where(place == 2, low, 0.0)))
    return block.astype(BF16)


def decay_row(block):
    return jnp.sum(block.astype(F32), axis=0, keepdims=True)


def decay_map(heads, width):
    return head_of_lane(-(-heads // 16) * 16, width, 6)


def decay_lanes(block, heads_map):
    return jnp.sum(dot(block[:16, : heads_map.shape[0]], heads_map), axis=0, keepdims=True)


def column_block(width):
    return width // 5 if width % (5 * LANES) == 0 else width


def local_call(body, name, outs, args, scratch=(), limit=8 * MIB, flops=0, after=(), aliases=None):
    size = sum(a.size * a.dtype.itemsize for a in args) + sum(o.size * o.dtype.itemsize for o in outs)

    def kernel(*refs):
        body(*refs[: len(args)], *refs[len(args) + len(after) :])

    return pl.pallas_call(
        kernel,
        name=name,
        out_shape=outs,
        in_specs=[pl.BlockSpec(memory_space=pltpu.VMEM)] * len(args)
        + [pl.BlockSpec(memory_space=pl.ANY)] * len(after),
        out_specs=[pl.BlockSpec(memory_space=pltpu.VMEM)] * len(outs),
        scratch_shapes=list(scratch),
        input_output_aliases=aliases or {},
        compiler_params=pltpu.CompilerParams(vmem_limit_bytes=limit),
        cost_estimate=pl.CostEstimate(flops=flops, bytes_accessed=size, transcendentals=0),
    )(*args, *after)


IN_VMEM = pl.BlockSpec(memory_space=pltpu.VMEM)
IN_HBM = pl.BlockSpec(memory_space=pltpu.HBM)
ANYWHERE = pl.BlockSpec(memory_space=pl.ANY)


def in_hbm(*arrays):
    return [pltpu.with_memory_space_constraint(a, pltpu.HBM) for a in arrays]


def state_kernel(
    band_ref,
    logits_hbm,
    mask_hbm,
    offset_hbm,
    decay_log_hbm,
    step_offset_hbm,
    write_hbm,
    read_hbm,
    signal_hbm,
    gate_hbm,
    running_ref,
    weight_ref,
    decay_ref,
    keep_ref,
    send_ref,
    write_ref,
    read_ref,
    signal_ref,
    gate_ref,
    logits_ref,
    mask_ref,
    offset_ref,
    decay_log_ref,
    step_offset_ref,
    rows_ref,
    factors_ref,
    sems,
    block_sems,
):
    heads, tokens = logits_ref.shape
    width = signal_ref.shape[1]
    block = column_block(width)
    is_first = lax.axis_index("band") == 0
    pairs = (
        (logits_hbm, logits_ref),
        (mask_hbm, mask_ref),
        (offset_hbm, offset_ref),
        (decay_log_hbm, decay_log_ref),
        (step_offset_hbm, step_offset_ref),
        (write_hbm, write_ref),
        (read_hbm, read_ref),
        (gate_hbm, gate_ref),
    )
    copies = [pltpu.make_async_copy(*pair, sems.at[i]) for i, pair in enumerate(pairs)]
    blocks = [
        pltpu.make_async_copy(
            signal_hbm.at[:, pl.ds(first, block)],
            signal_ref.at[:, pl.ds(first, block)],
            block_sems.at[first // block],
        )
        for first in range(0, width, block)
    ]
    for copy in copies[:6] + blocks + copies[6:]:
        copy.start()
    for copy in copies[:6]:
        copy.wait()

    offset = to_column(step_offset_ref[...] + offset_ref[pl.ds(band_ref[0], 1), :])
    raw = logits_ref[...] + offset
    step_size = jnp.maximum(raw, 0.0) + jnp.log1p(jnp.exp(-jnp.abs(raw)))
    log_decay = step_size * to_column(-jnp.exp(decay_log_ref[...]))
    earlier = lax.broadcasted_iota(jnp.int32, (tokens, tokens), 0)
    later = lax.broadcasted_iota(jnp.int32, (tokens, tokens), 1)
    sums = dot(
        piece_rows(log_decay, rows_ref).astype(BF16), jnp.where(earlier <= later, 1.0, 0.0).astype(BF16)
    )
    slot = slot_of(heads)
    running = sums[:heads] + sums[slot : slot + heads] + sums[2 * slot : 2 * slot + heads]
    weight = step_size * mask_ref[...].astype(F32)
    running_ref[...] = running
    weight_ref[...] = weight
    total = running[:, tokens - 1 : tokens]
    row = jnp.sum(jnp.where(diagonal(heads, LANES), jnp.exp(total), 0.0), axis=0, keepdims=True)
    send_ref[:, width:] = decay_block(row, HALF)
    decay_ref[...] = decay_block(row, 16)

    tail = piece_rows(jnp.exp(total - running) * weight, rows_ref).T.astype(BF16)
    write = write_ref[...].astype(F32).T
    low, high = write[:HALF], write[HALF:]
    write = jnp.concatenate(
        [jnp.where(is_first, low, high), jnp.where(is_first, high, low)], axis=0
    ).astype(BF16)
    away = piece_away(heads, block, 6)
    for first in range(0, width, block):
        factors_ref[:, first : first + block] = dot(tail, piece_map(away, first // HEAD_DIM))
    for copy in blocks:
        copy.wait()
    for first in range(0, width, block):
        lanes = slice(first, first + block)
        scaled = (signal_ref[:, lanes].astype(F32) * factors_ref[:, lanes]).astype(BF16)
        state = dot(write, scaled)
        keep_ref[:, lanes] = state[:HALF]
        send_ref[:, lanes] = state[HALF:].astype(BF16)
    for copy in copies[6:]:
        copy.wait()


def own_state(stretch_band, small, write_proj, read_proj, signal, gate_branch):
    tokens, width = signal.shape
    heads = small[0].shape[0]
    passed = (write_proj, read_proj, signal, gate_branch)
    return pl.pallas_call(
        state_kernel,
        name="own_state",
        out_shape=[
            jax.ShapeDtypeStruct((heads, tokens), F32),
            jax.ShapeDtypeStruct((heads, tokens), F32),
            jax.ShapeDtypeStruct((16, LANES), BF16),
            jax.ShapeDtypeStruct((HALF, width), F32),
            jax.ShapeDtypeStruct((HALF, width + LANES), BF16),
        ]
        + [jax.ShapeDtypeStruct(a.shape, a.dtype) for a in passed],
        in_specs=[pl.BlockSpec(memory_space=pltpu.SMEM)] + [IN_HBM] * 9,
        out_specs=[IN_VMEM] * 9,
        scratch_shapes=[pltpu.VMEM(a.shape, a.dtype) for a in small]
        + [
            pltpu.VMEM((LANES, tokens), F32),
            pltpu.VMEM((tokens, width), F32),
            pltpu.SemaphoreType.DMA((8,)),
            pltpu.SemaphoreType.DMA((width // column_block(width),)),
        ],
        compiler_params=pltpu.CompilerParams(vmem_limit_bytes=16 * MIB),
        cost_estimate=pl.CostEstimate(
            flops=4 * tokens * width * STATE, bytes_accessed=tokens * width * 2, transcendentals=0
        ),
    )(stretch_band, *in_hbm(*small, *passed))


def prepare_local(
    running_ref, write_ref, read_ref, decay_ref, got_ref, scores_ref, running_pieces_ref, decay_pieces_ref, lanes_ref, rows_ref
):
    width = lanes_ref.shape[1]
    scores = lax.dot_general(
        read_ref[...], write_ref[...], (((1,), (1,)), ((), ())), preferred_element_type=F32
    )
    row = lax.broadcasted_iota(jnp.int32, scores.shape, 0)
    lane = lax.broadcasted_iota(jnp.int32, scores.shape, 1)
    scores_ref[...] = jnp.where(row >= lane, scores, 0.0)
    running = running_ref[...]
    running_pieces_ref[...] = piece_rows(running, rows_ref).T.astype(BF16)
    decay_pieces_ref[...] = piece_rows(jnp.exp(running), rows_ref).T.astype(BF16)
    mine, got = decay_ref[...].astype(F32), got_ref[:16, width:].astype(F32)
    first_core = jnp.where(lax.axis_index("band") == 0, mine, got).astype(BF16)
    lanes_ref[...] = jnp.broadcast_to(
        decay_lanes(first_core, decay_map(width // HEAD_DIM, width)), lanes_ref.shape
    )


def local_heads(
    first_block,
    running_ref,
    weight_ref,
    signal_ref,
    gate_ref,
    scores_ref,
    running_pieces_ref,
    decay_pieces_ref,
    skip_ref,
    base_ref,
    factor_ref,
):
    heads, tokens = running_ref.shape
    block = column_block(signal_ref.shape[1])
    half = tokens // 2
    low_lanes = lax.broadcasted_iota(jnp.int32, (half, LANES), 1) < HEAD_DIM
    early, late = slice(0, half), slice(half, tokens)

    wide_away, away = piece_away(heads, 2 * block, 7), piece_away(heads, block, 6)

    def heads_block(at, _):
        first_head = (first_block + at) * (block // HEAD_DIM)

        def whole_lanes(lane, count):
            return pl.ds(pl.multiple_of((first_block + at) * block + lane, LANES), count)

        def part_lanes(lane, count):
            return pl.ds(pl.multiple_of(at * block + lane, LANES), count)

        wide = dot(running_pieces_ref[...], piece_map(wide_away, first_head))
        gate = gate_ref[:, whole_lanes(0, block)].astype(F32)
        gate = gate / (1.0 + jnp.exp(-gate))
        factor_ref[:, part_lanes(0, block)] = (
            dot(decay_pieces_ref[...], piece_map(away, first_head)) * gate
        )
        skip = spread_heads(skip_ref[...], head_of_lane(heads, block, 6, first_head))
        for pair in range(block // LANES):
            lanes = slice(pair * LANES, (pair + 1) * LANES)
            values = signal_ref[:, whole_lanes(pair * LANES, LANES)]
            top, bottom = [], []
            for k in (2 * pair, 2 * pair + 1):
                row = running_ref[pl.ds(first_head + k, 1), :]
                weight = weight_ref[pl.ds(first_head + k, 1), :]
                column = wide[:, k * LANES : (k + 1) * LANES]

                def mixing(rows, cols):
                    span = jnp.minimum(column[rows] - row[:, cols], 0.0)
                    return (jnp.exp(span) * scores_ref[rows, cols] * weight[:, cols]).astype(BF16)

                top.append(mixing(early, early))
                bottom.append(jnp.concatenate([mixing(late, early), mixing(late, late)], axis=1))
            top = dot(jnp.concatenate(top, axis=0), values[early])
            bottom = dot(jnp.concatenate(bottom, axis=0), values)
            skipped = values.astype(F32) * skip[:, lanes]
            out_lanes = part_lanes(pair * LANES, LANES)
            base_ref[early, out_lanes] = (
                jnp.where(low_lanes, top[:half], top[half:]) + skipped[early]
            ) * gate[early, lanes]
            base_ref[late, out_lanes] = (
                jnp.where(low_lanes, bottom[:half], bottom[half:]) + skipped[late]
            ) * gate[late, lanes]
        return 0

    lax.fori_loop(0, base_ref.shape[1] // block, heads_block, 0)


def local_first_kernel(
    chips,
    running_ref,
    weight_ref,
    signal_ref,
    gate_ref,
    write_ref,
    read_ref,
    decay_ref,
    got_ref,
    state_ref,
    skip_hbm,
    gain_hbm,
    matrix_hbm,
    after_ref,
    base_ref,
    factor_ref,
    matrix_ref,
    second_ref,
    halves_ref,
    gain_ref,
    scores_ref,
    running_pieces_ref,
    decay_pieces_ref,
    skip_ref,
    lanes_ref,
    rows_ref,
    sems,
):
    rows = matrix_ref.shape[0]
    pairs = (
        (skip_hbm, skip_ref),
        (gain_hbm, gain_ref),
        (matrix_hbm.at[pl.ds(0, rows), :], matrix_ref),
    )
    copies = [pltpu.make_async_copy(*pair, sems.at[i]) for i, pair in enumerate(pairs)]
    for copy in copies:
        copy.start()
    read = read_ref[...].astype(F32)
    swapped = jnp.concatenate([read[:, HALF:], read[:, :HALF]], axis=1)
    read = jnp.where(lax.axis_index("band") == 0, read, swapped)
    if chips == 4:
        late = HALF + PART
        turned = jnp.concatenate([read[:, :HALF], read[:, late:], read[:, HALF:late]], axis=1)
        read = jnp.where(lax.axis_index("scan") == 2, turned, read)
    halves_ref[...] = read.astype(BF16)
    upper = lax.axis_index("scan") == 2
    second_ref[...] = state_ref[pl.ds(pl.multiple_of(jnp.where(upper, 0, PART), PART), PART), :]
    prepared = (scores_ref, running_pieces_ref, decay_pieces_ref)
    prepare_local(running_ref, write_ref, read_ref, decay_ref, got_ref, *prepared, lanes_ref, rows_ref)
    copies[0].wait()
    local_heads(
        0, running_ref, weight_ref, signal_ref, gate_ref, *prepared, skip_ref, base_ref, factor_ref
    )
    for copy in copies[1:]:
        copy.wait()


def local_rest_kernel(
    first_block,
    first_row,
    running_ref,
    weight_ref,
    signal_ref,
    gate_ref,
    scores_ref,
    running_pieces_ref,
    decay_pieces_ref,
    skip_ref,
    matrix_hbm,
    after_ref,
    base_ref,
    factor_ref,
    matrix_ref,
    sem,
):
    rows = matrix_ref.shape[0]
    copy = pltpu.make_async_copy(matrix_hbm.at[pl.ds(first_row, rows), :], matrix_ref, sem)
    copy.start()
    local_heads(
        first_block,
        running_ref,
        weight_ref,
        signal_ref,
        gate_ref,
        scores_ref,
        running_pieces_ref,
        decay_pieces_ref,
        skip_ref,
        base_ref,
        factor_ref,
    )
    copy.wait()


def local_shares(width):
    if width % (10 * LANES):
        return (width // column_block(width), 0, 0), (width, 0, 0)
    tenth = width // 10
    return (1, 2, 2), (tenth, 4 * tenth, 5 * tenth)


def local_call_of(kernel, name, part, outs, resident, passed, after, scratch):
    tokens, width = resident[2].shape
    matrix = passed[-1]
    blocks, rows = local_shares(width)
    columns = blocks[part] * column_block(width)
    return pl.pallas_call(
        kernel,
        name=name,
        out_shape=[jax.ShapeDtypeStruct((tokens, columns), F32)] * 2
        + [jax.ShapeDtypeStruct((rows[part], matrix.shape[1]), BF16)]
        + outs,
        in_specs=[IN_VMEM] * len(resident) + [IN_HBM] * len(passed) + [ANYWHERE],
        out_specs=[IN_VMEM] * (3 + len(outs)),
        scratch_shapes=scratch,
        compiler_params=pltpu.CompilerParams(vmem_limit_bytes=16 * MIB),
        cost_estimate=pl.CostEstimate(
            flops=6 * columns * tokens * tokens,
            bytes_accessed=tokens * columns * 12,
            transcendentals=columns // HEAD_DIM * tokens * tokens,
        ),
    )(*resident, *in_hbm(*passed), after)


def local_first(chips, values, state, constants, after):
    running, signal = values[0], values[2]
    skip_gain, norm_gain, _ = constants
    tokens, width = signal.shape
    pieces_shape = jax.ShapeDtypeStruct((tokens, LANES), BF16)
    return local_call_of(
        functools.partial(local_first_kernel, chips),
        "local_first",
        0,
        [
            jax.ShapeDtypeStruct((PART, state.shape[1]), BF16),
            jax.ShapeDtypeStruct((tokens, STATE), BF16),
            jax.ShapeDtypeStruct(norm_gain.shape, F32),
            jax.ShapeDtypeStruct((tokens, tokens), F32),
            pieces_shape,
            pieces_shape,
            jax.ShapeDtypeStruct(skip_gain.shape, F32),
            jax.ShapeDtypeStruct((8, width), F32),
        ],
        (*values, state),
        constants,
        after,
        [pltpu.VMEM((LANES, tokens), F32), pltpu.SemaphoreType.DMA((3,))],
    )


def local_rest(part, values, prepared, out_weight, after):
    blocks, rows = local_shares(values[2].shape[1])
    return local_call_of(
        functools.partial(local_rest_kernel, sum(blocks[:part]), sum(rows[:part])),
        "local_rest",
        part,
        [],
        (*values, *prepared),
        (out_weight,),
        after,
        [pltpu.SemaphoreType.DMA(())],
    )


def chip_kernel(keep_ref, got_ref, decay_ref, state_ref, first_ref):
    width = keep_ref.shape[1]
    core = lax.axis_index("band")
    chip = lax.axis_index("scan")
    heads_map = decay_map(width // HEAD_DIM, width)
    got_decay = got_ref[:16, width:]
    mine = decay_ref[...]
    later = jnp.where(core == 0, got_decay.astype(F32), mine.astype(F32)).astype(BF16)
    lanes = decay_lanes(later, heads_map)
    got = got_ref[:, :width].astype(F32)
    keep = keep_ref[...]
    early, late = jnp.where(core == 0, keep, got), jnp.where(core == 0, got, keep)
    state_ref[:, :width] = (early * lanes + late).astype(BF16)
    block = decay_block(decay_row(got_decay) * decay_row(mine), PART)
    state_ref[:PART, width:] = block
    state_ref[PART:, width:] = block

    lower = jnp.where(chip == 1, PART, 0)
    first_ref[...] = state_ref[pl.ds(pl.multiple_of(lower, PART), PART), :]


def early_kernel(state_ref, near_ref, out_ref):
    width = out_ref.shape[1]
    chip = lax.axis_index("scan")

    @pl.when(chip == 0)
    def _():
        out_ref[...] = state_ref[PART:, :width]

    @pl.when(chip == 1)
    def _():
        lanes = decay_lanes(state_ref[:16, width:], decay_map(width // HEAD_DIM, width))
        out_ref[...] = (
            lanes * near_ref[:, :width].astype(F32) + state_ref[:PART, :width].astype(F32)
        ).astype(BF16)


def middle_kernel(state_ref, near_ref, far_ref, out_ref, lanes_ref):
    width = out_ref.shape[1]
    chip = lax.axis_index("scan")

    @pl.when(chip == 2)
    def _():
        heads_map = decay_map(width // HEAD_DIM, width)
        lanes = decay_lanes(near_ref[:16, width:], heads_map)
        lanes_ref[...] = jnp.broadcast_to(lanes, lanes_ref.shape)
        entered = lanes * far_ref[:, :width].astype(F32) + near_ref[:, :width].astype(F32)
        own = decay_lanes(state_ref[:16, width:], heads_map)
        out_ref[...] = (own * entered + state_ref[PART:, :width].astype(F32)).astype(BF16)

    @pl.when(chip == 3)
    def _():
        lanes = decay_lanes(far_ref[:16, width:], decay_map(width // HEAD_DIM, width))
        lanes_ref[...] = jnp.broadcast_to(lanes, lanes_ref.shape)


def enter_first_kernel(
    near_ref, far_ref, early_ref, far_lanes_ref, keep_ref, got_ref, lanes_ref, mine_ref, send_ref
):
    width = keep_ref.shape[1]
    chip = lax.axis_index("scan")
    near, far = (ref.at[:, pl.ds(0, width)] for ref in (near_ref, far_ref))
    refs = (keep_ref, got_ref, lanes_ref, mine_ref, send_ref)

    @pl.when(chip == 0)
    def _():
        share_enter(jnp.zeros((PART, width), F32), 0, 0, *refs)

    @pl.when(chip == 1)
    def _():
        share_enter(near[...].astype(F32), 0, 0, *refs)

    @pl.when(chip == 2)
    def _():
        enter = far_lanes_ref[:1] * far[...].astype(F32) + near[...].astype(F32)
        share_enter(enter, PART, 0, *refs)

    @pl.when(chip == 3)
    def _():
        enter = far_lanes_ref[:1] * early_ref[...].astype(F32) + far[...].astype(F32)
        share_enter(enter, 0, 0, *refs)


def enter_rest_kernel(
    early_ref, next_ref, last_ref, keep_ref, got_ref, lanes_ref, old_ref, mine_ref, send_ref
):
    width = keep_ref.shape[1]
    chip = lax.axis_index("scan")
    refs = (keep_ref, got_ref, lanes_ref, mine_ref, send_ref)

    @pl.when(chip == 0)
    def _():
        share_enter(jnp.zeros((PART, width), F32), PART, 0, *refs)

    @pl.when(chip == 1)
    def _():
        share_enter(early_ref[...].astype(F32), PART, 0, *refs)

    @pl.when(chip == 2)
    def _():
        share_enter(next_ref[...].astype(F32), 0, 0, *refs)

    @pl.when(chip == 3)
    def _():
        share_enter(last_ref[...].astype(F32), PART, 0, *refs)


def share_enter(enter, first, place, keep_ref, got_ref, lanes_ref, mine_ref, send_ref):
    width = keep_ref.shape[1]
    core = lax.axis_index("band")
    rows = slice(first, first + enter.shape[0])
    sent = slice(place, place + enter.shape[0])

    @pl.when(core == 0)
    def _():
        mine_ref[rows, :] = enter.astype(BF16)
        send_ref[sent, :] = (lanes_ref[:1] * enter + keep_ref[rows, :]).astype(BF16)

    @pl.when(core == 1)
    def _():
        send_ref[sent, :] = enter.astype(BF16)
        mine_ref[rows, :] = (lanes_ref[:1] * enter + got_ref[rows, :width].astype(F32)).astype(BF16)


def gathered_kernel(all_ref, keep_ref, got_ref, lanes_ref, mine_ref, send_ref, enter_ref):
    width = keep_ref.shape[1]
    chip = lax.axis_index("scan")
    heads_map = decay_map(width // HEAD_DIM, width)
    enter_ref[...] = jnp.zeros(enter_ref.shape, F32)
    for source in range(all_ref.shape[0]):

        @pl.when(source < chip)
        def _():
            lanes = decay_lanes(all_ref[source, :16, width:], heads_map)
            enter_ref[...] = lanes * enter_ref[...] + all_ref[source, :, :width].astype(F32)

    share_enter(enter_ref[...], 0, 0, keep_ref, got_ref, lanes_ref, mine_ref, send_ref)


def chip_state(keep, got, decay):
    width = keep.shape[1]
    return local_call(
        chip_kernel,
        "chip_state",
        [
            jax.ShapeDtypeStruct((HALF, width + LANES), BF16),
            jax.ShapeDtypeStruct((PART, width + LANES), BF16),
        ],
        (keep, got, decay),
    )


def entering_state(chips, state, first, keep, got, local):
    width = keep.shape[1]
    half = jax.ShapeDtypeStruct((HALF, width), BF16)
    part = jax.ShapeDtypeStruct((PART, width), BF16)
    cores = [(0, 1), (1, 0)]
    if chips != 4:
        gathered = lax.all_gather(state, "scan", axis=0)
        second, lanes = local(0, first)
        local(1, second)
        local(2, second)
        mine, give = local_call(
            gathered_kernel,
            "enter_state",
            [half, half],
            (gathered, keep, got, lanes),
            (pltpu.VMEM((HALF, width), F32),),
        )
        return mine, lax.ppermute(give, "band", cores)
    near = lax.ppermute(first, "scan", [(0, 1), (1, 2)])
    second, lanes = local(0, first)
    far = lax.ppermute(second, "scan", [(0, 2), (2, 3)])
    done = local(1, second)
    (ahead,) = local_call(
        early_kernel,
        "early_state",
        [jax.ShapeDtypeStruct((PART, width), BF16)],
        (state, near),
        after=(done,),
    )
    early = lax.ppermute(ahead, "scan", [(1, 3), (0, 1)])
    following = lax.ppermute(ahead, "scan", [(1, 2)])
    middle, far_lanes = local_call(
        middle_kernel,
        "middle_state",
        [jax.ShapeDtypeStruct((PART, width), BF16), jax.ShapeDtypeStruct((8, width), F32)],
        (state, near, far),
        after=(ahead,),
    )
    last = lax.ppermute(middle, "scan", [(2, 3)])
    done = local(2, middle)
    mine, give = local_call(
        enter_first_kernel,
        "enter_first",
        [half, part],
        (near, far, early, far_lanes, keep, got, lanes),
        after=(done,),
    )
    other = lax.ppermute(give, "band", cores)
    mine, give = local_call(
        enter_rest_kernel,
        "enter_rest",
        [half, part],
        (early, following, last, keep, got, lanes, mine),
        after=(other,),
        aliases={6: 0},
    )
    return mine, other, lax.ppermute(give, "band", cores)


def gated_kernel(states, parts, *refs):
    state_refs, (read_ref, gain_ref, *refs) = refs[:states], refs[states:]
    bases, factors, weights = refs[:parts], refs[parts : 2 * parts], refs[2 * parts : 3 * parts]
    out_ref, square_ref, *first_refs = refs[3 * parts :]
    tokens, width = out_ref.shape
    block = column_block(width)
    read = read_ref[...]
    sums = jnp.zeros((tokens, LANES), F32)
    first = 0
    for base_ref, factor_ref in zip(bases, factors):
        for start in range(0, base_ref.shape[1], block):
            lanes = slice(first, first + block)
            carried = dot(read, jnp.concatenate([ref[:, lanes] for ref in state_refs], axis=0))
            lanes = slice(start, start + block)
            gated = base_ref[:, lanes] + factor_ref[:, lanes] * carried
            for k in range(0, block, LANES):
                column = gated[:, k : k + LANES]
                row = (first + k) // LANES
                out_ref[:, first + k : first + k + LANES] = (
                    column * gain_ref[row : row + 1, :]
                ).astype(BF16)
                sums += column * column
            first += block
    for first_ref in first_refs:
        send_kernel(0, out_ref, *weights, first_ref)
    squares = jnp.sum(sums.T, axis=0, keepdims=True)
    for row in range(tokens // LANES):
        square_ref[row : row + 1, :] = squares[:, row * LANES : (row + 1) * LANES]


def gated_part(states, read_proj, gain, bases, factors, weights, first):
    tokens = read_proj.shape[0]
    width = states[0].shape[1]
    return local_call(
        functools.partial(gated_kernel, len(states), len(bases)),
        "gated_part",
        [
            jax.ShapeDtypeStruct((tokens, width), BF16),
            jax.ShapeDtypeStruct((tokens // LANES, LANES), F32),
        ]
        + [jax.ShapeDtypeStruct((tokens, first), BF16)] * (first > 0),
        (*states, read_proj, gain, *bases, *factors, *weights),
        flops=2 * tokens * width * STATE,
    )


SENDS = (256, 384, 384, 256)
FINISH_FLOPS = 2 * 10**9


def project(gated_ref, weights, other, first, count):
    columns = weights[0].shape[1] // 2
    member = lax.axis_index("tensor")
    start = (1 - member if other else member) * columns + first
    lanes = pl.ds(pl.multiple_of(start, LANES), count)
    row, total = 0, None
    for weight_ref in weights:
        rows = weight_ref.shape[0]
        term = dot(gated_ref[:, row : row + rows], weight_ref[:, lanes])
        row, total = row + rows, term if total is None else total + term
    return total


def send_kernel(first, gated_ref, *refs):
    *weights, out_ref = refs
    count = out_ref.shape[1]
    out_ref[...] = project(gated_ref, weights, True, first, count).astype(BF16)


def own_kernel(gated_ref, *refs):
    *weights, out_ref = refs
    count = out_ref.shape[1] // 5
    for first in range(0, out_ref.shape[1], count):
        out_ref[:, first : first + count] = project(gated_ref, weights, False, first, count)


def finish_kernel(first, squares_ref, other_squares_ref, own_ref, got_ref, *refs):
    out_ref, sent_ref, sem = refs[-3:]
    tokens, count = got_ref.shape
    mean = (squares_ref[...] + other_squares_ref[...]) / INNER
    scale = lax.rsqrt(mean + EPSILON)
    scale = jnp.concatenate(
        [jnp.broadcast_to(scale[k : k + 1], (LANES, LANES)).T for k in range(tokens // LANES)], axis=0
    )
    for lane in range(0, count, LANES):
        lanes = slice(lane, lane + LANES)
        total = own_ref[:, first + lane : first + lane + LANES] + got_ref[:, lanes].astype(F32)
        sent_ref[:, lanes] = (total * scale).astype(BF16)
    copy = pltpu.make_async_copy(sent_ref, out_ref.at[:, pl.ds(first, count)], sem)
    copy.start()
    copy.wait()


def finish(squares, other_squares, own, got):
    result, first = [], 0
    for part in got:
        args = (squares, other_squares, own, part)
        result = [
            pl.pallas_call(
                functools.partial(finish_kernel, first),
                name="finish",
                out_shape=jax.ShapeDtypeStruct(own.shape, BF16),
                in_specs=[IN_VMEM] * len(args) + [IN_HBM] * len(result),
                out_specs=IN_HBM,
                input_output_aliases={len(args): 0} if result else {},
                scratch_shapes=[pltpu.VMEM(part.shape, BF16), pltpu.SemaphoreType.DMA(())],
                compiler_params=pltpu.CompilerParams(vmem_limit_bytes=8 * MIB),
                cost_estimate=pl.CostEstimate(flops=FINISH_FLOPS, bytes_accessed=0, transcendentals=0),
            )(*args, *result)
        ]
        first += part.shape[1]
    return result[0]


def direct(members, columns):
    return members == 2 and columns == sum(SENDS)


def layer_columns(members, gated, squares, weights, ready):
    columns = weights[0].shape[1] // members
    if not direct(members, columns):
        mean = lax.psum(squares.reshape(-1), "tensor") / INNER
        partial = dot(gated, jnp.concatenate(weights, axis=0)).astype(BF16)
        total = lax.psum_scatter(partial, "tensor", scatter_dimension=1, tiled=True)
        return (total.astype(F32) * lax.rsqrt(mean + EPSILON)[:, None]).astype(BF16)
    swap = [(0, 1), (1, 0)]
    tokens = gated.shape[0]
    parts, first = [ready[0]], SENDS[0]
    for count in SENDS[1:]:
        parts += local_call(
            functools.partial(send_kernel, first),
            "project_other",
            [jax.ShapeDtypeStruct((tokens, count), BF16)],
            (gated, *weights),
            after=parts[-1:],
        )
        first += count
    got = [lax.ppermute(part, "tensor", swap) for part in parts]
    other_squares = lax.ppermute(squares, "tensor", swap)
    (own,) = local_call(
        own_kernel,
        "project_own",
        [jax.ShapeDtypeStruct((tokens, columns), F32)],
        (gated, *weights),
        after=parts[-1:],
    )
    return finish(squares, other_squares, own, got)


def on_device(
    chips,
    members,
    signal,
    gate_branch,
    write_proj,
    read_proj,
    step_logits,
    valid_mask,
    stretch_band,
    band_offset,
    decay_log,
    step_offset,
    skip_gain,
    norm_gain,
    out_weight,
):
    small = (step_logits, valid_mask[None], band_offset, decay_log[None], step_offset[None])
    running, weight, decay, keep, send, *passed = own_state(
        stretch_band, small, write_proj, read_proj, signal, gate_branch
    )
    cores = [(0, 1), (1, 0)]
    got = lax.ppermute(send, "band", cores)
    state, first = chip_state(keep, got, decay)
    constants = (skip_gain[None], norm_gain.reshape(-1, LANES), out_weight)
    write, read, *streams = passed
    values = (running, weight, *streams)
    bases, factors, weights, prepared, halves, gains = [], [], [], [], [], []

    def local(part, after):
        if not local_shares(signal.shape[1])[0][part]:
            return after
        if part:
            base, factor, matrix = local_rest(part, values, prepared, out_weight, after)
        else:
            base, factor, matrix, second, *kept, lanes = local_first(
                chips, (*values, write, read, decay, got), state, constants, after
            )
            halves.append(kept[0])
            gains.append(kept[1])
            prepared.extend(kept[2:])
        bases.append(base)
        factors.append(factor)
        weights.append(matrix)
        return base if part else (second, lanes)

    states = entering_state(chips, state, first, keep, got, local)
    ahead = SENDS[0] if direct(members, out_weight.shape[1] // members) else 0
    gated, squares, *ready = gated_part(
        states, halves[0], gains[0], bases, factors, weights, ahead
    )
    return layer_columns(members, gated, squares, weights, ready)


def solution(mesh):
    placed = (
        P(("group", "scan", "band"), "tensor"),
        P(("group", "scan", "band"), "tensor"),
        P(("group", "scan", "band"), None),
        P(("group", "scan", "band"), None),
        P("tensor", ("group", "scan", "band")),
        P(("group", "scan", "band")),
        P(("group", "scan", "band")),
        P(None, "tensor"),
        P("tensor"),
        P("tensor"),
        P("tensor"),
        P("tensor"),
        P("tensor", None),
    )
    return jax.shard_map(
        functools.partial(on_device, mesh.shape["scan"], mesh.shape["tensor"]),
        mesh=mesh,
        in_specs=placed,
        out_specs=P(("group", "scan", "band"), "tensor"),
        check_vma=False,
    )
```

```python
import functools

import jax
import jax.numpy as jnp
from jax import lax
from jax.experimental import pallas as pl
from jax.experimental.pallas import tpu as pltpu
from jax.sharding import PartitionSpec as P

HEAD_DIM = 64
STATE = 128
HALF = STATE // 2
PART = HALF // 2
STRETCH = 256
BANDS = 12
INNER = 5120
LANES = 128

EPSILON = 1e-05
HIGHEST = lax.Precision.HIGHEST
F32 = jnp.float32
BF16 = jnp.bfloat16
MIB = 1 << 20


def dot(a, b):
    return lax.dot_general(a, b, (((1,), (0,)), ((), ())), preferred_element_type=F32)


def pieces(x):
    high = x.astype(BF16)
    rest = x - high.astype(F32)
    middle = rest.astype(BF16)
    return high, middle, (rest - middle.astype(F32)).astype(BF16)


def head_of_lane(heads, lanes, group, first=0):
    row = lax.broadcasted_iota(jnp.int32, (heads, lanes), 0)
    lane = lax.broadcasted_iota(jnp.int32, (heads, lanes), 1)
    return (row == first + lax.shift_right_logical(lane, group)).astype(F32).astype(BF16)


def slot_of(heads):
    return -(-heads // 8) * 8


def piece_rows(values, ref):
    heads = values.shape[0]
    ref[...] = jnp.zeros(ref.shape, F32)
    for k, piece in enumerate(pieces(values)):
        first = k * slot_of(heads)
        ref[first : first + heads, :] = piece.astype(F32)
    return ref[...]


def piece_away(heads, lanes, group):
    slot = slot_of(heads)
    row = lax.broadcasted_iota(jnp.int32, (LANES, lanes), 0)
    head = row - jnp.where(row >= 2 * slot, 2 * slot, jnp.where(row >= slot, slot, 0))
    head = jnp.where(row < 3 * slot, head, -LANES)
    return head - lax.shift_right_logical(lax.broadcasted_iota(jnp.int32, (LANES, lanes), 1), group)


def piece_map(away, first):
    return jnp.where(away == first, 1.0, 0.0).astype(BF16)


def spread_heads(row, heads_map):
    return sum(dot(piece, heads_map) for piece in pieces(jnp.broadcast_to(row, (8, row.shape[1]))))[:1]


def diagonal(rows, lanes):
    return lax.broadcasted_iota(jnp.int32, (rows, lanes), 0) == lax.broadcasted_iota(
        jnp.int32, (rows, lanes), 1
    )


def to_column(row):
    count = row.shape[1]
    return jnp.sum(jnp.where(diagonal(count, count), row, 0.0), axis=1, keepdims=True)


def decay_block(row, rows):
    place = lax.broadcasted_iota(jnp.int32, (rows, LANES), 0)
    high, middle, low = (piece.astype(F32) for piece in pieces(row))
    block = jnp.where(place == 0, high, jnp.where(place == 1, middle, jnp.where(place == 2, low, 0.0)))
    return block.astype(BF16)


def decay_row(block):
    return jnp.sum(block.astype(F32), axis=0, keepdims=True)


def decay_map(heads, width):
    return head_of_lane(-(-heads // 16) * 16, width, 6)


def decay_lanes(block, heads_map):
    return jnp.sum(dot(block[:16, : heads_map.shape[0]], heads_map), axis=0, keepdims=True)


def column_block(width):
    return width // 5 if width % (5 * LANES) == 0 else width


def local_call(body, name, outs, args, scratch=(), limit=8 * MIB, flops=0, after=(), aliases=None):
    size = sum(a.size * a.dtype.itemsize for a in args) + sum(o.size * o.dtype.itemsize for o in outs)

    def kernel(*refs):
        body(*refs[: len(args)], *refs[len(args) + len(after) :])

    return pl.pallas_call(
        kernel,
        name=name,
        out_shape=outs,
        in_specs=[pl.BlockSpec(memory_space=pltpu.VMEM)] * len(args)
        + [pl.BlockSpec(memory_space=pl.ANY)] * len(after),
        out_specs=[pl.BlockSpec(memory_space=pltpu.VMEM)] * len(outs),
        scratch_shapes=list(scratch),
        input_output_aliases=aliases or {},
        compiler_params=pltpu.CompilerParams(vmem_limit_bytes=limit),
        cost_estimate=pl.CostEstimate(flops=flops, bytes_accessed=size, transcendentals=0),
    )(*args, *after)


IN_VMEM = pl.BlockSpec(memory_space=pltpu.VMEM)
IN_HBM = pl.BlockSpec(memory_space=pltpu.HBM)
ANYWHERE = pl.BlockSpec(memory_space=pl.ANY)


def in_hbm(*arrays):
    return [pltpu.with_memory_space_constraint(a, pltpu.HBM) for a in arrays]


def state_kernel(
    band_ref,
    logits_hbm,
    mask_hbm,
    offset_hbm,
    decay_log_hbm,
    step_offset_hbm,
    write_hbm,
    read_hbm,
    signal_hbm,
    gate_hbm,
    running_ref,
    weight_ref,
    decay_ref,
    keep_ref,
    send_ref,
    write_ref,
    read_ref,
    signal_ref,
    gate_ref,
    logits_ref,
    mask_ref,
    offset_ref,
    decay_log_ref,
    step_offset_ref,
    rows_ref,
    factors_ref,
    sems,
    block_sems,
):
    heads, tokens = logits_ref.shape
    width = signal_ref.shape[1]
    block = column_block(width)
    is_first = lax.axis_index("band") == 0
    pairs = (
        (logits_hbm, logits_ref),
        (mask_hbm, mask_ref),
        (offset_hbm, offset_ref),
        (decay_log_hbm, decay_log_ref),
        (step_offset_hbm, step_offset_ref),
        (write_hbm, write_ref),
        (read_hbm, read_ref),
        (gate_hbm, gate_ref),
    )
    copies = [pltpu.make_async_copy(*pair, sems.at[i]) for i, pair in enumerate(pairs)]
    blocks = [
        pltpu.make_async_copy(
            signal_hbm.at[:, pl.ds(first, block)],
            signal_ref.at[:, pl.ds(first, block)],
            block_sems.at[first // block],
        )
        for first in range(0, width, block)
    ]
    for copy in copies[:6] + blocks + copies[6:]:
        copy.start()
    for copy in copies[:6]:
        copy.wait()

    offset = to_column(step_offset_ref[...] + offset_ref[pl.ds(band_ref[0], 1), :])
    raw = logits_ref[...] + offset
    step_size = jnp.maximum(raw, 0.0) + jnp.log1p(jnp.exp(-jnp.abs(raw)))
    log_decay = step_size * to_column(-jnp.exp(decay_log_ref[...]))
    earlier = lax.broadcasted_iota(jnp.int32, (tokens, tokens), 0)
    later = lax.broadcasted_iota(jnp.int32, (tokens, tokens), 1)
    sums = dot(
        piece_rows(log_decay, rows_ref).astype(BF16), jnp.where(earlier <= later, 1.0, 0.0).astype(BF16)
    )
    slot = slot_of(heads)
    running = sums[:heads] + sums[slot : slot + heads] + sums[2 * slot : 2 * slot + heads]
    weight = step_size * mask_ref[...].astype(F32)
    running_ref[...] = running
    weight_ref[...] = weight
    total = running[:, tokens - 1 : tokens]
    row = jnp.sum(jnp.where(diagonal(heads, LANES), jnp.exp(total), 0.0), axis=0, keepdims=True)
    send_ref[:, width:] = decay_block(row, HALF)
    decay_ref[...] = decay_block(row, 16)

    tail = piece_rows(jnp.exp(total - running) * weight, rows_ref).T.astype(BF16)
    write = write_ref[...].astype(F32).T
    low, high = write[:HALF], write[HALF:]
    write = jnp.concatenate(
        [jnp.where(is_first, low, high), jnp.where(is_first, high, low)], axis=0
    ).astype(BF16)
    away = piece_away(heads, block, 6)
    for first in range(0, width, block):
        factors_ref[:, first : first + block] = dot(tail, piece_map(away, first // HEAD_DIM))
    for copy in blocks:
        copy.wait()
    for first in range(0, width, block):
        lanes = slice(first, first + block)
        scaled = (signal_ref[:, lanes].astype(F32) * factors_ref[:, lanes]).astype(BF16)
        state = dot(write, scaled)
        keep_ref[:, lanes] = state[:HALF]
        send_ref[:, lanes] = state[HALF:].astype(BF16)
    for copy in copies[6:]:
        copy.wait()


def own_state(stretch_band, small, write_proj, read_proj, signal, gate_branch):
    tokens, width = signal.shape
    heads = small[0].shape[0]
    passed = (write_proj, read_proj, signal, gate_branch)
    return pl.pallas_call(
        state_kernel,
        name="own_state",
        out_shape=[
            jax.ShapeDtypeStruct((heads, tokens), F32),
            jax.ShapeDtypeStruct((heads, tokens), F32),
            jax.ShapeDtypeStruct((16, LANES), BF16),
            jax.ShapeDtypeStruct((HALF, width), F32),
            jax.ShapeDtypeStruct((HALF, width + LANES), BF16),
        ]
        + [jax.ShapeDtypeStruct(a.shape, a.dtype) for a in passed],
        in_specs=[pl.BlockSpec(memory_space=pltpu.SMEM)] + [IN_HBM] * 9,
        out_specs=[IN_VMEM] * 9,
        scratch_shapes=[pltpu.VMEM(a.shape, a.dtype) for a in small]
        + [
            pltpu.VMEM((LANES, tokens), F32),
            pltpu.VMEM((tokens, width), F32),
            pltpu.SemaphoreType.DMA((8,)),
            pltpu.SemaphoreType.DMA((width // column_block(width),)),
        ],
        compiler_params=pltpu.CompilerParams(vmem_limit_bytes=16 * MIB),
        cost_estimate=pl.CostEstimate(
            flops=4 * tokens * width * STATE, bytes_accessed=tokens * width * 2, transcendentals=0
        ),
    )(stretch_band, *in_hbm(*small, *passed))


def prepare_local(
    running_ref, write_ref, read_ref, decay_ref, got_ref, scores_ref, running_pieces_ref, decay_pieces_ref, lanes_ref, rows_ref
):
    width = lanes_ref.shape[1]
    scores = lax.dot_general(
        read_ref[...], write_ref[...], (((1,), (1,)), ((), ())), preferred_element_type=F32
    )
    row = lax.broadcasted_iota(jnp.int32, scores.shape, 0)
    lane = lax.broadcasted_iota(jnp.int32, scores.shape, 1)
    scores_ref[...] = jnp.where(row >= lane, scores, 0.0)
    running = running_ref[...]
    running_pieces_ref[...] = piece_rows(running, rows_ref).T.astype(BF16)
    decay_pieces_ref[...] = piece_rows(jnp.exp(running), rows_ref).T.astype(BF16)
    mine, got = decay_ref[...].astype(F32), got_ref[:16, width:].astype(F32)
    first_core = jnp.where(lax.axis_index("band") == 0, mine, got).astype(BF16)
    lanes_ref[...] = jnp.broadcast_to(
        decay_lanes(first_core, decay_map(width // HEAD_DIM, width)), lanes_ref.shape
    )


def local_heads(
    first_block,
    running_ref,
    weight_ref,
    signal_ref,
    gate_ref,
    scores_ref,
    running_pieces_ref,
    decay_pieces_ref,
    skip_ref,
    base_ref,
    factor_ref,
):
    heads, tokens = running_ref.shape
    block = column_block(signal_ref.shape[1])
    half = tokens // 2
    low_lanes = lax.broadcasted_iota(jnp.int32, (half, LANES), 1) < HEAD_DIM
    early, late = slice(0, half), slice(half, tokens)

    wide_away, away = piece_away(heads, 2 * block, 7), piece_away(heads, block, 6)

    def heads_block(at, _):
        first_head = (first_block + at) * (block // HEAD_DIM)

        def whole_lanes(lane, count):
            return pl.ds(pl.multiple_of((first_block + at) * block + lane, LANES), count)

        def part_lanes(lane, count):
            return pl.ds(pl.multiple_of(at * block + lane, LANES), count)

        wide = dot(running_pieces_ref[...], piece_map(wide_away, first_head))
        gate = gate_ref[:, whole_lanes(0, block)].astype(F32)
        gate = gate / (1.0 + jnp.exp(-gate))
        factor_ref[:, part_lanes(0, block)] = (
            dot(decay_pieces_ref[...], piece_map(away, first_head)) * gate
        )
        skip = spread_heads(skip_ref[...], head_of_lane(heads, block, 6, first_head))
        for pair in range(block // LANES):
            lanes = slice(pair * LANES, (pair + 1) * LANES)
            values = signal_ref[:, whole_lanes(pair * LANES, LANES)]
            top, bottom = [], []
            for k in (2 * pair, 2 * pair + 1):
                row = running_ref[pl.ds(first_head + k, 1), :]
                weight = weight_ref[pl.ds(first_head + k, 1), :]
                column = wide[:, k * LANES : (k + 1) * LANES]

                def mixing(rows, cols):
                    span = jnp.minimum(column[rows] - row[:, cols], 0.0)
                    return (jnp.exp(span) * scores_ref[rows, cols] * weight[:, cols]).astype(BF16)

                top.append(mixing(early, early))
                bottom.append(jnp.concatenate([mixing(late, early), mixing(late, late)], axis=1))
            top = dot(jnp.concatenate(top, axis=0), values[early])
            bottom = dot(jnp.concatenate(bottom, axis=0), values)
            skipped = values.astype(F32) * skip[:, lanes]
            out_lanes = part_lanes(pair * LANES, LANES)
            base_ref[early, out_lanes] = (
                jnp.where(low_lanes, top[:half], top[half:]) + skipped[early]
            ) * gate[early, lanes]
            base_ref[late, out_lanes] = (
                jnp.where(low_lanes, bottom[:half], bottom[half:]) + skipped[late]
            ) * gate[late, lanes]
        return 0

    lax.fori_loop(0, base_ref.shape[1] // block, heads_block, 0)


def local_first_kernel(
    chips,
    running_ref,
    weight_ref,
    signal_ref,
    gate_ref,
    write_ref,
    read_ref,
    decay_ref,
    got_ref,
    state_ref,
    skip_hbm,
    gain_hbm,
    matrix_hbm,
    after_ref,
    base_ref,
    factor_ref,
    matrix_ref,
    second_ref,
    halves_ref,
    gain_ref,
    scores_ref,
    running_pieces_ref,
    decay_pieces_ref,
    skip_ref,
    lanes_ref,
    rows_ref,
    sems,
):
    rows = matrix_ref.shape[0]
    pairs = (
        (skip_hbm, skip_ref),
        (gain_hbm, gain_ref),
        (matrix_hbm.at[pl.ds(0, rows), :], matrix_ref),
    )
    copies = [pltpu.make_async_copy(*pair, sems.at[i]) for i, pair in enumerate(pairs)]
    for copy in copies:
        copy.start()
    read = read_ref[...].astype(F32)
    swapped = jnp.concatenate([read[:, HALF:], read[:, :HALF]], axis=1)
    read = jnp.where(lax.axis_index("band") == 0, read, swapped)
    if chips == 4:
        late = HALF + PART
        turned = jnp.concatenate([read[:, :HALF], read[:, late:], read[:, HALF:late]], axis=1)
        read = jnp.where(lax.axis_index("scan") == 2, turned, read)
    halves_ref[...] = read.astype(BF16)
    upper = lax.axis_index("scan") == 2
    second_ref[...] = state_ref[pl.ds(pl.multiple_of(jnp.where(upper, 0, PART), PART), PART), :]
    prepared = (scores_ref, running_pieces_ref, decay_pieces_ref)
    prepare_local(running_ref, write_ref, read_ref, decay_ref, got_ref, *prepared, lanes_ref, rows_ref)
    copies[0].wait()
    local_heads(
        0, running_ref, weight_ref, signal_ref, gate_ref, *prepared, skip_ref, base_ref, factor_ref
    )
    for copy in copies[1:]:
        copy.wait()


def local_rest_kernel(
    first_block,
    first_row,
    running_ref,
    weight_ref,
    signal_ref,
    gate_ref,
    scores_ref,
    running_pieces_ref,
    decay_pieces_ref,
    skip_ref,
    matrix_hbm,
    after_ref,
    base_ref,
    factor_ref,
    matrix_ref,
    sem,
):
    rows = matrix_ref.shape[0]
    copy = pltpu.make_async_copy(matrix_hbm.at[pl.ds(first_row, rows), :], matrix_ref, sem)
    copy.start()
    local_heads(
        first_block,
        running_ref,
        weight_ref,
        signal_ref,
        gate_ref,
        scores_ref,
        running_pieces_ref,
        decay_pieces_ref,
        skip_ref,
        base_ref,
        factor_ref,
    )
    copy.wait()


def local_shares(width):
    if width % (10 * LANES):
        return (width // column_block(width), 0, 0), (width, 0, 0)
    tenth = width // 10
    return (1, 2, 2), (tenth, 4 * tenth, 5 * tenth)


def local_call_of(kernel, name, part, outs, resident, passed, after, scratch):
    tokens, width = resident[2].shape
    matrix = passed[-1]
    blocks, rows = local_shares(width)
    columns = blocks[part] * column_block(width)
    return pl.pallas_call(
        kernel,
        name=name,
        out_shape=[jax.ShapeDtypeStruct((tokens, columns), F32)] * 2
        + [jax.ShapeDtypeStruct((rows[part], matrix.shape[1]), BF16)]
        + outs,
        in_specs=[IN_VMEM] * len(resident) + [IN_HBM] * len(passed) + [ANYWHERE],
        out_specs=[IN_VMEM] * (3 + len(outs)),
        scratch_shapes=scratch,
        compiler_params=pltpu.CompilerParams(vmem_limit_bytes=16 * MIB),
        cost_estimate=pl.CostEstimate(
            flops=6 * columns * tokens * tokens,
            bytes_accessed=tokens * columns * 12,
            transcendentals=columns // HEAD_DIM * tokens * tokens,
        ),
    )(*resident, *in_hbm(*passed), after)


def local_first(chips, values, state, constants, after):
    running, signal = values[0], values[2]
    skip_gain, norm_gain, _ = constants
    tokens, width = signal.shape
    pieces_shape = jax.ShapeDtypeStruct((tokens, LANES), BF16)
    return local_call_of(
        functools.partial(local_first_kernel, chips),
        "local_first",
        0,
        [
            jax.ShapeDtypeStruct((PART, state.shape[1]), BF16),
            jax.ShapeDtypeStruct((tokens, STATE), BF16),
            jax.ShapeDtypeStruct(norm_gain.shape, F32),
            jax.ShapeDtypeStruct((tokens, tokens), F32),
            pieces_shape,
            pieces_shape,
            jax.ShapeDtypeStruct(skip_gain.shape, F32),
            jax.ShapeDtypeStruct((8, width), F32),
        ],
        (*values, state),
        constants,
        after,
        [pltpu.VMEM((LANES, tokens), F32), pltpu.SemaphoreType.DMA((3,))],
    )


def local_rest(part, values, prepared, out_weight, after):
    blocks, rows = local_shares(values[2].shape[1])
    return local_call_of(
        functools.partial(local_rest_kernel, sum(blocks[:part]), sum(rows[:part])),
        "local_rest",
        part,
        [],
        (*values, *prepared),
        (out_weight,),
        after,
        [pltpu.SemaphoreType.DMA(())],
    )


def chip_kernel(keep_ref, got_ref, decay_ref, state_ref, first_ref):
    width = keep_ref.shape[1]
    core = lax.axis_index("band")
    chip = lax.axis_index("scan")
    heads_map = decay_map(width // HEAD_DIM, width)
    got_decay = got_ref[:16, width:]
    mine = decay_ref[...]
    later = jnp.where(core == 0, got_decay.astype(F32), mine.astype(F32)).astype(BF16)
    lanes = decay_lanes(later, heads_map)
    got = got_ref[:, :width].astype(F32)
    keep = keep_ref[...]
    early, late = jnp.where(core == 0, keep, got), jnp.where(core == 0, got, keep)
    state_ref[:, :width] = (early * lanes + late).astype(BF16)
    block = decay_block(decay_row(got_decay) * decay_row(mine), PART)
    state_ref[:PART, width:] = block
    state_ref[PART:, width:] = block

    lower = jnp.where(chip == 1, PART, 0)
    first_ref[...] = state_ref[pl.ds(pl.multiple_of(lower, PART), PART), :]


def early_kernel(state_ref, near_ref, out_ref, lanes_ref):
    width = out_ref.shape[1]
    chip = lax.axis_index("scan")
    heads_map = decay_map(width // HEAD_DIM, width)

    @pl.when(chip == 0)
    def _():
        out_ref[...] = state_ref[PART:, :width]

    @pl.when(chip == 1)
    def _():
        lanes = decay_lanes(state_ref[:16, width:], heads_map)
        out_ref[...] = (
            lanes * near_ref[:, :width].astype(F32) + state_ref[:PART, :width].astype(F32)
        ).astype(BF16)

    @pl.when(chip == 2)
    def _():
        for first, ref in ((0, near_ref), (8, state_ref)):
            lanes = decay_lanes(ref[:16, width:], heads_map)
            lanes_ref[first : first + 8, :] = jnp.broadcast_to(lanes, (8, width))


def middle_kernel(state_ref, near_ref, far_ref, lanes_ref, out_ref, far_lanes_ref):
    width = out_ref.shape[1]
    chip = lax.axis_index("scan")

    @pl.when(chip == 3)
    def _():
        lanes = decay_lanes(far_ref[:16, width:], decay_map(width // HEAD_DIM, width))
        far_lanes_ref[...] = jnp.broadcast_to(lanes, far_lanes_ref.shape)

    @pl.when(chip == 2)
    def _():
        entered = lanes_ref[:1] * far_ref[:, :width].astype(F32) + near_ref[:, :width].astype(F32)
        out_ref[...] = (lanes_ref[8:9] * entered + state_ref[PART:, :width].astype(F32)).astype(BF16)


def enter_first_kernel(
    near_ref,
    far_ref,
    early_ref,
    near_lanes_ref,
    far_lanes_ref,
    keep_ref,
    got_ref,
    lanes_ref,
    mine_ref,
    send_ref,
):
    width = keep_ref.shape[1]
    chip = lax.axis_index("scan")
    near, far = (ref.at[:, pl.ds(0, width)] for ref in (near_ref, far_ref))
    refs = (keep_ref, got_ref, lanes_ref, mine_ref, send_ref)

    @pl.when(chip == 0)
    def _():
        share_enter(jnp.zeros((PART, width), F32), 0, 0, *refs)

    @pl.when(chip == 1)
    def _():
        share_enter(near[...].astype(F32), 0, 0, *refs)

    @pl.when(chip == 2)
    def _():
        enter = near_lanes_ref[:1] * far[...].astype(F32) + near[...].astype(F32)
        share_enter(enter, PART, 0, *refs)

    @pl.when(chip == 3)
    def _():
        enter = far_lanes_ref[:1] * early_ref[...].astype(F32) + far[...].astype(F32)
        share_enter(enter, 0, 0, *refs)


def enter_rest_kernel(
    early_ref, next_ref, last_ref, keep_ref, got_ref, lanes_ref, old_ref, mine_ref, send_ref
):
    width = keep_ref.shape[1]
    chip = lax.axis_index("scan")
    refs = (keep_ref, got_ref, lanes_ref, mine_ref, send_ref)

    @pl.when(chip == 0)
    def _():
        share_enter(jnp.zeros((PART, width), F32), PART, 0, *refs)

    @pl.when(chip == 1)
    def _():
        share_enter(early_ref[...].astype(F32), PART, 0, *refs)

    @pl.when(chip == 2)
    def _():
        share_enter(next_ref[...].astype(F32), 0, 0, *refs)

    @pl.when(chip == 3)
    def _():
        share_enter(last_ref[...].astype(F32), PART, 0, *refs)


def share_enter(enter, first, place, keep_ref, got_ref, lanes_ref, mine_ref, send_ref):
    width = keep_ref.shape[1]
    core = lax.axis_index("band")
    rows = slice(first, first + enter.shape[0])
    sent = slice(place, place + enter.shape[0])

    @pl.when(core == 0)
    def _():
        mine_ref[rows, :] = enter.astype(BF16)
        send_ref[sent, :] = (lanes_ref[:1] * enter + keep_ref[rows, :]).astype(BF16)

    @pl.when(core == 1)
    def _():
        send_ref[sent, :] = enter.astype(BF16)
        mine_ref[rows, :] = (lanes_ref[:1] * enter + got_ref[rows, :width].astype(F32)).astype(BF16)


def gathered_kernel(all_ref, keep_ref, got_ref, lanes_ref, mine_ref, send_ref, enter_ref):
    width = keep_ref.shape[1]
    chip = lax.axis_index("scan")
    heads_map = decay_map(width // HEAD_DIM, width)
    enter_ref[...] = jnp.zeros(enter_ref.shape, F32)
    for source in range(all_ref.shape[0]):

        @pl.when(source < chip)
        def _():
            lanes = decay_lanes(all_ref[source, :16, width:], heads_map)
            enter_ref[...] = lanes * enter_ref[...] + all_ref[source, :, :width].astype(F32)

    share_enter(enter_ref[...], 0, 0, keep_ref, got_ref, lanes_ref, mine_ref, send_ref)


def chip_state(keep, got, decay):
    width = keep.shape[1]
    return local_call(
        chip_kernel,
        "chip_state",
        [
            jax.ShapeDtypeStruct((HALF, width + LANES), BF16),
            jax.ShapeDtypeStruct((PART, width + LANES), BF16),
        ],
        (keep, got, decay),
    )


def entering_state(chips, state, first, keep, got, local):
    width = keep.shape[1]
    half = jax.ShapeDtypeStruct((HALF, width), BF16)
    part = jax.ShapeDtypeStruct((PART, width), BF16)
    cores = [(0, 1), (1, 0)]
    if chips != 4:
        gathered = lax.all_gather(state, "scan", axis=0)
        second, lanes = local(0, first)
        local(1, second)
        local(2, second)
        mine, give = local_call(
            gathered_kernel,
            "enter_state",
            [half, half],
            (gathered, keep, got, lanes),
            (pltpu.VMEM((HALF, width), F32),),
        )
        return mine, lax.ppermute(give, "band", cores)
    near = lax.ppermute(first, "scan", [(0, 1), (1, 2)])
    second, lanes = local(0, first)
    far = lax.ppermute(second, "scan", [(0, 2), (2, 3)])
    done = local(1, second)
    ahead, near_lanes = local_call(
        early_kernel,
        "early_state",
        [part, jax.ShapeDtypeStruct((16, width), F32)],
        (state, near),
        after=(done,),
    )
    early = lax.ppermute(ahead, "scan", [(1, 3), (0, 1)])
    following = lax.ppermute(ahead, "scan", [(1, 2)])
    middle, far_lanes = local_call(
        middle_kernel,
        "middle_state",
        [part, jax.ShapeDtypeStruct((8, width), F32)],
        (state, near, far, near_lanes),
        after=(ahead,),
    )
    last = lax.ppermute(middle, "scan", [(2, 3)])
    done = local(2, middle)
    mine, give = local_call(
        enter_first_kernel,
        "enter_first",
        [half, part],
        (near, far, early, near_lanes, far_lanes, keep, got, lanes),
        after=(done,),
    )
    other = lax.ppermute(give, "band", cores)
    mine, give = local_call(
        enter_rest_kernel,
        "enter_rest",
        [half, part],
        (early, following, last, keep, got, lanes, mine),
        after=(other,),
        aliases={6: 0},
    )
    return mine, other, lax.ppermute(give, "band", cores)


def gated_kernel(states, parts, *refs):
    state_refs, (read_ref, gain_ref, *refs) = refs[:states], refs[states:]
    bases, factors, weights = refs[:parts], refs[parts : 2 * parts], refs[2 * parts : 3 * parts]
    out_ref, square_ref, *first_refs = refs[3 * parts :]
    tokens, width = out_ref.shape
    block = column_block(width)
    read = read_ref[...]
    sums = jnp.zeros((tokens, LANES), F32)
    first = 0
    for base_ref, factor_ref in zip(bases, factors):
        for start in range(0, base_ref.shape[1], block):
            lanes = slice(first, first + block)
            carried = dot(read, jnp.concatenate([ref[:, lanes] for ref in state_refs], axis=0))
            lanes = slice(start, start + block)
            gated = base_ref[:, lanes] + factor_ref[:, lanes] * carried
            for k in range(0, block, LANES):
                column = gated[:, k : k + LANES]
                row = (first + k) // LANES
                out_ref[:, first + k : first + k + LANES] = (
                    column * gain_ref[row : row + 1, :]
                ).astype(BF16)
                sums += column * column
            first += block
    for first_ref in first_refs:
        send_kernel(0, out_ref, *weights, first_ref)
    squares = jnp.sum(sums.T, axis=0, keepdims=True)
    for row in range(tokens // LANES):
        square_ref[row : row + 1, :] = squares[:, row * LANES : (row + 1) * LANES]


def gated_part(states, read_proj, gain, bases, factors, weights, first):
    tokens = read_proj.shape[0]
    width = states[0].shape[1]
    return local_call(
        functools.partial(gated_kernel, len(states), len(bases)),
        "gated_part",
        [
            jax.ShapeDtypeStruct((tokens, width), BF16),
            jax.ShapeDtypeStruct((tokens // LANES, LANES), F32),
        ]
        + [jax.ShapeDtypeStruct((tokens, first), BF16)] * (first > 0),
        (*states, read_proj, gain, *bases, *factors, *weights),
        flops=2 * tokens * width * STATE,
    )


SENDS = (256, 384, 384, 256)
FINISH_FLOPS = 2 * 10**9


def project(gated_ref, weights, other, first, count):
    columns = weights[0].shape[1] // 2
    member = lax.axis_index("tensor")
    start = (1 - member if other else member) * columns + first
    lanes = pl.ds(pl.multiple_of(start, LANES), count)
    row, total = 0, None
    for weight_ref in weights:
        rows = weight_ref.shape[0]
        term = dot(gated_ref[:, row : row + rows], weight_ref[:, lanes])
        row, total = row + rows, term if total is None else total + term
    return total


def send_kernel(first, gated_ref, *refs):
    *weights, out_ref = refs
    count = out_ref.shape[1]
    out_ref[...] = project(gated_ref, weights, True, first, count).astype(BF16)


def own_kernel(gated_ref, *refs):
    *weights, out_ref = refs
    count = out_ref.shape[1] // 5
    for first in range(0, out_ref.shape[1], count):
        out_ref[:, first : first + count] = project(gated_ref, weights, False, first, count)


def finish_kernel(first, squares_ref, other_squares_ref, own_ref, got_ref, *refs):
    out_ref, sent_ref, sem = refs[-3:]
    tokens, count = got_ref.shape
    mean = (squares_ref[...] + other_squares_ref[...]) / INNER
    scale = lax.rsqrt(mean + EPSILON)
    scale = jnp.concatenate(
        [jnp.broadcast_to(scale[k : k + 1], (LANES, LANES)).T for k in range(tokens // LANES)], axis=0
    )
    for lane in range(0, count, LANES):
        lanes = slice(lane, lane + LANES)
        total = own_ref[:, first + lane : first + lane + LANES] + got_ref[:, lanes].astype(F32)
        sent_ref[:, lanes] = (total * scale).astype(BF16)
    copy = pltpu.make_async_copy(sent_ref, out_ref.at[:, pl.ds(first, count)], sem)
    copy.start()
    copy.wait()


def finish(squares, other_squares, own, got):
    result, first = [], 0
    for part in got:
        args = (squares, other_squares, own, part)
        result = [
            pl.pallas_call(
                functools.partial(finish_kernel, first),
                name="finish",
                out_shape=jax.ShapeDtypeStruct(own.shape, BF16),
                in_specs=[IN_VMEM] * len(args) + [IN_HBM] * len(result),
                out_specs=IN_HBM,
                input_output_aliases={len(args): 0} if result else {},
                scratch_shapes=[pltpu.VMEM(part.shape, BF16), pltpu.SemaphoreType.DMA(())],
                compiler_params=pltpu.CompilerParams(vmem_limit_bytes=8 * MIB),
                cost_estimate=pl.CostEstimate(flops=FINISH_FLOPS, bytes_accessed=0, transcendentals=0),
            )(*args, *result)
        ]
        first += part.shape[1]
    return result[0]


def direct(members, columns):
    return members == 2 and columns == sum(SENDS)


def layer_columns(members, gated, squares, weights, ready):
    columns = weights[0].shape[1] // members
    if not direct(members, columns):
        mean = lax.psum(squares.reshape(-1), "tensor") / INNER
        partial = dot(gated, jnp.concatenate(weights, axis=0)).astype(BF16)
        total = lax.psum_scatter(partial, "tensor", scatter_dimension=1, tiled=True)
        return (total.astype(F32) * lax.rsqrt(mean + EPSILON)[:, None]).astype(BF16)
    swap = [(0, 1), (1, 0)]
    tokens = gated.shape[0]
    parts, first = [ready[0]], SENDS[0]
    for count in SENDS[1:]:
        parts += local_call(
            functools.partial(send_kernel, first),
            "project_other",
            [jax.ShapeDtypeStruct((tokens, count), BF16)],
            (gated, *weights),
            after=parts[-1:],
        )
        first += count
    got = [lax.ppermute(part, "tensor", swap) for part in parts]
    other_squares = lax.ppermute(squares, "tensor", swap)
    (own,) = local_call(
        own_kernel,
        "project_own",
        [jax.ShapeDtypeStruct((tokens, columns), F32)],
        (gated, *weights),
        after=parts[-1:],
    )
    return finish(squares, other_squares, own, got)


def on_device(
    chips,
    members,
    signal,
    gate_branch,
    write_proj,
    read_proj,
    step_logits,
    valid_mask,
    stretch_band,
    band_offset,
    decay_log,
    step_offset,
    skip_gain,
    norm_gain,
    out_weight,
):
    small = (step_logits, valid_mask[None], band_offset, decay_log[None], step_offset[None])
    running, weight, decay, keep, send, *passed = own_state(
        stretch_band, small, write_proj, read_proj, signal, gate_branch
    )
    cores = [(0, 1), (1, 0)]
    got = lax.ppermute(send, "band", cores)
    state, first = chip_state(keep, got, decay)
    constants = (skip_gain[None], norm_gain.reshape(-1, LANES), out_weight)
    write, read, *streams = passed
    values = (running, weight, *streams)
    bases, factors, weights, prepared, halves, gains = [], [], [], [], [], []

    def local(part, after):
        if not local_shares(signal.shape[1])[0][part]:
            return after
        if part:
            base, factor, matrix = local_rest(part, values, prepared, out_weight, after)
        else:
            base, factor, matrix, second, *kept, lanes = local_first(
                chips, (*values, write, read, decay, got), state, constants, after
            )
            halves.append(kept[0])
            gains.append(kept[1])
            prepared.extend(kept[2:])
        bases.append(base)
        factors.append(factor)
        weights.append(matrix)
        return base if part else (second, lanes)

    states = entering_state(chips, state, first, keep, got, local)
    ahead = SENDS[0] if direct(members, out_weight.shape[1] // members) else 0
    gated, squares, *ready = gated_part(
        states, halves[0], gains[0], bases, factors, weights, ahead
    )
    return layer_columns(members, gated, squares, weights, ready)


def solution(mesh):
    placed = (
        P(("group", "scan", "band"), "tensor"),
        P(("group", "scan", "band"), "tensor"),
        P(("group", "scan", "band"), None),
        P(("group", "scan", "band"), None),
        P("tensor", ("group", "scan", "band")),
        P(("group", "scan", "band")),
        P(("group", "scan", "band")),
        P(None, "tensor"),
        P("tensor"),
        P("tensor"),
        P("tensor"),
        P("tensor"),
        P("tensor", None),
    )
    return jax.shard_map(
        functools.partial(on_device, mesh.shape["scan"], mesh.shape["tensor"]),
        mesh=mesh,
        in_specs=placed,
        out_specs=P(("group", "scan", "band"), "tensor"),
        check_vma=False,
    )
```

```python
import functools

import jax
import jax.numpy as jnp
from jax import lax
from jax.experimental import pallas as pl
from jax.experimental.pallas import tpu as pltpu
from jax.sharding import PartitionSpec as P

HEAD_DIM = 64
STATE = 128
HALF = STATE // 2
PART = HALF // 2
STRETCH = 256
BANDS = 12
INNER = 5120
LANES = 128

EPSILON = 1e-05
HIGHEST = lax.Precision.HIGHEST
F32 = jnp.float32
BF16 = jnp.bfloat16
MIB = 1 << 20


def dot(a, b):
    return lax.dot_general(a, b, (((1,), (0,)), ((), ())), preferred_element_type=F32)


def pieces(x):
    high = x.astype(BF16)
    rest = x - high.astype(F32)
    middle = rest.astype(BF16)
    return high, middle, (rest - middle.astype(F32)).astype(BF16)


def head_of_lane(heads, lanes, group, first=0):
    row = lax.broadcasted_iota(jnp.int32, (heads, lanes), 0)
    lane = lax.broadcasted_iota(jnp.int32, (heads, lanes), 1)
    return (row == first + lax.shift_right_logical(lane, group)).astype(F32).astype(BF16)


def slot_of(heads):
    return -(-heads // 8) * 8


def piece_rows(values, ref):
    heads = values.shape[0]
    ref[...] = jnp.zeros(ref.shape, F32)
    for k, piece in enumerate(pieces(values)):
        first = k * slot_of(heads)
        ref[first : first + heads, :] = piece.astype(F32)
    return ref[...]


def piece_away(heads, lanes, group):
    slot = slot_of(heads)
    row = lax.broadcasted_iota(jnp.int32, (LANES, lanes), 0)
    head = row - jnp.where(row >= 2 * slot, 2 * slot, jnp.where(row >= slot, slot, 0))
    head = jnp.where(row < 3 * slot, head, -LANES)
    return head - lax.shift_right_logical(lax.broadcasted_iota(jnp.int32, (LANES, lanes), 1), group)


def piece_map(away, first):
    return jnp.where(away == first, 1.0, 0.0).astype(BF16)


def spread_heads(row, heads_map):
    return sum(dot(piece, heads_map) for piece in pieces(jnp.broadcast_to(row, (8, row.shape[1]))))[:1]


def diagonal(rows, lanes):
    return lax.broadcasted_iota(jnp.int32, (rows, lanes), 0) == lax.broadcasted_iota(
        jnp.int32, (rows, lanes), 1
    )


def to_column(row):
    count = row.shape[1]
    return jnp.sum(jnp.where(diagonal(count, count), row, 0.0), axis=1, keepdims=True)


def decay_block(row, rows):
    place = lax.broadcasted_iota(jnp.int32, (rows, LANES), 0)
    high, middle, low = (piece.astype(F32) for piece in pieces(row))
    block = jnp.where(place == 0, high, jnp.where(place == 1, middle, jnp.where(place == 2, low, 0.0)))
    return block.astype(BF16)


def decay_row(block):
    return jnp.sum(block.astype(F32), axis=0, keepdims=True)


def decay_map(heads, width):
    return head_of_lane(-(-heads // 16) * 16, width, 6)


def decay_lanes(block, heads_map):
    return jnp.sum(dot(block[:16, : heads_map.shape[0]], heads_map), axis=0, keepdims=True)


def column_block(width):
    return width // 5 if width % (5 * LANES) == 0 else width


def local_call(body, name, outs, args, scratch=(), limit=8 * MIB, flops=0, after=(), aliases=None):
    size = sum(a.size * a.dtype.itemsize for a in args) + sum(o.size * o.dtype.itemsize for o in outs)

    def kernel(*refs):
        body(*refs[: len(args)], *refs[len(args) + len(after) :])

    return pl.pallas_call(
        kernel,
        name=name,
        out_shape=outs,
        in_specs=[pl.BlockSpec(memory_space=pltpu.VMEM)] * len(args)
        + [pl.BlockSpec(memory_space=pl.ANY)] * len(after),
        out_specs=[pl.BlockSpec(memory_space=pltpu.VMEM)] * len(outs),
        scratch_shapes=list(scratch),
        input_output_aliases=aliases or {},
        compiler_params=pltpu.CompilerParams(vmem_limit_bytes=limit),
        cost_estimate=pl.CostEstimate(flops=flops, bytes_accessed=size, transcendentals=0),
    )(*args, *after)


IN_VMEM = pl.BlockSpec(memory_space=pltpu.VMEM)
IN_HBM = pl.BlockSpec(memory_space=pltpu.HBM)
ANYWHERE = pl.BlockSpec(memory_space=pl.ANY)


def in_hbm(*arrays):
    return [pltpu.with_memory_space_constraint(a, pltpu.HBM) for a in arrays]


def state_kernel(
    band_ref,
    logits_hbm,
    mask_hbm,
    offset_hbm,
    decay_log_hbm,
    step_offset_hbm,
    write_hbm,
    read_hbm,
    signal_hbm,
    gate_hbm,
    running_ref,
    weight_ref,
    decay_ref,
    keep_ref,
    send_ref,
    write_ref,
    read_ref,
    signal_ref,
    gate_ref,
    logits_ref,
    mask_ref,
    offset_ref,
    decay_log_ref,
    step_offset_ref,
    rows_ref,
    factors_ref,
    sems,
    block_sems,
):
    heads, tokens = logits_ref.shape
    width = signal_ref.shape[1]
    block = column_block(width)
    is_first = lax.axis_index("band") == 0
    pairs = (
        (logits_hbm, logits_ref),
        (mask_hbm, mask_ref),
        (offset_hbm, offset_ref),
        (decay_log_hbm, decay_log_ref),
        (step_offset_hbm, step_offset_ref),
        (write_hbm, write_ref),
        (read_hbm, read_ref),
        (gate_hbm, gate_ref),
    )
    copies = [pltpu.make_async_copy(*pair, sems.at[i]) for i, pair in enumerate(pairs)]
    blocks = [
        pltpu.make_async_copy(
            signal_hbm.at[:, pl.ds(first, block)],
            signal_ref.at[:, pl.ds(first, block)],
            block_sems.at[first // block],
        )
        for first in range(0, width, block)
    ]
    for copy in copies[:6] + blocks + copies[6:]:
        copy.start()
    for copy in copies[:6]:
        copy.wait()

    offset = to_column(step_offset_ref[...] + offset_ref[pl.ds(band_ref[0], 1), :])
    raw = logits_ref[...] + offset
    step_size = jnp.maximum(raw, 0.0) + jnp.log1p(jnp.exp(-jnp.abs(raw)))
    log_decay = step_size * to_column(-jnp.exp(decay_log_ref[...]))
    earlier = lax.broadcasted_iota(jnp.int32, (tokens, tokens), 0)
    later = lax.broadcasted_iota(jnp.int32, (tokens, tokens), 1)
    sums = dot(
        piece_rows(log_decay, rows_ref).astype(BF16), jnp.where(earlier <= later, 1.0, 0.0).astype(BF16)
    )
    slot = slot_of(heads)
    running = sums[:heads] + sums[slot : slot + heads] + sums[2 * slot : 2 * slot + heads]
    weight = step_size * mask_ref[...].astype(F32)
    running_ref[...] = running
    weight_ref[...] = weight
    total = running[:, tokens - 1 : tokens]
    row = jnp.sum(jnp.where(diagonal(heads, LANES), jnp.exp(total), 0.0), axis=0, keepdims=True)
    send_ref[:, width:] = decay_block(row, HALF)
    decay_ref[...] = decay_block(row, 16)

    tail = piece_rows(jnp.exp(total - running) * weight, rows_ref).T.astype(BF16)
    write = write_ref[...].astype(F32).T
    low, high = write[:HALF], write[HALF:]
    write = jnp.concatenate(
        [jnp.where(is_first, low, high), jnp.where(is_first, high, low)], axis=0
    ).astype(BF16)
    away = piece_away(heads, block, 6)
    for first in range(0, width, block):
        factors_ref[:, first : first + block] = dot(tail, piece_map(away, first // HEAD_DIM))
    for copy in blocks:
        copy.wait()
    for first in range(0, width, block):
        lanes = slice(first, first + block)
        scaled = (signal_ref[:, lanes].astype(F32) * factors_ref[:, lanes]).astype(BF16)
        state = dot(write, scaled)
        keep_ref[:, lanes] = state[:HALF]
        send_ref[:, lanes] = state[HALF:].astype(BF16)
    for copy in copies[6:]:
        copy.wait()


def own_state(stretch_band, small, write_proj, read_proj, signal, gate_branch):
    tokens, width = signal.shape
    heads = small[0].shape[0]
    passed = (write_proj, read_proj, signal, gate_branch)
    return pl.pallas_call(
        state_kernel,
        name="own_state",
        out_shape=[
            jax.ShapeDtypeStruct((heads, tokens), F32),
            jax.ShapeDtypeStruct((heads, tokens), F32),
            jax.ShapeDtypeStruct((16, LANES), BF16),
            jax.ShapeDtypeStruct((HALF, width), F32),
            jax.ShapeDtypeStruct((HALF, width + LANES), BF16),
        ]
        + [jax.ShapeDtypeStruct(a.shape, a.dtype) for a in passed],
        in_specs=[pl.BlockSpec(memory_space=pltpu.SMEM)] + [IN_HBM] * 9,
        out_specs=[IN_VMEM] * 9,
        scratch_shapes=[pltpu.VMEM(a.shape, a.dtype) for a in small]
        + [
            pltpu.VMEM((LANES, tokens), F32),
            pltpu.VMEM((tokens, width), F32),
            pltpu.SemaphoreType.DMA((8,)),
            pltpu.SemaphoreType.DMA((width // column_block(width),)),
        ],
        compiler_params=pltpu.CompilerParams(vmem_limit_bytes=16 * MIB),
        cost_estimate=pl.CostEstimate(
            flops=4 * tokens * width * STATE, bytes_accessed=tokens * width * 2, transcendentals=0
        ),
    )(stretch_band, *in_hbm(*small, *passed))


def prepare_local(
    running_ref, write_ref, read_ref, decay_ref, got_ref, scores_ref, running_pieces_ref, decay_pieces_ref, lanes_ref, rows_ref
):
    width = lanes_ref.shape[1]
    scores = lax.dot_general(
        read_ref[...], write_ref[...], (((1,), (1,)), ((), ())), preferred_element_type=F32
    )
    row = lax.broadcasted_iota(jnp.int32, scores.shape, 0)
    lane = lax.broadcasted_iota(jnp.int32, scores.shape, 1)
    scores_ref[...] = jnp.where(row >= lane, scores, 0.0)
    running = running_ref[...]
    running_pieces_ref[...] = piece_rows(running, rows_ref).T.astype(BF16)
    decay_pieces_ref[...] = piece_rows(jnp.exp(running), rows_ref).T.astype(BF16)
    mine, got = decay_ref[...].astype(F32), got_ref[:16, width:].astype(F32)
    first_core = jnp.where(lax.axis_index("band") == 0, mine, got).astype(BF16)
    lanes_ref[...] = jnp.broadcast_to(
        decay_lanes(first_core, decay_map(width // HEAD_DIM, width)), lanes_ref.shape
    )


def local_heads(
    first_block,
    running_ref,
    weight_ref,
    signal_ref,
    gate_ref,
    scores_ref,
    running_pieces_ref,
    decay_pieces_ref,
    skip_ref,
    base_ref,
    factor_ref,
):
    heads, tokens = running_ref.shape
    block = column_block(signal_ref.shape[1])
    half = tokens // 2
    low_lanes = lax.broadcasted_iota(jnp.int32, (half, LANES), 1) < HEAD_DIM
    early, late = slice(0, half), slice(half, tokens)

    wide_away, away = piece_away(heads, 2 * block, 7), piece_away(heads, block, 6)

    def heads_block(at, _):
        first_head = (first_block + at) * (block // HEAD_DIM)

        def whole_lanes(lane, count):
            return pl.ds(pl.multiple_of((first_block + at) * block + lane, LANES), count)

        def part_lanes(lane, count):
            return pl.ds(pl.multiple_of(at * block + lane, LANES), count)

        wide = dot(running_pieces_ref[...], piece_map(wide_away, first_head))
        gate = gate_ref[:, whole_lanes(0, block)].astype(F32)
        gate = gate / (1.0 + jnp.exp(-gate))
        factor_ref[:, part_lanes(0, block)] = (
            dot(decay_pieces_ref[...], piece_map(away, first_head)) * gate
        )
        skip = spread_heads(skip_ref[...], head_of_lane(heads, block, 6, first_head))
        for pair in range(block // LANES):
            lanes = slice(pair * LANES, (pair + 1) * LANES)
            values = signal_ref[:, whole_lanes(pair * LANES, LANES)]
            top, bottom = [], []
            for k in (2 * pair, 2 * pair + 1):
                row = running_ref[pl.ds(first_head + k, 1), :]
                weight = weight_ref[pl.ds(first_head + k, 1), :]
                column = wide[:, k * LANES : (k + 1) * LANES]

                def mixing(rows, cols):
                    span = jnp.minimum(column[rows] - row[:, cols], 0.0)
                    return (jnp.exp(span) * scores_ref[rows, cols] * weight[:, cols]).astype(BF16)

                top.append(mixing(early, early))
                bottom.append(jnp.concatenate([mixing(late, early), mixing(late, late)], axis=1))
            top = dot(jnp.concatenate(top, axis=0), values[early])
            bottom = dot(jnp.concatenate(bottom, axis=0), values)
            skipped = values.astype(F32) * skip[:, lanes]
            out_lanes = part_lanes(pair * LANES, LANES)
            base_ref[early, out_lanes] = (
                jnp.where(low_lanes, top[:half], top[half:]) + skipped[early]
            ) * gate[early, lanes]
            base_ref[late, out_lanes] = (
                jnp.where(low_lanes, bottom[:half], bottom[half:]) + skipped[late]
            ) * gate[late, lanes]
        return 0

    lax.fori_loop(0, base_ref.shape[1] // block, heads_block, 0)


def local_first_kernel(
    chips,
    running_ref,
    weight_ref,
    signal_ref,
    gate_ref,
    write_ref,
    read_ref,
    decay_ref,
    got_ref,
    state_ref,
    skip_hbm,
    gain_hbm,
    matrix_hbm,
    after_ref,
    base_ref,
    factor_ref,
    matrix_ref,
    second_ref,
    halves_ref,
    gain_ref,
    scores_ref,
    running_pieces_ref,
    decay_pieces_ref,
    skip_ref,
    lanes_ref,
    rows_ref,
    sems,
):
    rows = matrix_ref.shape[0]
    pairs = (
        (skip_hbm, skip_ref),
        (gain_hbm, gain_ref),
        (matrix_hbm.at[pl.ds(0, rows), :], matrix_ref),
    )
    copies = [pltpu.make_async_copy(*pair, sems.at[i]) for i, pair in enumerate(pairs)]
    for copy in copies:
        copy.start()
    read = read_ref[...].astype(F32)
    swapped = jnp.concatenate([read[:, HALF:], read[:, :HALF]], axis=1)
    read = jnp.where(lax.axis_index("band") == 0, read, swapped)
    if chips == 4:
        late = HALF + PART
        turned = jnp.concatenate([read[:, :HALF], read[:, late:], read[:, HALF:late]], axis=1)
        read = jnp.where(lax.axis_index("scan") == 2, turned, read)
    halves_ref[...] = read.astype(BF16)
    upper = lax.axis_index("scan") == 2
    second_ref[...] = state_ref[pl.ds(pl.multiple_of(jnp.where(upper, 0, PART), PART), PART), :]
    prepared = (scores_ref, running_pieces_ref, decay_pieces_ref)
    prepare_local(running_ref, write_ref, read_ref, decay_ref, got_ref, *prepared, lanes_ref, rows_ref)
    copies[0].wait()
    local_heads(
        0, running_ref, weight_ref, signal_ref, gate_ref, *prepared, skip_ref, base_ref, factor_ref
    )
    for copy in copies[1:]:
        copy.wait()


def local_rest_kernel(
    first_block,
    first_row,
    running_ref,
    weight_ref,
    signal_ref,
    gate_ref,
    scores_ref,
    running_pieces_ref,
    decay_pieces_ref,
    skip_ref,
    matrix_hbm,
    after_ref,
    base_ref,
    factor_ref,
    matrix_ref,
    sem,
):
    rows = matrix_ref.shape[0]
    copy = pltpu.make_async_copy(matrix_hbm.at[pl.ds(first_row, rows), :], matrix_ref, sem)
    copy.start()
    local_heads(
        first_block,
        running_ref,
        weight_ref,
        signal_ref,
        gate_ref,
        scores_ref,
        running_pieces_ref,
        decay_pieces_ref,
        skip_ref,
        base_ref,
        factor_ref,
    )
    copy.wait()


def local_shares(width):
    if width % (10 * LANES):
        return (width // column_block(width), 0, 0), (width, 0, 0)
    tenth = width // 10
    return (1, 2, 2), (tenth, 4 * tenth, 5 * tenth)


def local_call_of(kernel, name, part, outs, resident, passed, after, scratch):
    tokens, width = resident[2].shape
    matrix = passed[-1]
    blocks, rows = local_shares(width)
    columns = blocks[part] * column_block(width)
    return pl.pallas_call(
        kernel,
        name=name,
        out_shape=[jax.ShapeDtypeStruct((tokens, columns), F32)] * 2
        + [jax.ShapeDtypeStruct((rows[part], matrix.shape[1]), BF16)]
        + outs,
        in_specs=[IN_VMEM] * len(resident) + [IN_HBM] * len(passed) + [ANYWHERE],
        out_specs=[IN_VMEM] * (3 + len(outs)),
        scratch_shapes=scratch,
        compiler_params=pltpu.CompilerParams(vmem_limit_bytes=16 * MIB),
        cost_estimate=pl.CostEstimate(
            flops=6 * columns * tokens * tokens,
            bytes_accessed=tokens * columns * 12,
            transcendentals=columns // HEAD_DIM * tokens * tokens,
        ),
    )(*resident, *in_hbm(*passed), after)


def local_first(chips, values, state, constants, after):
    running, signal = values[0], values[2]
    skip_gain, norm_gain, _ = constants
    tokens, width = signal.shape
    pieces_shape = jax.ShapeDtypeStruct((tokens, LANES), BF16)
    return local_call_of(
        functools.partial(local_first_kernel, chips),
        "local_first",
        0,
        [
            jax.ShapeDtypeStruct((PART, state.shape[1]), BF16),
            jax.ShapeDtypeStruct((tokens, STATE), BF16),
            jax.ShapeDtypeStruct(norm_gain.shape, F32),
            jax.ShapeDtypeStruct((tokens, tokens), F32),
            pieces_shape,
            pieces_shape,
            jax.ShapeDtypeStruct(skip_gain.shape, F32),
            jax.ShapeDtypeStruct((8, width), F32),
        ],
        (*values, state),
        constants,
        after,
        [pltpu.VMEM((LANES, tokens), F32), pltpu.SemaphoreType.DMA((3,))],
    )


def local_rest(part, values, prepared, out_weight, after):
    blocks, rows = local_shares(values[2].shape[1])
    return local_call_of(
        functools.partial(local_rest_kernel, sum(blocks[:part]), sum(rows[:part])),
        "local_rest",
        part,
        [],
        (*values, *prepared),
        (out_weight,),
        after,
        [pltpu.SemaphoreType.DMA(())],
    )


def chip_kernel(keep_ref, got_ref, decay_ref, state_ref, first_ref):
    width = keep_ref.shape[1]
    core = lax.axis_index("band")
    chip = lax.axis_index("scan")
    heads_map = decay_map(width // HEAD_DIM, width)
    got_decay = got_ref[:16, width:]
    mine = decay_ref[...]
    later = jnp.where(core == 0, got_decay.astype(F32), mine.astype(F32)).astype(BF16)
    lanes = decay_lanes(later, heads_map)
    got = got_ref[:, :width].astype(F32)
    keep = keep_ref[...]
    early, late = jnp.where(core == 0, keep, got), jnp.where(core == 0, got, keep)
    state_ref[:, :width] = (early * lanes + late).astype(BF16)
    block = decay_block(decay_row(got_decay) * decay_row(mine), PART)
    state_ref[:PART, width:] = block
    state_ref[PART:, width:] = block

    lower = jnp.where(chip == 1, PART, 0)
    first_ref[...] = state_ref[pl.ds(pl.multiple_of(lower, PART), PART), :]


def early_kernel(state_ref, near_ref, out_ref):
    width = out_ref.shape[1]
    chip = lax.axis_index("scan")

    @pl.when(chip == 0)
    def _():
        out_ref[...] = state_ref[PART:, :width]

    @pl.when(chip == 1)
    def _():
        lanes = decay_lanes(state_ref[:16, width:], decay_map(width // HEAD_DIM, width))
        out_ref[...] = (
            lanes * near_ref[:, :width].astype(F32) + state_ref[:PART, :width].astype(F32)
        ).astype(BF16)


def middle_kernel(state_ref, near_ref, far_ref, out_ref, lanes_ref):
    width = out_ref.shape[1]
    chip = lax.axis_index("scan")

    @pl.when(chip == 2)
    def _():
        heads_map = decay_map(width // HEAD_DIM, width)
        lanes = decay_lanes(near_ref[:16, width:], heads_map)
        lanes_ref[...] = jnp.broadcast_to(lanes, lanes_ref.shape)
        entered = lanes * far_ref[:, :width].astype(F32) + near_ref[:, :width].astype(F32)
        own = decay_lanes(state_ref[:16, width:], heads_map)
        out_ref[...] = (own * entered + state_ref[PART:, :width].astype(F32)).astype(BF16)

    @pl.when(chip == 3)
    def _():
        lanes = decay_lanes(far_ref[:16, width:], decay_map(width // HEAD_DIM, width))
        lanes_ref[...] = jnp.broadcast_to(lanes, lanes_ref.shape)


def enter_first_kernel(
    near_ref, far_ref, early_ref, far_lanes_ref, keep_ref, got_ref, lanes_ref, mine_ref, send_ref
):
    width = keep_ref.shape[1]
    chip = lax.axis_index("scan")
    near, far = (ref.at[:, pl.ds(0, width)] for ref in (near_ref, far_ref))
    refs = (keep_ref, got_ref, lanes_ref, mine_ref, send_ref)

    @pl.when(chip == 0)
    def _():
        share_enter(jnp.zeros((PART, width), F32), 0, 0, *refs)

    @pl.when(chip == 1)
    def _():
        share_enter(near[...].astype(F32), 0, 0, *refs)

    @pl.when(chip == 2)
    def _():
        enter = far_lanes_ref[:1] * far[...].astype(F32) + near[...].astype(F32)
        share_enter(enter, PART, 0, *refs)

    @pl.when(chip == 3)
    def _():
        enter = far_lanes_ref[:1] * early_ref[...].astype(F32) + far[...].astype(F32)
        share_enter(enter, 0, 0, *refs)


def enter_rest_kernel(
    early_ref, next_ref, last_ref, keep_ref, got_ref, lanes_ref, old_ref, mine_ref, send_ref
):
    width = keep_ref.shape[1]
    chip = lax.axis_index("scan")
    refs = (keep_ref, got_ref, lanes_ref, mine_ref, send_ref)

    @pl.when(chip == 0)
    def _():
        share_enter(jnp.zeros((PART, width), F32), PART, 0, *refs)

    @pl.when(chip == 1)
    def _():
        share_enter(early_ref[...].astype(F32), PART, 0, *refs)

    @pl.when(chip == 2)
    def _():
        share_enter(next_ref[...].astype(F32), 0, 0, *refs)

    @pl.when(chip == 3)
    def _():
        share_enter(last_ref[...].astype(F32), PART, 0, *refs)


def share_enter(enter, first, place, keep_ref, got_ref, lanes_ref, mine_ref, send_ref):
    width = keep_ref.shape[1]
    core = lax.axis_index("band")
    rows = slice(first, first + enter.shape[0])
    sent = slice(place, place + enter.shape[0])

    @pl.when(core == 0)
    def _():
        mine_ref[rows, :] = enter.astype(BF16)
        send_ref[sent, :] = (lanes_ref[:1] * enter + keep_ref[rows, :]).astype(BF16)

    @pl.when(core == 1)
    def _():
        send_ref[sent, :] = enter.astype(BF16)
        mine_ref[rows, :] = (lanes_ref[:1] * enter + got_ref[rows, :width].astype(F32)).astype(BF16)


def gathered_kernel(all_ref, keep_ref, got_ref, lanes_ref, mine_ref, send_ref, enter_ref):
    width = keep_ref.shape[1]
    chip = lax.axis_index("scan")
    heads_map = decay_map(width // HEAD_DIM, width)
    enter_ref[...] = jnp.zeros(enter_ref.shape, F32)
    for source in range(all_ref.shape[0]):

        @pl.when(source < chip)
        def _():
            lanes = decay_lanes(all_ref[source, :16, width:], heads_map)
            enter_ref[...] = lanes * enter_ref[...] + all_ref[source, :, :width].astype(F32)

    share_enter(enter_ref[...], 0, 0, keep_ref, got_ref, lanes_ref, mine_ref, send_ref)


def chip_state(keep, got, decay):
    width = keep.shape[1]
    return local_call(
        chip_kernel,
        "chip_state",
        [
            jax.ShapeDtypeStruct((HALF, width + LANES), BF16),
            jax.ShapeDtypeStruct((PART, width + LANES), BF16),
        ],
        (keep, got, decay),
    )


def entering_state(chips, state, first, keep, got, local):
    width = keep.shape[1]
    half = jax.ShapeDtypeStruct((HALF, width), BF16)
    part = jax.ShapeDtypeStruct((PART, width), BF16)
    cores = [(0, 1), (1, 0)]
    if chips != 4:
        gathered = lax.all_gather(state, "scan", axis=0)
        second, lanes = local(0, first)
        local(1, second)
        local(2, second)
        mine, give = local_call(
            gathered_kernel,
            "enter_state",
            [half, half],
            (gathered, keep, got, lanes),
            (pltpu.VMEM((HALF, width), F32),),
        )
        return mine, lax.ppermute(give, "band", cores)
    near = lax.ppermute(first, "scan", [(0, 1), (1, 2)])
    second, lanes = local(0, first)
    far = lax.ppermute(second, "scan", [(0, 2), (2, 3)])
    done = local(1, second)
    (ahead,) = local_call(
        early_kernel,
        "early_state",
        [jax.ShapeDtypeStruct((PART, width), BF16)],
        (state, near),
        after=(done,),
    )
    early = lax.ppermute(ahead, "scan", [(1, 3), (0, 1)])
    following = lax.ppermute(ahead, "scan", [(1, 2)])
    middle, far_lanes = local_call(
        middle_kernel,
        "middle_state",
        [jax.ShapeDtypeStruct((PART, width), BF16), jax.ShapeDtypeStruct((8, width), F32)],
        (state, near, far),
        after=(ahead,),
    )
    last = lax.ppermute(middle, "scan", [(2, 3)])
    done = local(2, middle)
    mine, give = local_call(
        enter_first_kernel,
        "enter_first",
        [half, part],
        (near, far, early, far_lanes, keep, got, lanes),
        after=(done,),
    )
    other = lax.ppermute(give, "band", cores)
    mine, give = local_call(
        enter_rest_kernel,
        "enter_rest",
        [half, part],
        (early, following, last, keep, got, lanes, mine),
        after=(other,),
        aliases={6: 0},
    )
    return mine, other, lax.ppermute(give, "band", cores)


def gated_kernel(states, parts, *refs):
    state_refs, (read_ref, gain_ref, *refs) = refs[:states], refs[states:]
    bases, factors, weights = refs[:parts], refs[parts : 2 * parts], refs[2 * parts : 3 * parts]
    out_ref, square_ref, *first_refs = refs[3 * parts :]
    tokens, width = out_ref.shape
    block = column_block(width)
    read = read_ref[...]
    sums = jnp.zeros((tokens, LANES), F32)
    first = 0
    for base_ref, factor_ref in zip(bases, factors):
        for start in range(0, base_ref.shape[1], block):
            lanes = slice(first, first + block)
            carried = dot(read, jnp.concatenate([ref[:, lanes] for ref in state_refs], axis=0))
            lanes = slice(start, start + block)
            gated = base_ref[:, lanes] + factor_ref[:, lanes] * carried
            for k in range(0, block, LANES):
                column = gated[:, k : k + LANES]
                row = (first + k) // LANES
                out_ref[:, first + k : first + k + LANES] = (
                    column * gain_ref[row : row + 1, :]
                ).astype(BF16)
                sums += column * column
            first += block
    for first_ref in first_refs:
        send_kernel(0, out_ref, *weights, first_ref)
    squares = jnp.sum(sums.T, axis=0, keepdims=True)
    for row in range(tokens // LANES):
        square_ref[row : row + 1, :] = squares[:, row * LANES : (row + 1) * LANES]


def gated_part(states, read_proj, gain, bases, factors, weights, first):
    tokens = read_proj.shape[0]
    width = states[0].shape[1]
    return local_call(
        functools.partial(gated_kernel, len(states), len(bases)),
        "gated_part",
        [
            jax.ShapeDtypeStruct((tokens, width), BF16),
            jax.ShapeDtypeStruct((tokens // LANES, LANES), F32),
        ]
        + [jax.ShapeDtypeStruct((tokens, first), BF16)] * (first > 0),
        (*states, read_proj, gain, *bases, *factors, *weights),
        flops=2 * tokens * width * STATE,
    )


SENDS = (256, 512, 384, 128)
FINISH_FLOPS = 2 * 10**9


def project(gated_ref, weights, other, first, count):
    columns = weights[0].shape[1] // 2
    member = lax.axis_index("tensor")
    start = (1 - member if other else member) * columns + first
    lanes = pl.ds(pl.multiple_of(start, LANES), count)
    row, total = 0, None
    for weight_ref in weights:
        rows = weight_ref.shape[0]
        term = dot(gated_ref[:, row : row + rows], weight_ref[:, lanes])
        row, total = row + rows, term if total is None else total + term
    return total


def send_kernel(first, gated_ref, *refs):
    *weights, out_ref = refs
    count = out_ref.shape[1]
    out_ref[...] = project(gated_ref, weights, True, first, count).astype(BF16)


def own_kernel(gated_ref, *refs):
    *weights, out_ref = refs
    count = out_ref.shape[1] // 5
    for first in range(0, out_ref.shape[1], count):
        out_ref[:, first : first + count] = project(gated_ref, weights, False, first, count)


def finish_kernel(first, squares_ref, other_squares_ref, own_ref, got_ref, *refs):
    out_ref, sent_ref, sem = refs[-3:]
    tokens, count = got_ref.shape
    mean = (squares_ref[...] + other_squares_ref[...]) / INNER
    scale = lax.rsqrt(mean + EPSILON)
    scale = jnp.concatenate(
        [jnp.broadcast_to(scale[k : k + 1], (LANES, LANES)).T for k in range(tokens // LANES)], axis=0
    )
    for lane in range(0, count, LANES):
        lanes = slice(lane, lane + LANES)
        total = own_ref[:, first + lane : first + lane + LANES] + got_ref[:, lanes].astype(F32)
        sent_ref[:, lanes] = (total * scale).astype(BF16)
    copy = pltpu.make_async_copy(sent_ref, out_ref.at[:, pl.ds(first, count)], sem)
    copy.start()
    copy.wait()


def finish(squares, other_squares, own, got):
    result, first = [], 0
    for part in got:
        args = (squares, other_squares, own, part)
        result = [
            pl.pallas_call(
                functools.partial(finish_kernel, first),
                name="finish",
                out_shape=jax.ShapeDtypeStruct(own.shape, BF16),
                in_specs=[IN_VMEM] * len(args) + [IN_HBM] * len(result),
                out_specs=IN_HBM,
                input_output_aliases={len(args): 0} if result else {},
                scratch_shapes=[pltpu.VMEM(part.shape, BF16), pltpu.SemaphoreType.DMA(())],
                compiler_params=pltpu.CompilerParams(vmem_limit_bytes=8 * MIB),
                cost_estimate=pl.CostEstimate(flops=FINISH_FLOPS, bytes_accessed=0, transcendentals=0),
            )(*args, *result)
        ]
        first += part.shape[1]
    return result[0]


def direct(members, columns):
    return members == 2 and columns == sum(SENDS)


def layer_columns(members, gated, squares, weights, ready):
    columns = weights[0].shape[1] // members
    if not direct(members, columns):
        mean = lax.psum(squares.reshape(-1), "tensor") / INNER
        partial = dot(gated, jnp.concatenate(weights, axis=0)).astype(BF16)
        total = lax.psum_scatter(partial, "tensor", scatter_dimension=1, tiled=True)
        return (total.astype(F32) * lax.rsqrt(mean + EPSILON)[:, None]).astype(BF16)
    swap = [(0, 1), (1, 0)]
    tokens = gated.shape[0]
    parts, first = [ready[0]], SENDS[0]
    for count in SENDS[1:]:
        parts += local_call(
            functools.partial(send_kernel, first),
            "project_other",
            [jax.ShapeDtypeStruct((tokens, count), BF16)],
            (gated, *weights),
            after=parts[-1:],
        )
        first += count
    got = [lax.ppermute(part, "tensor", swap) for part in parts]
    other_squares = lax.ppermute(squares, "tensor", swap)
    (own,) = local_call(
        own_kernel,
        "project_own",
        [jax.ShapeDtypeStruct((tokens, columns), F32)],
        (gated, *weights),
        after=parts[-1:],
    )
    return finish(squares, other_squares, own, got)


def on_device(
    chips,
    members,
    signal,
    gate_branch,
    write_proj,
    read_proj,
    step_logits,
    valid_mask,
    stretch_band,
    band_offset,
    decay_log,
    step_offset,
    skip_gain,
    norm_gain,
    out_weight,
):
    small = (step_logits, valid_mask[None], band_offset, decay_log[None], step_offset[None])
    running, weight, decay, keep, send, *passed = own_state(
        stretch_band, small, write_proj, read_proj, signal, gate_branch
    )
    cores = [(0, 1), (1, 0)]
    got = lax.ppermute(send, "band", cores)
    state, first = chip_state(keep, got, decay)
    constants = (skip_gain[None], norm_gain.reshape(-1, LANES), out_weight)
    write, read, *streams = passed
    values = (running, weight, *streams)
    bases, factors, weights, prepared, halves, gains = [], [], [], [], [], []

    def local(part, after):
        if not local_shares(signal.shape[1])[0][part]:
            return after
        if part:
            base, factor, matrix = local_rest(part, values, prepared, out_weight, after)
        else:
            base, factor, matrix, second, *kept, lanes = local_first(
                chips, (*values, write, read, decay, got), state, constants, after
            )
            halves.append(kept[0])
            gains.append(kept[1])
            prepared.extend(kept[2:])
        bases.append(base)
        factors.append(factor)
        weights.append(matrix)
        return base if part else (second, lanes)

    states = entering_state(chips, state, first, keep, got, local)
    ahead = SENDS[0] if direct(members, out_weight.shape[1] // members) else 0
    gated, squares, *ready = gated_part(
        states, halves[0], gains[0], bases, factors, weights, ahead
    )
    return layer_columns(members, gated, squares, weights, ready)


def solution(mesh):
    placed = (
        P(("group", "scan", "band"), "tensor"),
        P(("group", "scan", "band"), "tensor"),
        P(("group", "scan", "band"), None),
        P(("group", "scan", "band"), None),
        P("tensor", ("group", "scan", "band")),
        P(("group", "scan", "band")),
        P(("group", "scan", "band")),
        P(None, "tensor"),
        P("tensor"),
        P("tensor"),
        P("tensor"),
        P("tensor"),
        P("tensor", None),
    )
    return jax.shard_map(
        functools.partial(on_device, mesh.shape["scan"], mesh.shape["tensor"]),
        mesh=mesh,
        in_specs=placed,
        out_specs=P(("group", "scan", "band"), "tensor"),
        check_vma=False,
    )
```

```python
import functools

import jax
import jax.numpy as jnp
from jax import lax
from jax.experimental import pallas as pl
from jax.experimental.pallas import tpu as pltpu
from jax.sharding import PartitionSpec as P

HEAD_DIM = 64
STATE = 128
HALF = STATE // 2
PART = HALF // 2
STRETCH = 256
BANDS = 12
INNER = 5120
LANES = 128

EPSILON = 1e-05
HIGHEST = lax.Precision.HIGHEST
F32 = jnp.float32
BF16 = jnp.bfloat16
MIB = 1 << 20


def dot(a, b):
    return lax.dot_general(a, b, (((1,), (0,)), ((), ())), preferred_element_type=F32)


def pieces(x):
    high = x.astype(BF16)
    rest = x - high.astype(F32)
    middle = rest.astype(BF16)
    return high, middle, (rest - middle.astype(F32)).astype(BF16)


def head_of_lane(heads, lanes, group, first=0):
    row = lax.broadcasted_iota(jnp.int32, (heads, lanes), 0)
    lane = lax.broadcasted_iota(jnp.int32, (heads, lanes), 1)
    return (row == first + lax.shift_right_logical(lane, group)).astype(F32).astype(BF16)


def slot_of(heads):
    return -(-heads // 8) * 8


def piece_rows(values, ref):
    heads = values.shape[0]
    ref[...] = jnp.zeros(ref.shape, F32)
    for k, piece in enumerate(pieces(values)):
        first = k * slot_of(heads)
        ref[first : first + heads, :] = piece.astype(F32)
    return ref[...]


def piece_away(heads, lanes, group):
    slot = slot_of(heads)
    row = lax.broadcasted_iota(jnp.int32, (LANES, lanes), 0)
    head = row - jnp.where(row >= 2 * slot, 2 * slot, jnp.where(row >= slot, slot, 0))
    head = jnp.where(row < 3 * slot, head, -LANES)
    return head - lax.shift_right_logical(lax.broadcasted_iota(jnp.int32, (LANES, lanes), 1), group)


def piece_map(away, first):
    return jnp.where(away == first, 1.0, 0.0).astype(BF16)


def spread_heads(row, heads_map):
    return sum(dot(piece, heads_map) for piece in pieces(jnp.broadcast_to(row, (8, row.shape[1]))))[:1]


def diagonal(rows, lanes):
    return lax.broadcasted_iota(jnp.int32, (rows, lanes), 0) == lax.broadcasted_iota(
        jnp.int32, (rows, lanes), 1
    )


def to_column(row):
    count = row.shape[1]
    return jnp.sum(jnp.where(diagonal(count, count), row, 0.0), axis=1, keepdims=True)


def decay_block(row, rows):
    place = lax.broadcasted_iota(jnp.int32, (rows, LANES), 0)
    high, middle, low = (piece.astype(F32) for piece in pieces(row))
    block = jnp.where(place == 0, high, jnp.where(place == 1, middle, jnp.where(place == 2, low, 0.0)))
    return block.astype(BF16)


def decay_row(block):
    return jnp.sum(block.astype(F32), axis=0, keepdims=True)


def decay_map(heads, width):
    return head_of_lane(-(-heads // 16) * 16, width, 6)


def decay_lanes(block, heads_map):
    return jnp.sum(dot(block[:16, : heads_map.shape[0]], heads_map), axis=0, keepdims=True)


def column_block(width):
    return width // 5 if width % (5 * LANES) == 0 else width


def local_call(body, name, outs, args, scratch=(), limit=8 * MIB, flops=0, after=(), aliases=None):
    size = sum(a.size * a.dtype.itemsize for a in args) + sum(o.size * o.dtype.itemsize for o in outs)

    def kernel(*refs):
        body(*refs[: len(args)], *refs[len(args) + len(after) :])

    return pl.pallas_call(
        kernel,
        name=name,
        out_shape=outs,
        in_specs=[pl.BlockSpec(memory_space=pltpu.VMEM)] * len(args)
        + [pl.BlockSpec(memory_space=pl.ANY)] * len(after),
        out_specs=[pl.BlockSpec(memory_space=pltpu.VMEM)] * len(outs),
        scratch_shapes=list(scratch),
        input_output_aliases=aliases or {},
        compiler_params=pltpu.CompilerParams(vmem_limit_bytes=limit),
        cost_estimate=pl.CostEstimate(flops=flops, bytes_accessed=size, transcendentals=0),
    )(*args, *after)


IN_VMEM = pl.BlockSpec(memory_space=pltpu.VMEM)
IN_HBM = pl.BlockSpec(memory_space=pltpu.HBM)
ANYWHERE = pl.BlockSpec(memory_space=pl.ANY)


def in_hbm(*arrays):
    return [pltpu.with_memory_space_constraint(a, pltpu.HBM) for a in arrays]


def state_kernel(
    band_ref,
    logits_hbm,
    mask_hbm,
    offset_hbm,
    decay_log_hbm,
    step_offset_hbm,
    write_hbm,
    read_hbm,
    signal_hbm,
    gate_hbm,
    running_ref,
    weight_ref,
    decay_ref,
    keep_ref,
    send_ref,
    write_ref,
    read_ref,
    signal_ref,
    gate_ref,
    logits_ref,
    mask_ref,
    offset_ref,
    decay_log_ref,
    step_offset_ref,
    rows_ref,
    factors_ref,
    sems,
    block_sems,
):
    heads, tokens = logits_ref.shape
    width = signal_ref.shape[1]
    block = column_block(width)
    is_first = lax.axis_index("band") == 0
    pairs = (
        (logits_hbm, logits_ref),
        (mask_hbm, mask_ref),
        (offset_hbm, offset_ref),
        (decay_log_hbm, decay_log_ref),
        (step_offset_hbm, step_offset_ref),
        (write_hbm, write_ref),
        (read_hbm, read_ref),
        (gate_hbm, gate_ref),
    )
    copies = [pltpu.make_async_copy(*pair, sems.at[i]) for i, pair in enumerate(pairs)]
    blocks = [
        pltpu.make_async_copy(
            signal_hbm.at[:, pl.ds(first, block)],
            signal_ref.at[:, pl.ds(first, block)],
            block_sems.at[first // block],
        )
        for first in range(0, width, block)
    ]
    for copy in copies[:6] + blocks + copies[6:]:
        copy.start()
    for copy in copies[:6]:
        copy.wait()

    offset = to_column(step_offset_ref[...] + offset_ref[pl.ds(band_ref[0], 1), :])
    raw = logits_ref[...] + offset
    step_size = jnp.maximum(raw, 0.0) + jnp.log1p(jnp.exp(-jnp.abs(raw)))
    log_decay = step_size * to_column(-jnp.exp(decay_log_ref[...]))
    earlier = lax.broadcasted_iota(jnp.int32, (tokens, tokens), 0)
    later = lax.broadcasted_iota(jnp.int32, (tokens, tokens), 1)
    sums = dot(
        piece_rows(log_decay, rows_ref).astype(BF16), jnp.where(earlier <= later, 1.0, 0.0).astype(BF16)
    )
    slot = slot_of(heads)
    running = sums[:heads] + sums[slot : slot + heads] + sums[2 * slot : 2 * slot + heads]
    weight = step_size * mask_ref[...].astype(F32)
    running_ref[...] = running
    weight_ref[...] = weight
    total = running[:, tokens - 1 : tokens]
    row = jnp.sum(jnp.where(diagonal(heads, LANES), jnp.exp(total), 0.0), axis=0, keepdims=True)
    send_ref[:, width:] = decay_block(row, HALF)
    decay_ref[...] = decay_block(row, 16)

    tail = piece_rows(jnp.exp(total - running) * weight, rows_ref).T.astype(BF16)
    write = write_ref[...].astype(F32).T
    low, high = write[:HALF], write[HALF:]
    write = jnp.concatenate(
        [jnp.where(is_first, low, high), jnp.where(is_first, high, low)], axis=0
    ).astype(BF16)
    away = piece_away(heads, block, 6)
    for first in range(0, width, block):
        factors_ref[:, first : first + block] = dot(tail, piece_map(away, first // HEAD_DIM))
    for copy in blocks:
        copy.wait()
    for first in range(0, width, block):
        lanes = slice(first, first + block)
        scaled = (signal_ref[:, lanes].astype(F32) * factors_ref[:, lanes]).astype(BF16)
        state = dot(write, scaled)
        keep_ref[:, lanes] = state[:HALF]
        send_ref[:, lanes] = state[HALF:].astype(BF16)
    for copy in copies[6:]:
        copy.wait()


def own_state(stretch_band, small, write_proj, read_proj, signal, gate_branch):
    tokens, width = signal.shape
    heads = small[0].shape[0]
    passed = (write_proj, read_proj, signal, gate_branch)
    return pl.pallas_call(
        state_kernel,
        name="own_state",
        out_shape=[
            jax.ShapeDtypeStruct((heads, tokens), F32),
            jax.ShapeDtypeStruct((heads, tokens), F32),
            jax.ShapeDtypeStruct((16, LANES), BF16),
            jax.ShapeDtypeStruct((HALF, width), F32),
            jax.ShapeDtypeStruct((HALF, width + LANES), BF16),
        ]
        + [jax.ShapeDtypeStruct(a.shape, a.dtype) for a in passed],
        in_specs=[pl.BlockSpec(memory_space=pltpu.SMEM)] + [IN_HBM] * 9,
        out_specs=[IN_VMEM] * 9,
        scratch_shapes=[pltpu.VMEM(a.shape, a.dtype) for a in small]
        + [
            pltpu.VMEM((LANES, tokens), F32),
            pltpu.VMEM((tokens, width), F32),
            pltpu.SemaphoreType.DMA((8,)),
            pltpu.SemaphoreType.DMA((width // column_block(width),)),
        ],
        compiler_params=pltpu.CompilerParams(vmem_limit_bytes=16 * MIB),
        cost_estimate=pl.CostEstimate(
            flops=4 * tokens * width * STATE, bytes_accessed=tokens * width * 2, transcendentals=0
        ),
    )(stretch_band, *in_hbm(*small, *passed))


def prepare_local(
    running_ref, write_ref, read_ref, decay_ref, got_ref, scores_ref, running_pieces_ref, decay_pieces_ref, lanes_ref, rows_ref
):
    width = lanes_ref.shape[1]
    scores = lax.dot_general(
        read_ref[...], write_ref[...], (((1,), (1,)), ((), ())), preferred_element_type=F32
    )
    row = lax.broadcasted_iota(jnp.int32, scores.shape, 0)
    lane = lax.broadcasted_iota(jnp.int32, scores.shape, 1)
    scores_ref[...] = jnp.where(row >= lane, scores, 0.0)
    running = running_ref[...]
    running_pieces_ref[...] = piece_rows(running, rows_ref).T.astype(BF16)
    decay_pieces_ref[...] = piece_rows(jnp.exp(running), rows_ref).T.astype(BF16)
    mine, got = decay_ref[...].astype(F32), got_ref[:16, width:].astype(F32)
    first_core = jnp.where(lax.axis_index("band") == 0, mine, got).astype(BF16)
    lanes_ref[...] = jnp.broadcast_to(
        decay_lanes(first_core, decay_map(width // HEAD_DIM, width)), lanes_ref.shape
    )


def local_heads(
    first_block,
    running_ref,
    weight_ref,
    signal_ref,
    gate_ref,
    scores_ref,
    running_pieces_ref,
    decay_pieces_ref,
    skip_ref,
    base_ref,
    factor_ref,
):
    heads, tokens = running_ref.shape
    block = column_block(signal_ref.shape[1])
    half = tokens // 2
    low_lanes = lax.broadcasted_iota(jnp.int32, (half, LANES), 1) < HEAD_DIM
    early, late = slice(0, half), slice(half, tokens)

    wide_away, away = piece_away(heads, 2 * block, 7), piece_away(heads, block, 6)

    def heads_block(at, _):
        first_head = (first_block + at) * (block // HEAD_DIM)

        def whole_lanes(lane, count):
            return pl.ds(pl.multiple_of((first_block + at) * block + lane, LANES), count)

        def part_lanes(lane, count):
            return pl.ds(pl.multiple_of(at * block + lane, LANES), count)

        wide = dot(running_pieces_ref[...], piece_map(wide_away, first_head))
        gate = gate_ref[:, whole_lanes(0, block)].astype(F32)
        gate = gate / (1.0 + jnp.exp(-gate))
        factor_ref[:, part_lanes(0, block)] = (
            dot(decay_pieces_ref[...], piece_map(away, first_head)) * gate
        )
        skip = spread_heads(skip_ref[...], head_of_lane(heads, block, 6, first_head))
        for pair in range(block // LANES):
            lanes = slice(pair * LANES, (pair + 1) * LANES)
            values = signal_ref[:, whole_lanes(pair * LANES, LANES)]
            top, bottom = [], []
            for k in (2 * pair, 2 * pair + 1):
                row = running_ref[pl.ds(first_head + k, 1), :]
                weight = weight_ref[pl.ds(first_head + k, 1), :]
                column = wide[:, k * LANES : (k + 1) * LANES]

                def mixing(rows, cols):
                    span = jnp.minimum(column[rows] - row[:, cols], 0.0)
                    return (jnp.exp(span) * scores_ref[rows, cols] * weight[:, cols]).astype(BF16)

                top.append(mixing(early, early))
                bottom.append(jnp.concatenate([mixing(late, early), mixing(late, late)], axis=1))
            top = dot(jnp.concatenate(top, axis=0), values[early])
            bottom = dot(jnp.concatenate(bottom, axis=0), values)
            skipped = values.astype(F32) * skip[:, lanes]
            out_lanes = part_lanes(pair * LANES, LANES)
            base_ref[early, out_lanes] = (
                jnp.where(low_lanes, top[:half], top[half:]) + skipped[early]
            ) * gate[early, lanes]
            base_ref[late, out_lanes] = (
                jnp.where(low_lanes, bottom[:half], bottom[half:]) + skipped[late]
            ) * gate[late, lanes]
        return 0

    lax.fori_loop(0, base_ref.shape[1] // block, heads_block, 0)


def local_first_kernel(
    chips,
    running_ref,
    weight_ref,
    signal_ref,
    gate_ref,
    write_ref,
    read_ref,
    decay_ref,
    got_ref,
    state_ref,
    skip_hbm,
    gain_hbm,
    matrix_hbm,
    after_ref,
    base_ref,
    factor_ref,
    matrix_ref,
    second_ref,
    halves_ref,
    gain_ref,
    scores_ref,
    running_pieces_ref,
    decay_pieces_ref,
    skip_ref,
    lanes_ref,
    rows_ref,
    sems,
):
    rows = matrix_ref.shape[0]
    pairs = (
        (skip_hbm, skip_ref),
        (gain_hbm, gain_ref),
        (matrix_hbm.at[pl.ds(0, rows), :], matrix_ref),
    )
    copies = [pltpu.make_async_copy(*pair, sems.at[i]) for i, pair in enumerate(pairs)]
    for copy in copies:
        copy.start()
    read = read_ref[...].astype(F32)
    swapped = jnp.concatenate([read[:, HALF:], read[:, :HALF]], axis=1)
    read = jnp.where(lax.axis_index("band") == 0, read, swapped)
    if chips == 4:
        late = HALF + PART
        turned = jnp.concatenate([read[:, :HALF], read[:, late:], read[:, HALF:late]], axis=1)
        read = jnp.where(lax.axis_index("scan") == 2, turned, read)
    halves_ref[...] = read.astype(BF16)
    upper = lax.axis_index("scan") == 2
    second_ref[...] = state_ref[pl.ds(pl.multiple_of(jnp.where(upper, 0, PART), PART), PART), :]
    prepared = (scores_ref, running_pieces_ref, decay_pieces_ref)
    prepare_local(running_ref, write_ref, read_ref, decay_ref, got_ref, *prepared, lanes_ref, rows_ref)
    copies[0].wait()
    local_heads(
        0, running_ref, weight_ref, signal_ref, gate_ref, *prepared, skip_ref, base_ref, factor_ref
    )
    for copy in copies[1:]:
        copy.wait()


def local_rest_kernel(
    first_block,
    first_row,
    running_ref,
    weight_ref,
    signal_ref,
    gate_ref,
    scores_ref,
    running_pieces_ref,
    decay_pieces_ref,
    skip_ref,
    matrix_hbm,
    after_ref,
    base_ref,
    factor_ref,
    matrix_ref,
    sem,
):
    rows = matrix_ref.shape[0]
    copy = pltpu.make_async_copy(matrix_hbm.at[pl.ds(first_row, rows), :], matrix_ref, sem)
    copy.start()
    local_heads(
        first_block,
        running_ref,
        weight_ref,
        signal_ref,
        gate_ref,
        scores_ref,
        running_pieces_ref,
        decay_pieces_ref,
        skip_ref,
        base_ref,
        factor_ref,
    )
    copy.wait()


def local_shares(width):
    if width % (10 * LANES):
        return (width // column_block(width), 0, 0), (width, 0, 0)
    tenth = width // 10
    return (1, 2, 2), (tenth, 4 * tenth, 5 * tenth)


def local_call_of(kernel, name, part, outs, resident, passed, after, scratch):
    tokens, width = resident[2].shape
    matrix = passed[-1]
    blocks, rows = local_shares(width)
    columns = blocks[part] * column_block(width)
    return pl.pallas_call(
        kernel,
        name=name,
        out_shape=[jax.ShapeDtypeStruct((tokens, columns), F32)] * 2
        + [jax.ShapeDtypeStruct((rows[part], matrix.shape[1]), BF16)]
        + outs,
        in_specs=[IN_VMEM] * len(resident) + [IN_HBM] * len(passed) + [ANYWHERE],
        out_specs=[IN_VMEM] * (3 + len(outs)),
        scratch_shapes=scratch,
        compiler_params=pltpu.CompilerParams(vmem_limit_bytes=16 * MIB),
        cost_estimate=pl.CostEstimate(
            flops=6 * columns * tokens * tokens,
            bytes_accessed=tokens * columns * 12,
            transcendentals=columns // HEAD_DIM * tokens * tokens,
        ),
    )(*resident, *in_hbm(*passed), after)


def local_first(chips, values, state, constants, after):
    running, signal = values[0], values[2]
    skip_gain, norm_gain, _ = constants
    tokens, width = signal.shape
    pieces_shape = jax.ShapeDtypeStruct((tokens, LANES), BF16)
    return local_call_of(
        functools.partial(local_first_kernel, chips),
        "local_first",
        0,
        [
            jax.ShapeDtypeStruct((PART, state.shape[1]), BF16),
            jax.ShapeDtypeStruct((tokens, STATE), BF16),
            jax.ShapeDtypeStruct(norm_gain.shape, F32),
            jax.ShapeDtypeStruct((tokens, tokens), F32),
            pieces_shape,
            pieces_shape,
            jax.ShapeDtypeStruct(skip_gain.shape, F32),
            jax.ShapeDtypeStruct((8, width), F32),
        ],
        (*values, state),
        constants,
        after,
        [pltpu.VMEM((LANES, tokens), F32), pltpu.SemaphoreType.DMA((3,))],
    )


def local_rest(part, values, prepared, out_weight, after):
    blocks, rows = local_shares(values[2].shape[1])
    return local_call_of(
        functools.partial(local_rest_kernel, sum(blocks[:part]), sum(rows[:part])),
        "local_rest",
        part,
        [],
        (*values, *prepared),
        (out_weight,),
        after,
        [pltpu.SemaphoreType.DMA(())],
    )


def chip_kernel(keep_ref, got_ref, decay_ref, state_ref, first_ref):
    width = keep_ref.shape[1]
    core = lax.axis_index("band")
    chip = lax.axis_index("scan")
    heads_map = decay_map(width // HEAD_DIM, width)
    got_decay = got_ref[:16, width:]
    mine = decay_ref[...]
    later = jnp.where(core == 0, got_decay.astype(F32), mine.astype(F32)).astype(BF16)
    lanes = decay_lanes(later, heads_map)
    got = got_ref[:, :width].astype(F32)
    keep = keep_ref[...]
    early, late = jnp.where(core == 0, keep, got), jnp.where(core == 0, got, keep)
    state_ref[:, :width] = (early * lanes + late).astype(BF16)
    block = decay_block(decay_row(got_decay) * decay_row(mine), PART)
    state_ref[:PART, width:] = block
    state_ref[PART:, width:] = block

    lower = jnp.where(chip == 1, PART, 0)
    first_ref[...] = state_ref[pl.ds(pl.multiple_of(lower, PART), PART), :]


def early_kernel(state_ref, near_ref, out_ref, lanes_ref):
    width = out_ref.shape[1]
    chip = lax.axis_index("scan")
    heads_map = decay_map(width // HEAD_DIM, width)

    @pl.when(chip == 0)
    def _():
        out_ref[...] = state_ref[PART:, :width]

    @pl.when(chip == 1)
    def _():
        lanes = decay_lanes(state_ref[:16, width:], heads_map)
        out_ref[...] = (
            lanes * near_ref[:, :width].astype(F32) + state_ref[:PART, :width].astype(F32)
        ).astype(BF16)

    @pl.when(chip == 2)
    def _():
        for first, ref in ((0, near_ref), (8, state_ref)):
            lanes = decay_lanes(ref[:16, width:], heads_map)
            lanes_ref[first : first + 8, :] = jnp.broadcast_to(lanes, (8, width))


def middle_kernel(state_ref, near_ref, far_ref, lanes_ref, out_ref, far_lanes_ref):
    width = out_ref.shape[1]
    chip = lax.axis_index("scan")

    @pl.when(chip == 3)
    def _():
        lanes = decay_lanes(far_ref[:16, width:], decay_map(width // HEAD_DIM, width))
        far_lanes_ref[...] = jnp.broadcast_to(lanes, far_lanes_ref.shape)

    @pl.when(chip == 2)
    def _():
        entered = lanes_ref[:1] * far_ref[:, :width].astype(F32) + near_ref[:, :width].astype(F32)
        out_ref[...] = (lanes_ref[8:9] * entered + state_ref[PART:, :width].astype(F32)).astype(BF16)


def enter_first_kernel(
    near_ref,
    far_ref,
    early_ref,
    near_lanes_ref,
    far_lanes_ref,
    keep_ref,
    got_ref,
    lanes_ref,
    mine_ref,
    send_ref,
):
    width = keep_ref.shape[1]
    chip = lax.axis_index("scan")
    near, far = (ref.at[:, pl.ds(0, width)] for ref in (near_ref, far_ref))
    refs = (keep_ref, got_ref, lanes_ref, mine_ref, send_ref)

    @pl.when(chip == 0)
    def _():
        share_enter(jnp.zeros((PART, width), F32), 0, 0, *refs)

    @pl.when(chip == 1)
    def _():
        share_enter(near[...].astype(F32), 0, 0, *refs)

    @pl.when(chip == 2)
    def _():
        enter = near_lanes_ref[:1] * far[...].astype(F32) + near[...].astype(F32)
        share_enter(enter, PART, 0, *refs)

    @pl.when(chip == 3)
    def _():
        enter = far_lanes_ref[:1] * early_ref[...].astype(F32) + far[...].astype(F32)
        share_enter(enter, 0, 0, *refs)


def enter_rest_kernel(
    early_ref, next_ref, last_ref, keep_ref, got_ref, lanes_ref, old_ref, mine_ref, send_ref
):
    width = keep_ref.shape[1]
    chip = lax.axis_index("scan")
    refs = (keep_ref, got_ref, lanes_ref, mine_ref, send_ref)

    @pl.when(chip == 0)
    def _():
        share_enter(jnp.zeros((PART, width), F32), PART, 0, *refs)

    @pl.when(chip == 1)
    def _():
        share_enter(early_ref[...].astype(F32), PART, 0, *refs)

    @pl.when(chip == 2)
    def _():
        share_enter(next_ref[...].astype(F32), 0, 0, *refs)

    @pl.when(chip == 3)
    def _():
        share_enter(last_ref[...].astype(F32), PART, 0, *refs)


def share_enter(enter, first, place, keep_ref, got_ref, lanes_ref, mine_ref, send_ref):
    width = keep_ref.shape[1]
    core = lax.axis_index("band")
    rows = slice(first, first + enter.shape[0])
    sent = slice(place, place + enter.shape[0])

    @pl.when(core == 0)
    def _():
        mine_ref[rows, :] = enter.astype(BF16)
        send_ref[sent, :] = (lanes_ref[:1] * enter + keep_ref[rows, :]).astype(BF16)

    @pl.when(core == 1)
    def _():
        send_ref[sent, :] = enter.astype(BF16)
        mine_ref[rows, :] = (lanes_ref[:1] * enter + got_ref[rows, :width].astype(F32)).astype(BF16)


def gathered_kernel(all_ref, keep_ref, got_ref, lanes_ref, mine_ref, send_ref, enter_ref):
    width = keep_ref.shape[1]
    chip = lax.axis_index("scan")
    heads_map = decay_map(width // HEAD_DIM, width)
    enter_ref[...] = jnp.zeros(enter_ref.shape, F32)
    for source in range(all_ref.shape[0]):

        @pl.when(source < chip)
        def _():
            lanes = decay_lanes(all_ref[source, :16, width:], heads_map)
            enter_ref[...] = lanes * enter_ref[...] + all_ref[source, :, :width].astype(F32)

    share_enter(enter_ref[...], 0, 0, keep_ref, got_ref, lanes_ref, mine_ref, send_ref)


def chip_state(keep, got, decay):
    width = keep.shape[1]
    return local_call(
        chip_kernel,
        "chip_state",
        [
            jax.ShapeDtypeStruct((HALF, width + LANES), BF16),
            jax.ShapeDtypeStruct((PART, width + LANES), BF16),
        ],
        (keep, got, decay),
    )


def entering_state(chips, state, first, keep, got, local):
    width = keep.shape[1]
    half = jax.ShapeDtypeStruct((HALF, width), BF16)
    part = jax.ShapeDtypeStruct((PART, width), BF16)
    cores = [(0, 1), (1, 0)]
    if chips != 4:
        gathered = lax.all_gather(state, "scan", axis=0)
        second, lanes = local(0, first)
        local(1, second)
        local(2, second)
        mine, give = local_call(
            gathered_kernel,
            "enter_state",
            [half, half],
            (gathered, keep, got, lanes),
            (pltpu.VMEM((HALF, width), F32),),
        )
        return mine, lax.ppermute(give, "band", cores)
    near = lax.ppermute(first, "scan", [(0, 1), (1, 2)])
    second, lanes = local(0, first)
    far = lax.ppermute(second, "scan", [(0, 2), (2, 3)])
    done = local(1, second)
    ahead, near_lanes = local_call(
        early_kernel,
        "early_state",
        [part, jax.ShapeDtypeStruct((16, width), F32)],
        (state, near),
        after=(done,),
    )
    early = lax.ppermute(ahead, "scan", [(1, 3), (0, 1)])
    following = lax.ppermute(ahead, "scan", [(1, 2)])
    middle, far_lanes = local_call(
        middle_kernel,
        "middle_state",
        [part, jax.ShapeDtypeStruct((8, width), F32)],
        (state, near, far, near_lanes),
        after=(ahead,),
    )
    last = lax.ppermute(middle, "scan", [(2, 3)])
    done = local(2, middle)
    mine, give = local_call(
        enter_first_kernel,
        "enter_first",
        [half, part],
        (near, far, early, near_lanes, far_lanes, keep, got, lanes),
        after=(done,),
    )
    other = lax.ppermute(give, "band", cores)
    mine, give = local_call(
        enter_rest_kernel,
        "enter_rest",
        [half, part],
        (early, following, last, keep, got, lanes, mine),
        after=(other,),
        aliases={6: 0},
    )
    return mine, other, lax.ppermute(give, "band", cores)


def gated_kernel(states, parts, *refs):
    state_refs, (read_ref, gain_ref, *refs) = refs[:states], refs[states:]
    bases, factors, weights = refs[:parts], refs[parts : 2 * parts], refs[2 * parts : 3 * parts]
    out_ref, square_ref, *first_refs = refs[3 * parts :]
    tokens, width = out_ref.shape
    block = column_block(width)
    read = read_ref[...]
    sums = jnp.zeros((tokens, LANES), F32)
    first = 0
    for base_ref, factor_ref in zip(bases, factors):
        for start in range(0, base_ref.shape[1], block):
            lanes = slice(first, first + block)
            carried = dot(read, jnp.concatenate([ref[:, lanes] for ref in state_refs], axis=0))
            lanes = slice(start, start + block)
            gated = base_ref[:, lanes] + factor_ref[:, lanes] * carried
            for k in range(0, block, LANES):
                column = gated[:, k : k + LANES]
                row = (first + k) // LANES
                out_ref[:, first + k : first + k + LANES] = (
                    column * gain_ref[row : row + 1, :]
                ).astype(BF16)
                sums += column * column
            first += block
    for first_ref in first_refs:
        send_kernel(0, out_ref, *weights, first_ref)
    squares = jnp.sum(sums.T, axis=0, keepdims=True)
    for row in range(tokens // LANES):
        square_ref[row : row + 1, :] = squares[:, row * LANES : (row + 1) * LANES]


def gated_part(states, read_proj, gain, bases, factors, weights, first):
    tokens = read_proj.shape[0]
    width = states[0].shape[1]
    return local_call(
        functools.partial(gated_kernel, len(states), len(bases)),
        "gated_part",
        [
            jax.ShapeDtypeStruct((tokens, width), BF16),
            jax.ShapeDtypeStruct((tokens // LANES, LANES), F32),
        ]
        + [jax.ShapeDtypeStruct((tokens, first), BF16)] * (first > 0),
        (*states, read_proj, gain, *bases, *factors, *weights),
        flops=2 * tokens * width * STATE,
    )


SENDS = (256, 512, 384, 128)
FINISH_FLOPS = 2 * 10**9


def project(gated_ref, weights, other, first, count):
    columns = weights[0].shape[1] // 2
    member = lax.axis_index("tensor")
    start = (1 - member if other else member) * columns + first
    lanes = pl.ds(pl.multiple_of(start, LANES), count)
    row, total = 0, None
    for weight_ref in weights:
        rows = weight_ref.shape[0]
        term = dot(gated_ref[:, row : row + rows], weight_ref[:, lanes])
        row, total = row + rows, term if total is None else total + term
    return total


def send_kernel(first, gated_ref, *refs):
    *weights, out_ref = refs
    count = out_ref.shape[1]
    out_ref[...] = project(gated_ref, weights, True, first, count).astype(BF16)


def own_kernel(gated_ref, *refs):
    *weights, out_ref = refs
    count = out_ref.shape[1] // 5
    for first in range(0, out_ref.shape[1], count):
        out_ref[:, first : first + count] = project(gated_ref, weights, False, first, count)


def finish_kernel(first, squares_ref, other_squares_ref, own_ref, got_ref, *refs):
    out_ref, sent_ref, sem = refs[-3:]
    tokens, count = got_ref.shape
    mean = (squares_ref[...] + other_squares_ref[...]) / INNER
    scale = lax.rsqrt(mean + EPSILON)
    scale = jnp.concatenate(
        [jnp.broadcast_to(scale[k : k + 1], (LANES, LANES)).T for k in range(tokens // LANES)], axis=0
    )
    for lane in range(0, count, LANES):
        lanes = slice(lane, lane + LANES)
        total = own_ref[:, first + lane : first + lane + LANES] + got_ref[:, lanes].astype(F32)
        sent_ref[:, lanes] = (total * scale).astype(BF16)
    copy = pltpu.make_async_copy(sent_ref, out_ref.at[:, pl.ds(first, count)], sem)
    copy.start()
    copy.wait()


def finish(squares, other_squares, own, got):
    result, first = [], 0
    for part in got:
        args = (squares, other_squares, own, part)
        result = [
            pl.pallas_call(
                functools.partial(finish_kernel, first),
                name="finish",
                out_shape=jax.ShapeDtypeStruct(own.shape, BF16),
                in_specs=[IN_VMEM] * len(args) + [IN_HBM] * len(result),
                out_specs=IN_HBM,
                input_output_aliases={len(args): 0} if result else {},
                scratch_shapes=[pltpu.VMEM(part.shape, BF16), pltpu.SemaphoreType.DMA(())],
                compiler_params=pltpu.CompilerParams(vmem_limit_bytes=8 * MIB),
                cost_estimate=pl.CostEstimate(flops=FINISH_FLOPS, bytes_accessed=0, transcendentals=0),
            )(*args, *result)
        ]
        first += part.shape[1]
    return result[0]


def direct(members, columns):
    return members == 2 and columns == sum(SENDS)


def layer_columns(members, gated, squares, weights, ready):
    columns = weights[0].shape[1] // members
    if not direct(members, columns):
        mean = lax.psum(squares.reshape(-1), "tensor") / INNER
        partial = dot(gated, jnp.concatenate(weights, axis=0)).astype(BF16)
        total = lax.psum_scatter(partial, "tensor", scatter_dimension=1, tiled=True)
        return (total.astype(F32) * lax.rsqrt(mean + EPSILON)[:, None]).astype(BF16)
    swap = [(0, 1), (1, 0)]
    tokens = gated.shape[0]
    parts, first = [ready[0]], SENDS[0]
    for count in SENDS[1:]:
        parts += local_call(
            functools.partial(send_kernel, first),
            "project_other",
            [jax.ShapeDtypeStruct((tokens, count), BF16)],
            (gated, *weights),
            after=parts[-1:],
        )
        first += count
    got = [lax.ppermute(part, "tensor", swap) for part in parts]
    other_squares = lax.ppermute(squares, "tensor", swap)
    (own,) = local_call(
        own_kernel,
        "project_own",
        [jax.ShapeDtypeStruct((tokens, columns), F32)],
        (gated, *weights),
        after=parts[-1:],
    )
    return finish(squares, other_squares, own, got)


def on_device(
    chips,
    members,
    signal,
    gate_branch,
    write_proj,
    read_proj,
    step_logits,
    valid_mask,
    stretch_band,
    band_offset,
    decay_log,
    step_offset,
    skip_gain,
    norm_gain,
    out_weight,
):
    small = (step_logits, valid_mask[None], band_offset, decay_log[None], step_offset[None])
    running, weight, decay, keep, send, *passed = own_state(
        stretch_band, small, write_proj, read_proj, signal, gate_branch
    )
    cores = [(0, 1), (1, 0)]
    got = lax.ppermute(send, "band", cores)
    state, first = chip_state(keep, got, decay)
    constants = (skip_gain[None], norm_gain.reshape(-1, LANES), out_weight)
    write, read, *streams = passed
    values = (running, weight, *streams)
    bases, factors, weights, prepared, halves, gains = [], [], [], [], [], []

    def local(part, after):
        if not local_shares(signal.shape[1])[0][part]:
            return after
        if part:
            base, factor, matrix = local_rest(part, values, prepared, out_weight, after)
        else:
            base, factor, matrix, second, *kept, lanes = local_first(
                chips, (*values, write, read, decay, got), state, constants, after
            )
            halves.append(kept[0])
            gains.append(kept[1])
            prepared.extend(kept[2:])
        bases.append(base)
        factors.append(factor)
        weights.append(matrix)
        return base if part else (second, lanes)

    states = entering_state(chips, state, first, keep, got, local)
    ahead = SENDS[0] if direct(members, out_weight.shape[1] // members) else 0
    gated, squares, *ready = gated_part(
        states, halves[0], gains[0], bases, factors, weights, ahead
    )
    return layer_columns(members, gated, squares, weights, ready)


def solution(mesh):
    placed = (
        P(("group", "scan", "band"), "tensor"),
        P(("group", "scan", "band"), "tensor"),
        P(("group", "scan", "band"), None),
        P(("group", "scan", "band"), None),
        P("tensor", ("group", "scan", "band")),
        P(("group", "scan", "band")),
        P(("group", "scan", "band")),
        P(None, "tensor"),
        P("tensor"),
        P("tensor"),
        P("tensor"),
        P("tensor"),
        P("tensor", None),
    )
    return jax.shard_map(
        functools.partial(on_device, mesh.shape["scan"], mesh.shape["tensor"]),
        mesh=mesh,
        in_specs=placed,
        out_specs=P(("group", "scan", "band"), "tensor"),
        check_vma=False,
    )
```
